32 devices in a mesh: dp: 4 (over z), hist: 4 (over y, x), mp: 2 (over core).
Axes of the slice: x: 2, y: 2, z: 4, core: 2. Of those that a mesh axis runs over, the one named last changes fastest.
Arguments:
- history: bfloat16 [4, 8192, 2048], P('hist', 'dp'), may hold values from -6 to 6
- mixer_in: bfloat16 [2048, 100], replicated, may hold values from -0.125 to 0.125
- mixer_out: bfloat16 [100, 4, 4], replicated, may hold values from -0.625 to 0.625
- mixer_bias: float32 [4, 4], replicated, may hold values from -3 to 3
- norm_gain: bfloat16 [4, 2048], P(None, ('dp', 'hist')), may hold values from 0.5 to 1.5
- query_weight: bfloat16 [2048, 2048], P(('dp', 'hist'), 'mp'), may hold values from -0.125 to 0.125
- key_weight: bfloat16 [2048, 2048], P(('dp', 'hist'), 'mp'), may hold values from -0.125 to 0.125
- value_weight: bfloat16 [2048, 2048], P(('dp', 'hist'), 'mp'), may hold values from -0.125 to 0.125
- out_weight: bfloat16 [2048, 2048], P('mp', ('dp', 'hist')), may hold values from -0.75 to 0.75
- up_weight: bfloat16 [2048, 8192], P(('dp', 'hist'), 'mp'), may hold values from -0.125 to 0.125
- down_weight: bfloat16 [8192, 2048], P('mp', ('dp', 'hist')), may hold values from -0.0625 to 0.0625
- target: bfloat16 [8192, 2048], P(('dp', 'hist')), may hold values from -6 to 6
- loss_count: int32 [8192], P(('dp', 'hist')), may hold values from 1 to 4
- domain: int32 [4], P('dp'), may hold values from 0 to 21
- domain_scale: float32 [22], replicated, may hold values from 0.3 to 1.5
Outputs:
- output: bfloat16 [8192, 2048], P(('dp', 'hist'))
- mix_weights: float32 [8192, 4, 4], P(('dp', 'hist'))
- history_grad: bfloat16 [4, 8192, 2048], P('hist', 'dp')
- mixer_in_grad: float32 [2048, 100], replicated
- mixer_out_grad: float32 [100, 4, 4], replicated
- mixer_bias_grad: float32 [4, 4], replicated
- norm_gain_grad: float32 [4, 2048], P(None, ('dp', 'hist'))
- query_grad: float32 [2048, 2048], P(('dp', 'hist'), 'mp')
- key_grad: float32 [2048, 2048], P(('dp', 'hist'), 'mp')
- value_grad: float32 [2048, 2048], P(('dp', 'hist'), 'mp')
- out_grad: float32 [2048, 2048], P('mp', ('dp', 'hist'))
- up_grad: float32 [2048, 8192], P(('dp', 'hist'), 'mp')
- down_grad: float32 [8192, 2048], P('mp', ('dp', 'hist'))
The draws below stay inside these ranges and needn't reach their ends.
All inputs are finite; a program needn't handle non-finite values.
Results may differ from the reference program's by a relative error of at most 0.015.
Values may be sent and summed in bfloat16 or wider, within the bound.
No kernel may reach another device: no remote copies, remote signals or barrier semaphores. Data moves between devices by JAX's collectives and lax.ppermute only.
A program may use at most 448 MiB of HBM per device.

```python
import math
import jax
import jax.numpy as jnp
from jax import lax

D = 2048
HEADS = 16
HD = 128
FF = 8192
ROT = 32
MIXH = 100
STREAMS = 4
GROUPS = 22
SEQ = 2048
LAYERS = 4
SEQS = 4
TOKENS = 8192


def plant(values, key, smallest, high):
    longest = values.shape.index(max(values.shape))
    spots = []
    for shift in (0, 1):
        where = [jax.random.randint(jax.random.fold_in(key, axis), (), 0, length) for axis, length in enumerate(values.shape)]
        where[longest] = (where[longest] + shift) % values.shape[longest]
        spots.append(tuple(where))
    return values.at[spots[0]].set(smallest).at[spots[1]].set(high)


def block_scale(key, extent, shards, smallest, high):
    level = 1.0
    for position, blocks in shards:
        steps = jax.random.uniform(jax.random.fold_in(jax.random.fold_in(key, 6), position), (blocks,), jnp.float32, smallest / len(shards), high / len(shards))
        level = level * jnp.repeat(jnp.exp(steps), extent[position] // blocks).reshape((-1,) + (1,) * (len(extent) - 1 - position))
    return level


def scatter_about(own_key, shape, deviation, limit, pieces=(), kind=jnp.bfloat16):
    array = deviation * jax.random.normal(own_key, shape, jnp.float32)
    if pieces:
        array = array * block_scale(own_key, shape, pieces, -0.22, 0.18)
    return jnp.clip(array, -limit, limit).astype(kind)


def setup_inputs(seed: int = 0) -> dict:
    key_of = jax.random.split(jax.random.key(seed), 16)
    return {
        "history": scatter_about(key_of[0], (LAYERS, TOKENS, D), 1.0, 6.0, ((0, 4), (1, 4))),
        "mixer_in": scatter_about(key_of[1], (D, MIXH), D ** -0.5, 0.125),
        "mixer_out": scatter_about(key_of[2], (MIXH, STREAMS, LAYERS), MIXH ** -0.5, 0.625),
        "mixer_bias": scatter_about(key_of[3], (STREAMS, LAYERS), 0.5, 3.0, (), jnp.float32),
        "norm_gain": jnp.clip(1.0 + 0.1 * jax.random.normal(key_of[4], (STREAMS, D), jnp.float32), 0.5, 1.5).astype(jnp.bfloat16),
        "query_weight": scatter_about(key_of[5], (D, HEADS * HD), D ** -0.5, 0.125, ((0, 16), (1, 2))),
        "key_weight": scatter_about(key_of[6], (D, HEADS * HD), D ** -0.5, 0.125, ((0, 16), (1, 2))),
        "value_weight": scatter_about(key_of[7], (D, HEADS * HD), D ** -0.5, 0.125, ((0, 16), (1, 2))),
        "out_weight": scatter_about(key_of[8], (HEADS * HD, D), (HEADS * HD // 32) ** -0.5, 0.75, ((0, 2), (1, 16))),
        "up_weight": scatter_about(key_of[9], (D, FF), D ** -0.5, 0.125, ((0, 16), (1, 2))),
        "down_weight": scatter_about(key_of[10], (FF, D), FF ** -0.5, 0.0625, ((0, 2), (1, 16))),
        "target": scatter_about(key_of[11], (TOKENS, D), 1.0, 6.0, ((0, 16),)),
        "loss_count": plant(jax.random.randint(key_of[12], (TOKENS,), 1, 5), jax.random.fold_in(key_of[12], 1), 1, 4).astype(jnp.int32),
        "domain": plant(jax.random.randint(key_of[13], (SEQS,), 0, GROUPS), jax.random.fold_in(key_of[13], 1), 0, GROUPS - 1).astype(jnp.int32),
        "domain_scale": jnp.clip(jnp.exp(jax.random.uniform(key_of[14], (GROUPS,), jnp.float32, math.log(0.3), math.log(1.5))), 0.3, 1.5),
    }


HIGHEST = lax.Precision.HIGHEST
EPS_NORM = 1e-05
EPS_RMS = 1e-06
ROPE_BASE = 10000.0

@jax.custom_vjp
def low(v):
    return lax.optimization_barrier(v.astype(jnp.bfloat16)).astype(jnp.float32)

@jax.custom_vjp
def low_back(v):
    return v

def low_keep(v):
    return (low(v), None)

def low_pass(kept, grad):
    return (grad,)

def back_keep(v):
    return (v, None)

def back_low(kept, grad):
    return (low(grad),)
low.defvjp(low_keep, low_pass)
low_back.defvjp(back_keep, back_low)

def matmul(left, right):
    return jnp.dot(left, right, precision=HIGHEST)

def layer_norm(stream, gain):
    centered_input = stream - lax.optimization_barrier(jnp.mean(stream, -1, keepdims=True))
    variance = lax.optimization_barrier(jnp.mean(centered_input * centered_input, -1, keepdims=True))
    return centered_input * lax.rsqrt(variance + EPS_NORM) * gain

def rotate(values, positions):
    half = ROT // 2
    freq = ROPE_BASE ** (-2.0 * jnp.arange(half, dtype=jnp.float32) / ROT)
    angle = positions[:, None] * freq[None, :]
    cosine = jnp.cos(angle)[:, None, :]
    sine = jnp.sin(angle)[:, None, :]
    first = values[..., :half]
    second = values[..., half:ROT]
    return jnp.concatenate([first * cosine - second * sine, second * cosine + first * sine, values[..., ROT:]], -1)

def block(params, stored):
    mixer_in, mixer_out, mixer_bias, norm_gain, query_weight, key_weight, value_weight, out_weight, up_weight, down_weight = params
    latest = stored[LAYERS - 1]
    unit = latest * lax.rsqrt(lax.optimization_barrier(jnp.mean(latest * latest, -1, keepdims=True)) + EPS_RMS)
    mixer_hidden = low(jax.nn.gelu(matmul(low(unit), mixer_in), approximate=False))
    mixing = jnp.einsum('tm,mcl->tcl', mixer_hidden, mixer_out, precision=HIGHEST) + mixer_bias[None]
    streams = low_back(jnp.einsum('tcl,ltd->tcd', mixing, stored, precision=HIGHEST))
    normed = low(layer_norm(streams, norm_gain[None]))
    positions = jnp.arange(SEQ, dtype=jnp.float32)
    query = low(rotate(low_back(matmul(normed[:, 0], query_weight)).reshape(SEQ, HEADS, HD), positions))
    keys = low(rotate(low_back(matmul(normed[:, 1], key_weight)).reshape(SEQ, HEADS, HD), positions))
    values = low(low_back(matmul(normed[:, 2], value_weight))).reshape(SEQ, HEADS, HD)
    scores = low_back(jnp.einsum('qhd,khd->hqk', query, keys, precision=HIGHEST) * HD ** (-0.5))
    index = jnp.arange(SEQ)
    scores = jnp.where((index[None, :] <= index[:, None])[None], scores, -1e+30)
    shifted = jnp.exp(scores - lax.optimization_barrier(jnp.max(scores, -1, keepdims=True)))
    probs = shifted / lax.optimization_barrier(jnp.sum(shifted, -1, keepdims=True))
    attended = jnp.einsum('hqk,khd->qhd', low(probs), values, precision=HIGHEST)
    attended = low(low_back(attended)).reshape(SEQ, HEADS * HD)
    hidden_pre = low_back(matmul(normed[:, 3], up_weight))
    hidden = low(jax.nn.gelu(hidden_pre, approximate=False))
    branch = low_back(matmul(attended, out_weight) + matmul(hidden, down_weight))
    return (low(streams[:, 3] + branch), mixing)

def reference(history, mixer_in, mixer_out, mixer_bias, norm_gain, query_weight, key_weight, value_weight, out_weight, up_weight, down_weight, target, loss_count, domain, domain_scale):
    params = tuple((item.astype(jnp.float32) for item in (mixer_in, mixer_out, mixer_bias, norm_gain, query_weight, key_weight, value_weight, out_weight, up_weight, down_weight)))
    stored = jnp.moveaxis(history.astype(jnp.float32).reshape(LAYERS, SEQS, SEQ, D), 1, 0)

    def forward(params, stored):

        def step(carry, piece):
            return (carry, jax.checkpoint(block)(params, piece))
        carry, (outputs, mixings) = lax.scan(step, jnp.zeros((), jnp.float32), stored)
        return (outputs.reshape(TOKENS, D), mixings.reshape(TOKENS, STREAMS, LAYERS))
    (output, mixing), pullback = jax.vjp(forward, params, stored)
    row_seq = (jnp.arange(TOKENS) // SEQ).astype(jnp.int32)
    row_domain = domain[row_seq].astype(jnp.int32)
    row_scale = domain_scale[row_domain] * loss_count.astype(jnp.float32)
    cotangent = target.astype(jnp.float32) * row_scale[:, None]
    grads, stored_grad = pullback((cotangent, jnp.zeros_like(mixing)))
    history_grad = jnp.moveaxis(stored_grad, 0, 1).reshape(LAYERS, TOKENS, D).astype(jnp.bfloat16)
    return (output.astype(jnp.bfloat16), mixing, history_grad, grads[0], grads[1], grads[2], grads[3], grads[4], grads[5], grads[6], grads[7], grads[8], grads[9])
```

```python
import jax
import jax.numpy as jnp
from jax import lax
from jax.experimental import pallas as pl
from jax.experimental.pallas import tpu as pltpu
from jax.sharding import PartitionSpec as P

HD = 128
ROT = 32
STREAMS = 4
LANES = 128
GROUP = 16

HIGHEST = lax.Precision.HIGHEST
EPS_NORM = 1e-05
EPS_RMS = 1e-06
ROPE_BASE = 10000.0
VMEM = 56 * 2**20
PLANE = ("hist", "mp")


def dot(left, right, contract):
    return lax.dot_general(
        left, right, (((contract[0],), (contract[1],)), ((), ())), preferred_element_type=jnp.float32
    )


def gelu_exact(value):
    return 0.5 * value * (1.0 + lax.erf(value * 0.7071067811865476))


def gelu_slope(value):
    return (
        0.5 * (1.0 + lax.erf(value * 0.7071067811865476))
        + value * jnp.exp(-0.5 * value * value) * 0.3989422804014327
    )


class Plane:
    def __init__(self):
        self.size = lax.axis_size("hist")
        self.cores = lax.axis_size("mp")
        self.bits = self.size.bit_length() - 1
        assert self.size == 1 << self.bits
        self.h = lax.axis_index("hist")
        self.m = lax.axis_index("mp")

    def turned(self, j):
        return sum(((j >> b) & 1) << (self.bits - 1 - b) for b in range(self.bits))

    def place(self, j):
        return jnp.where(self.m % 2 == 0, j, self.turned(j))

    def step(self, value, i):
        pairs = []
        for h in range(self.size):
            for m in range(self.cores):
                bit = 1 << (i if m % 2 == 0 else self.bits - 1 - i)
                pairs.append((h * self.cores + m, (h ^ bit) * self.cores + m))
        return lax.ppermute(value, PLANE, pairs)

    def gather(self, value):
        slots = [value]
        for i in range(self.bits):
            slots = slots + [self.step(s, i) for s in slots]
        return slots

    def scatter(self, held):
        for i in reversed(range(self.bits)):
            got = [self.step(x, i) for x in held[1 << i :]]
            held = [
                (x.astype(jnp.float32) + y.astype(jnp.float32)).astype(jnp.bfloat16)
                for x, y in zip(held[: 1 << i], got)
            ]
        return held[0]

    def ordered(self, slots):
        rows = slots[0].shape[0]
        out = jnp.zeros((self.size * rows,) + slots[0].shape[1:], slots[0].dtype)
        for j, slot in enumerate(slots):
            out = lax.dynamic_update_slice_in_dim(out, slot, (self.h ^ self.place(j)) * rows, 0)
        return out

    def trade(self, wide):
        cols = wide.shape[1] // self.size
        block = lambda r: lax.dynamic_slice_in_dim(wide, (self.h ^ r) * cols, cols, 1)
        return [block(0)] + [
            lax.ppermute(block(r), "hist", [(h, h ^ r) for h in range(self.size)]) for r in range(1, self.size)
        ]

    def trade_rows(self, tall):
        rows = tall.shape[0] // self.size
        block = lambda r: lax.dynamic_slice_in_dim(tall, (self.h ^ r) * rows, rows, 0)
        return [block(0)] + [
            lax.ppermute(block(r), "hist", [(h, h ^ r) for h in range(self.size)]) for r in range(1, self.size)
        ]

    def stacked(self, entries):
        rows = entries[0].shape[0]
        out = jnp.zeros((self.size * rows,) + entries[0].shape[1:], entries[0].dtype)
        for r, entry in enumerate(entries):
            out = lax.dynamic_update_slice_in_dim(out, entry, (self.h ^ r) * rows, 0)
        return out

    def swap(self, value):
        return lax.ppermute(value, "mp", [(m, m ^ 1) for m in range(self.cores)])

    def both(self, own, sibling, axis):
        first = self.m % 2 == 0
        return jnp.stack([jnp.where(first, own, sibling), jnp.where(first, sibling, own)], axis)


def forward_kernel(count, pick, *refs):
    slots = refs[:count]
    in_ref, out_ref, bias_ref, gain_ref = refs[count : count + 4]
    normed = refs[count + 4 : count + 4 + STREAMS]
    mix_ref, pre_ref, stat_ref, last_ref = refs[count + 4 + STREAMS :]
    for j in range(count):

        @pl.when(pick[0] == j)
        def _(j=j):
            last_ref[...] = slots[j][...]

    tile = last_ref.shape[0]
    last = last_ref[...].astype(jnp.float32)
    inverse = lax.rsqrt(jnp.mean(last * last, -1, keepdims=True) + EPS_RMS)
    unit = (last * inverse).astype(jnp.bfloat16)
    pre = jnp.dot(unit, in_ref[...], preferred_element_type=jnp.float32)
    pre_ref[...] = pre
    hidden = gelu_exact(pre).astype(jnp.bfloat16)
    mix_ref[...] = (
        jnp.dot(hidden, out_ref[...], preferred_element_type=jnp.float32) + bias_ref[...]
    )
    lane = lax.broadcasted_iota(jnp.int32, (GROUP, LANES), 1)

    def group(g, carry):
        rows = pl.ds(pl.multiple_of(g * GROUP, GROUP), GROUP)
        mix = mix_ref[rows, :]
        parts = [s[rows, :].astype(jnp.float32) for s in slots]
        stat = jnp.zeros((GROUP, LANES), jnp.float32)
        for c in range(STREAMS):
            stream = mix[:, c * count : c * count + 1] * parts[0]
            for j in range(1, count):
                stream = stream + mix[:, c * count + j : c * count + j + 1] * parts[j]
            centered = stream - jnp.mean(stream, -1, keepdims=True)
            scale = lax.rsqrt(jnp.mean(centered * centered, -1, keepdims=True) + EPS_NORM)
            normed[c][rows, :] = (centered * scale * gain_ref[c : c + 1, :]).astype(jnp.bfloat16)
            stat = jnp.where(lane == c, scale, stat)
        stat_ref[rows, :] = stat
        return carry

    lax.fori_loop(0, tile // GROUP, group, 0)


def forward_streams(slots, pick, mixer_in, mixer_out, bias, gain):
    count = len(slots)
    rows, width = slots[0].shape
    tile = min(128, rows)
    whole = lambda shape: pl.BlockSpec(shape, lambda i: (0,) * len(shape))
    by_row = lambda cols: pl.BlockSpec((tile, cols), lambda i: (i, 0))
    return pl.pallas_call(
        lambda *refs: forward_kernel(count, *refs),
        grid=(rows // tile,),
        in_specs=[pl.BlockSpec(memory_space=pltpu.SMEM)]
        + [by_row(width)] * count
        + [whole(mixer_in.shape), whole(mixer_out.shape), whole(bias.shape), whole(gain.shape)],
        out_specs=[by_row(width)] * STREAMS + [by_row(LANES)] * 3,
        out_shape=[jax.ShapeDtypeStruct((rows, width), jnp.bfloat16)] * STREAMS
        + [jax.ShapeDtypeStruct((rows, LANES), jnp.float32)] * 3,
        scratch_shapes=[pltpu.VMEM((tile, width), jnp.bfloat16)],
        compiler_params=pltpu.CompilerParams(vmem_limit_bytes=VMEM),
        cost_estimate=pl.CostEstimate(
            flops=rows * width * 80, bytes_accessed=rows * width * 2 * (count + STREAMS), transcendentals=0
        ),
        name="forward_streams",
    )(pick, *slots, mixer_in, mixer_out, bias, gain)


def split_dot(left, right, contract):
    high = right.astype(jnp.bfloat16)
    low = (right - high.astype(jnp.float32)).astype(jnp.bfloat16)
    return dot(left, high, contract) + dot(left, low, contract)


def backward_kernel(count, pick, *refs):
    slots, refs = refs[:count], refs[count:]
    mine, refs = refs[:STREAMS], refs[STREAMS:]
    theirs, refs = refs[:STREAMS], refs[STREAMS:]
    normed, refs = refs[:STREAMS], refs[STREAMS:]
    mix_ref, pre_ref, stat_ref, target_ref, scale_ref, refs = *refs[:5], refs[5:]
    in_ref, out_ref, gain_ref, inverse_gain_ref, refs = *refs[:4], refs[4:]
    grads, refs = refs[:count], refs[count:]
    gain_grad_ref, in_grad_ref, out_grad_ref, bias_grad_ref, last_ref, dmix_ref, gain_sum = refs
    tile = last_ref.shape[0]

    @pl.when(pl.program_id(0) == 0)
    def _():
        gain_sum[...] = jnp.zeros_like(gain_sum)
        in_grad_ref[...] = jnp.zeros_like(in_grad_ref)
        out_grad_ref[...] = jnp.zeros_like(out_grad_ref)
        bias_grad_ref[...] = jnp.zeros_like(bias_grad_ref)

    for j in range(count):

        @pl.when(pick[0] == j)
        def _(j=j):
            last_ref[...] = slots[j][...]

    lane = lax.broadcasted_iota(jnp.int32, (GROUP, LANES), 1)

    def group(g, carry):
        rows = pl.ds(pl.multiple_of(g * GROUP, GROUP), GROUP)
        mix = mix_ref[rows, :]
        stat = stat_ref[rows, :]
        dmix = jnp.zeros((GROUP, LANES), jnp.float32)
        grad = []
        for c in range(STREAMS):
            total = mine[c][rows, :].astype(jnp.float32) + theirs[c][rows, :].astype(jnp.float32)
            unit = normed[c][rows, :].astype(jnp.float32) * inverse_gain_ref[c : c + 1, :]
            product = total * unit
            gain_sum[c] += product[:8] + product[8:]
            scaled = total * gain_ref[c : c + 1, :]
            mean = jnp.mean(scaled, -1, keepdims=True)
            along = jnp.mean(product * gain_ref[c : c + 1, :], -1, keepdims=True)
            one = stat[:, c : c + 1] * (scaled - mean - unit * along)
            if c == STREAMS - 1:
                one = one + target_ref[rows, :].astype(jnp.float32) * scale_ref[rows, :1]
            grad.append(one)
        for j in range(count):
            part = slots[j][rows, :].astype(jnp.float32)
            total = mix[:, j : j + 1] * grad[0]
            for c in range(1, STREAMS):
                total = total + mix[:, c * count + j : c * count + j + 1] * grad[c]
            grads[j][rows, :] = total.astype(jnp.bfloat16)
            for c in range(STREAMS):
                value = jnp.sum(grad[c] * part, -1, keepdims=True)
                dmix = jnp.where(lane == c * count + j, value, dmix)
        dmix_ref[rows, :] = dmix
        return carry

    lax.fori_loop(0, tile // GROUP, group, 0)
    dmix = dmix_ref[...]
    last = last_ref[...].astype(jnp.float32)
    inverse = lax.rsqrt(jnp.mean(last * last, -1, keepdims=True) + EPS_RMS)
    unit = (last * inverse).astype(jnp.bfloat16)
    pre = pre_ref[...]
    hidden = gelu_exact(pre).astype(jnp.bfloat16)
    hidden_grad = lax.dot_general(
        dmix,
        out_ref[...].astype(jnp.float32),
        (((1,), (1,)), ((), ())),
        precision=HIGHEST,
        preferred_element_type=jnp.float32,
    )
    pre_grad = hidden_grad * gelu_slope(pre)
    in_grad_ref[...] += split_dot(unit, pre_grad, (0, 0))
    out_grad_ref[...] += split_dot(hidden, dmix, (0, 0))
    bias_grad_ref[...] += jnp.sum(dmix, 0, keepdims=True)
    high = pre_grad.astype(jnp.bfloat16)
    low = (pre_grad - high.astype(jnp.float32)).astype(jnp.bfloat16)
    unit_grad = dot(high, in_ref[...], (1, 1)) + dot(low, in_ref[...], (1, 1))
    cube = inverse * inverse * inverse * jnp.mean(unit_grad * last, -1, keepdims=True)
    extra = inverse * unit_grad - last * cube
    for j in range(count):

        @pl.when(pick[0] == j)
        def _(j=j):
            grads[j][...] = (grads[j][...].astype(jnp.float32) + extra).astype(jnp.bfloat16)

    @pl.when(pl.program_id(0) == pl.num_programs(0) - 1)
    def _():
        gain_grad_ref[...] = jnp.sum(gain_sum[...], 1)


def backward_streams(slots, mine, theirs, at, normed, mix, pre, stat, target, scale, pick, mixer_in, mixer_out, gain):
    count = len(slots)
    rows, width = slots[0].shape
    tile = min(128, rows)
    steps = rows // tile
    whole = lambda shape: pl.BlockSpec(shape, lambda i: (0,) * len(shape))
    by_row = lambda cols: pl.BlockSpec((tile, cols), lambda i: (i, 0))
    shifted = pl.BlockSpec((tile, width), lambda i: (at * steps + i, 0))
    hidden = mixer_in.shape[1]
    return pl.pallas_call(
        lambda *refs: backward_kernel(count, *refs),
        grid=(steps,),
        in_specs=[pl.BlockSpec(memory_space=pltpu.SMEM)]
        + [by_row(width)] * count
        + [shifted] * (2 * STREAMS)
        + [by_row(width)] * STREAMS
        + [by_row(LANES)] * 3
        + [by_row(width), by_row(LANES)]
        + [whole(mixer_in.shape), whole(mixer_out.shape), whole(gain.shape), whole(gain.shape)],
        out_specs=[by_row(width)] * count
        + [whole((STREAMS, width)), whole((width, hidden)), whole((hidden, LANES)), whole((1, LANES))],
        out_shape=[jax.ShapeDtypeStruct((rows, width), jnp.bfloat16)] * count
        + [
            jax.ShapeDtypeStruct((STREAMS, width), jnp.float32),
            jax.ShapeDtypeStruct((width, hidden), jnp.float32),
            jax.ShapeDtypeStruct((hidden, LANES), jnp.float32),
            jax.ShapeDtypeStruct((1, LANES), jnp.float32),
        ],
        scratch_shapes=[
            pltpu.VMEM((tile, width), jnp.bfloat16),
            pltpu.VMEM((tile, LANES), jnp.float32),
            pltpu.VMEM((STREAMS, 8, width), jnp.float32),
        ],
        compiler_params=pltpu.CompilerParams(vmem_limit_bytes=VMEM),
        cost_estimate=pl.CostEstimate(
            flops=rows * width * 160,
            bytes_accessed=rows * width * 2 * (2 * count + 3 * STREAMS),
            transcendentals=0,
        ),
        name="backward_streams",
    )(pick, *slots, *mine, *theirs, *normed, mix, pre, stat, target, scale, mixer_in, mixer_out, gain, 1.0 / gain)


def rope_tables(positions):
    side = ROT // 2
    freq = ROPE_BASE ** (-2.0 * jnp.arange(side, dtype=jnp.float32) / ROT)
    angle = positions.astype(jnp.float32)[:, None] * freq[None, :]
    cosine, sine = jnp.cos(angle), jnp.sin(angle)
    rest = HD - ROT
    return (
        jnp.pad(jnp.concatenate([cosine, cosine], 1), ((0, 0), (0, rest)), constant_values=1.0),
        jnp.pad(-sine, ((0, 0), (0, HD - side))),
        jnp.pad(sine, ((0, 0), (side, rest))),
    )


def turn(value, cosine, right, left, sign):
    side = ROT // 2
    moved = pltpu.roll(value, HD - side, 1) * right + pltpu.roll(value, side, 1) * left
    return value * cosine + moved * sign


def attention_kernel(count, half, heads, which, *refs):
    q_ref, k_ref, v_ref, g_ref, cos_ref, right_ref, left_ref = refs[:7]
    o_ref, dq_ref, dk_ref, dv_ref = refs[7:11]
    k_s, dk_s, dv_s, p_s, o_s, dq_s, top_s, sum_s = refs[11:]
    blocks = 2 * count
    scale = HD ** (-0.5)
    bf16, f32 = jnp.bfloat16, jnp.float32
    m = which[0]

    def at(b):
        return pl.ds(pl.multiple_of(((lax.rem(b, 2) ^ m) * count + lax.div(b, 2)) * half, half), half)

    def cols(n):
        return slice(n * HD, (n + 1) * HD)

    def prepare(b, carry):
        rows = pl.ds(pl.multiple_of(b * half, half), half)
        for n in range(heads):
            k_s[rows, cols(n)] = turn(
                k_ref[rows, cols(n)], cos_ref[rows, :], right_ref[rows, :], left_ref[rows, :], 1.0
            ).astype(bf16)
        dk_s[rows, :] = jnp.zeros((half, heads * HD), f32)
        dv_s[rows, :] = jnp.zeros((half, heads * HD), f32)
        return carry

    lax.fori_loop(0, blocks, prepare, 0)
    later = lax.broadcasted_iota(jnp.int32, (half, half), 1) > lax.broadcasted_iota(jnp.int32, (half, half), 0)

    def lanes(value, op):
        parts = [value[:, i : i + LANES] for i in range(0, value.shape[1], LANES)]
        out = parts[0]
        for part in parts[1:]:
            out = op(out, part)
        return out

    def query_block(i, carry):
        here = at(i)
        queries = [
            turn(
                q_ref[here, cols(n)], cos_ref[here, :], right_ref[here, :], left_ref[here, :], 1.0
            ).astype(bf16)
            for n in range(heads)
        ]
        grads = [g_ref[here, cols(n)] for n in range(heads)]

        def scores(j, last):
            there = at(j)
            for n in range(heads):
                s = dot(queries[n], k_s[there, cols(n)], (1, 1)) * scale
                if last:
                    s = jnp.where(later, -1e30, s)
                p_s[n, :, pl.ds(pl.multiple_of(j * half, half), half)] = s
                top = lanes(s, jnp.maximum)
                top_s[n] = jnp.maximum(top_s[n], top)

        top_s[...] = jnp.full(top_s.shape, -1e30, f32)
        lax.fori_loop(0, i, lambda j, c: (scores(j, False), c)[1], 0)
        scores(i, True)
        tops = [jnp.max(top_s[n], -1, keepdims=True) for n in range(heads)]
        o_s[...] = jnp.zeros(o_s.shape, f32)
        dq_s[...] = jnp.zeros(dq_s.shape, f32)
        sum_s[...] = jnp.zeros(sum_s.shape, f32)

        def mixing(j, c):
            there = at(j)
            spot = pl.ds(pl.multiple_of(j * half, half), half)
            for n in range(heads):
                p = jnp.exp(p_s[n, :, spot] - tops[n])
                p_s[n, :, spot] = p
                sum_s[n] += lanes(p, jnp.add)
                o_s[n] += dot(p.astype(bf16), v_ref[there, cols(n)], (1, 0))
            return c

        lax.fori_loop(0, i + 1, mixing, 0)
        shares, deltas = [], []
        for n in range(heads):
            share = 1.0 / jnp.sum(sum_s[n], -1, keepdims=True)
            found = o_s[n] * share
            o_ref[here, cols(n)] = found.astype(bf16)
            shares.append(share)
            deltas.append(jnp.sum(found * grads[n].astype(f32), -1, keepdims=True))

        def back(j, c):
            there = at(j)
            spot = pl.ds(pl.multiple_of(j * half, half), half)
            for n in range(heads):
                p = p_s[n, :, spot] * shares[n]
                dp = dot(grads[n], v_ref[there, cols(n)], (1, 1))
                ds = (p * (dp - deltas[n])).astype(bf16)
                dq_s[n] += dot(ds, k_s[there, cols(n)], (1, 0))
                dk_s[there, cols(n)] += dot(ds, queries[n], (0, 0))
                dv_s[there, cols(n)] += dot(p.astype(bf16), grads[n], (0, 0))
            return c

        lax.fori_loop(0, i + 1, back, 0)
        for n in range(heads):
            dq_ref[here, cols(n)] = turn(
                dq_s[n] * scale, cos_ref[here, :], right_ref[here, :], left_ref[here, :], -1.0
            ).astype(bf16)
        return carry

    lax.fori_loop(0, blocks, query_block, 0)

    def finish(b, carry):
        rows = pl.ds(pl.multiple_of(b * half, half), half)
        for n in range(heads):
            dk_ref[rows, cols(n)] = turn(
                dk_s[rows, cols(n)] * scale, cos_ref[rows, :], right_ref[rows, :], left_ref[rows, :], -1.0
            ).astype(bf16)
        dv_ref[rows, :] = dv_s[rows, :].astype(bf16)
        return carry

    lax.fori_loop(0, blocks, finish, 0)


def attention(query, keys, values, grad, positions, which, count):
    rows, piece = query.shape
    heads, half = piece // HD, rows // (2 * count)
    vmem = pl.BlockSpec(memory_space=pltpu.VMEM)
    out = jax.ShapeDtypeStruct((rows, piece), jnp.bfloat16)
    wide = lambda *shape: pltpu.VMEM(shape, jnp.float32)
    return pl.pallas_call(
        lambda *refs: attention_kernel(count, half, heads, *refs),
        in_specs=[pl.BlockSpec(memory_space=pltpu.SMEM)] + [vmem] * 7,
        out_specs=[vmem] * 4,
        out_shape=[out] * 4,
        scratch_shapes=[
            pltpu.VMEM((rows, piece), jnp.bfloat16),
            wide(rows, piece),
            wide(rows, piece),
            wide(heads, half, rows),
            wide(heads, half, HD),
            wide(heads, half, HD),
            wide(heads, half, LANES),
            wide(heads, half, LANES),
        ],
        compiler_params=pltpu.CompilerParams(vmem_limit_bytes=VMEM),
        cost_estimate=pl.CostEstimate(
            flops=6 * rows * rows * piece, bytes_accessed=rows * piece * 20, transcendentals=rows * rows * heads // 2
        ),
        name="attention",
    )(which, query, keys, values, grad, *rope_tables(positions))


def interleave(own, sibling, m):
    count = len(own)
    half, width = own[0].shape

    def kernel(which, *refs):
        out, sems = refs[2 * count], refs[2 * count + 1]
        copies = []
        for a in range(count):
            copies.append(pltpu.make_async_copy(refs[a], out.at[a, which[0]], sems.at[a]))
            copies.append(pltpu.make_async_copy(refs[count + a], out.at[a, 1 - which[0]], sems.at[count + a]))
        for copy in copies:
            copy.start()
        for copy in copies:
            copy.wait()

    return pl.pallas_call(
        kernel,
        in_specs=[pl.BlockSpec(memory_space=pltpu.SMEM)] + [pl.BlockSpec(memory_space=pl.ANY)] * (2 * count),
        out_specs=pl.BlockSpec(memory_space=pl.ANY),
        out_shape=jax.ShapeDtypeStruct((count, 2, half, width), own[0].dtype),
        scratch_shapes=[pltpu.SemaphoreType.DMA((2 * count,))],
        name="interleave",
    )(m, *own, *sibling)


def place_wide(entries, h, out_type, pieces, turned):
    count = len(entries)
    depth, cols = entries[0].shape
    size = cols // pieces

    def kernel(which, *refs):
        a = pl.program_id(0)
        for r in range(count):

            @pl.when((which[0] ^ a) == r)
            def _(r=r):
                for i in range(pieces):
                    block = refs[r][:, i * size : (i + 1) * size].astype(jnp.float32)
                    refs[count + i][...] = block.T if turned[i] else block

    return pl.pallas_call(
        kernel,
        grid=(count,),
        in_specs=[pl.BlockSpec(memory_space=pltpu.SMEM)] + [pl.BlockSpec((depth, cols), lambda a: (0, 0))] * count,
        out_specs=[
            pl.BlockSpec((size, depth), lambda a: (a, 0)) if t else pl.BlockSpec((depth, size), lambda a: (0, a))
            for t in turned
        ],
        out_shape=[
            jax.ShapeDtypeStruct((count * size, depth) if t else (depth, count * size), out_type) for t in turned
        ],
        compiler_params=pltpu.CompilerParams(vmem_limit_bytes=VMEM),
        name="place_wide",
    )(h, *entries)


def after(value, *others):
    return lax.optimization_barrier((value,) + others)[0]


def shards(
    history,
    mixer_in,
    mixer_out,
    mixer_bias,
    norm_gain,
    query_weight,
    key_weight,
    value_weight,
    out_weight,
    up_weight,
    down_weight,
    target,
    loss_count,
    domain,
    domain_scale,
):
    plane = Plane()
    count, cores, h, m = plane.size, plane.cores, plane.h, plane.m
    layers, group_rows, width = history.shape
    rows = target.shape[0]
    half = rows // cores
    depth = query_weight.shape[0]
    assert layers == 1 and cores == 2 and domain.shape[0] == 1 and group_rows == count * rows
    hidden_units = mixer_in.shape[1]
    bf16, f32 = jnp.bfloat16, jnp.float32

    near = count * half
    which_m = m.astype(jnp.int32).reshape(1)
    which_h = h.astype(jnp.int32).reshape(1)

    z, zs = lax.axis_index("dp"), lax.axis_size("dp")
    part = plane.ordered([x[None] for x in plane.gather(norm_gain)])
    gain = lax.dynamic_update_slice_in_dim(jnp.zeros((zs,) + part.shape, bf16), part[None], z, 0)
    for k in range(1, zs):
        came = lax.ppermute(part, "dp", [(i, (i + k) % zs) for i in range(zs)])
        gain = lax.dynamic_update_slice_in_dim(gain, came[None], (z + zs - k) % zs, 0)
    gain = gain.reshape(zs * count, STREAMS, -1).transpose(1, 0, 2).reshape(STREAMS, width).astype(f32)

    parted = history.reshape(count, cores, half, width)
    own_rows = [lax.dynamic_index_in_dim(parted[a], m, 0, keepdims=False) for a in range(count)]
    up_parts = plane.trade(up_weight)
    up_full = lax.all_gather(plane.stacked(up_parts), "dp", axis=0, tiled=True)
    slots, waited = [], up_parts[-1]
    marks = []
    for a in range(count):
        found = plane.gather(after(own_rows[a], waited))
        waited = found[1]
        marks.append(waited)
        slots.append(found)
    down_parts = plane.trade(after(down_weight, marks[0]).T)
    down_full = lax.all_gather(plane.stacked(down_parts), "dp", axis=0, tiled=True)
    packed = jnp.stack(
        [query_weight, key_weight, value_weight, after(out_weight, marks[min(1, count - 1)]).T], 0
    )
    packed = packed.reshape(4, depth, count, -1).transpose(1, 2, 0, 3).reshape(depth, -1)
    narrow_full = lax.all_gather(plane.stacked(plane.trade(packed)), "dp", axis=0, tiled=True)
    piece = narrow_full.shape[1] // 4
    query_full, key_full, value_full, out_full = (
        narrow_full[:, i * piece : (i + 1) * piece] for i in range(4)
    )

    layer_of = [h ^ plane.place(j) for j in range(count)]
    pick = sum(jnp.where(layer_of[j] == count - 1, j, 0) for j in range(count)).astype(jnp.int32).reshape(1)

    def to_slots(values):
        return jnp.stack(
            [sum(jnp.where(layer_of[j] == l, values[..., l], 0) for l in range(count)) for j in range(count)], -1
        )

    def from_slots(values):
        return jnp.stack(
            [sum(jnp.where(layer_of[j] == l, values[..., j], 0) for j in range(count)) for l in range(count)], -1
        )

    pairs = STREAMS * count
    in_wide = jnp.pad(mixer_in, ((0, 0), (0, LANES - hidden_units)))
    out_wide = jnp.pad(
        to_slots(mixer_out).reshape(hidden_units, pairs), ((0, LANES - hidden_units), (0, LANES - pairs))
    )
    bias_wide = jnp.pad(to_slots(mixer_bias).reshape(1, pairs), ((0, 0), (0, LANES - pairs)))

    normed, mixes, pres, stats, others = [], [], [], [], []
    for a in range(count):
        *one, mix, pre, stat = forward_streams(slots[a], pick, in_wide, out_wide, bias_wide, gain)
        normed.append(one)
        mixes.append(mix)
        pres.append(pre)
        stats.append(stat)
        others.append([plane.swap(x) for x in one])
    streams = [jnp.concatenate([x[c] for x in normed + others], 0) for c in range(STREAMS)]
    block = jnp.arange(count)[:, None] * rows + jnp.arange(half)[None, :]
    positions = jnp.concatenate([(block + m * half).reshape(-1), (block + (1 - m) * half).reshape(-1)])

    domain_one = jnp.sum(jnp.where(jnp.arange(domain_scale.shape[0]) == domain[0], domain_scale, 0.0))
    own_target = lax.dynamic_slice_in_dim(target, m * half, half, 0)
    own_scale = lax.dynamic_slice_in_dim(loss_count, m * half, half, 0).astype(f32) * domain_one
    branch_own = (own_target.astype(f32) * own_scale[:, None]).astype(bf16)
    branch_near = plane.ordered(plane.gather(after(branch_own, marks[-1])))
    branch_grad = jnp.concatenate([branch_near, plane.swap(branch_near)], 0)

    hidden_pre = dot(streams[3], up_full, (1, 0))
    hidden = gelu_exact(hidden_pre).astype(bf16)
    act_grad = dot(branch_grad, down_full, (1, 0))
    pre_grad = (act_grad * gelu_slope(hidden_pre)).astype(bf16)
    down_part = dot(branch_grad, hidden, (0, 0)).astype(bf16)
    up_part = dot(streams[3], pre_grad, (0, 0)).astype(bf16)

    streams[0], streams[1], streams[2] = lax.optimization_barrier(
        (streams[0], streams[1], streams[2], up_part, down_part)
    )[:3]
    query = dot(streams[0], query_full, (1, 0))
    keys = dot(streams[1], key_full, (1, 0))
    values = dot(streams[2], value_full, (1, 0)).astype(bf16)
    attended_grad = dot(branch_grad, out_full, (1, 0)).astype(bf16)
    attended, query_back, key_back, value_back = attention(
        query, keys, values, attended_grad, positions, which_m, count
    )

    branch_far = (
        dot(attended[near:], out_full, (1, 1)) + dot(hidden[near:], down_full, (1, 1))
    ).astype(bf16)
    query_back, key_back, value_back, branch_far = lax.optimization_barrier(
        (query_back, key_back, value_back, branch_far)
    )
    branch = dot(attended[:near], out_full, (1, 1)) + dot(hidden[:near], down_full, (1, 1))
    branch_sum = (branch + plane.swap(branch_far).astype(f32)).astype(bf16)
    branch_rows = plane.scatter(
        [lax.dynamic_slice_in_dim(branch_sum, layer_of[j] * half, half, 0) for j in range(count)]
    ).astype(f32)
    own_mix = lax.dynamic_index_in_dim(jnp.stack(mixes, 0), h, 0, keepdims=False)[:, :pairs]
    own_mix = own_mix.reshape(half, STREAMS, count)
    own_layers = [lax.dynamic_index_in_dim(jnp.stack([s[j] for s in slots], 0), h, 0, keepdims=False) for j in range(count)]
    residual = sum(own_mix[:, STREAMS - 1, j, None] * own_layers[j].astype(f32) for j in range(count))
    output_own = (residual + branch_rows).astype(bf16)
    output = plane.both(output_own, plane.swap(output_own), 0).reshape(rows, width)
    mix_own = from_slots(own_mix)
    mix_rows = plane.both(mix_own, plane.swap(mix_own), 0).reshape(rows, STREAMS, count)

    tails = [
        (query_back, query_full),
        (key_back, key_full),
        (value_back, value_full),
        (pre_grad, up_full),
    ]
    theirs = [plane.swap(dot(x[near:], w, (1, 1)).astype(bf16)) for x, w in tails]
    mine = [dot(x[:near], w, (1, 1)).astype(bf16) for x, w in tails]

    narrow_part = jnp.concatenate(
        [
            dot(streams[0], query_back, (0, 0)),
            dot(streams[1], key_back, (0, 0)),
            dot(streams[2], value_back, (0, 0)),
            dot(branch_grad, attended, (0, 0)),
        ],
        1,
    ).astype(bf16)

    def spread(part, turned):
        summed = lax.psum_scatter(part, "dp", scatter_dimension=0, tiled=True)
        return place_wide(plane.trade_rows(summed), which_h, f32, len(turned), turned)

    (up_grad,) = spread(up_part, (False,))
    (down_grad,) = spread(down_part, (True,))
    query_grad, key_grad, value_grad, out_grad = spread(narrow_part, (False, False, False, True))

    scale_wide = after(jnp.broadcast_to(own_scale[:, None], (half, LANES)), narrow_part)
    finals, sums = [], None
    for a in range(count):
        scale = jnp.where(h == a, scale_wide, 0.0)
        found = backward_streams(
            slots[a], mine, theirs, a, normed[a], mixes[a], pres[a], stats[a], own_target, scale, pick, in_wide, out_wide, gain
        )
        held, rest = list(found[:count]), found[count:]
        sums = rest if sums is None else tuple(x + y for x, y in zip(sums, rest))
        finals.append(plane.scatter(held))
    history_grad = interleave(finals, [plane.swap(x) for x in finals], which_m).reshape(history.shape)

    gain_sum, in_sum, out_sum, bias_sum = sums
    out_sum = from_slots(out_sum[:, :pairs].reshape(LANES, STREAMS, count)).reshape(LANES, pairs)
    bias_sum = from_slots(bias_sum[:, :pairs].reshape(1, STREAMS, count)).reshape(1, pairs)
    small = jnp.concatenate(
        [in_sum, gain_sum.T, jnp.pad(jnp.concatenate([out_sum, bias_sum], 0), ((0, width - LANES - 1), (0, 0)))], 1
    )
    small = lax.psum(small, ("dp", "hist", "mp"))
    mixer_in_grad = small[:, :hidden_units]
    gain_all = small[:, LANES : LANES + STREAMS].T
    place = (lax.axis_index("dp") * count + h) * norm_gain.shape[1]
    norm_gain_grad = lax.dynamic_slice_in_dim(gain_all, place, norm_gain.shape[1], 1)
    tail = small[:, LANES + STREAMS :]
    mixer_out_grad = tail[:hidden_units].reshape(hidden_units, STREAMS, count)
    mixer_bias_grad = tail[LANES].reshape(STREAMS, count)
    return (
        output,
        mix_rows,
        history_grad,
        mixer_in_grad,
        mixer_out_grad,
        mixer_bias_grad,
        norm_gain_grad,
        query_grad,
        key_grad,
        value_grad,
        out_grad,
        up_grad,
        down_grad,
    )


def solution(mesh):
    in_specs = (
        P("hist", "dp", None),
        P(),
        P(),
        P(),
        P(None, ("dp", "hist")),
        P(("dp", "hist"), "mp"),
        P(("dp", "hist"), "mp"),
        P(("dp", "hist"), "mp"),
        P("mp", ("dp", "hist")),
        P(("dp", "hist"), "mp"),
        P("mp", ("dp", "hist")),
        P(("dp", "hist"), None),
        P(("dp", "hist")),
        P("dp"),
        P(),
    )
    out_specs = (
        P(("dp", "hist"), None),
        P(("dp", "hist"), None, None),
        P("hist", "dp", None),
        P(),
        P(),
        P(),
        P(None, ("dp", "hist")),
        P(("dp", "hist"), "mp"),
        P(("dp", "hist"), "mp"),
        P(("dp", "hist"), "mp"),
        P("mp", ("dp", "hist")),
        P(("dp", "hist"), "mp"),
        P("mp", ("dp", "hist")),
    )
    return jax.shard_map(shards, mesh=mesh, in_specs=in_specs, out_specs=out_specs, check_vma=False)
```

```python
import jax
import jax.numpy as jnp
from jax import lax
from jax.experimental import pallas as pl
from jax.experimental.pallas import tpu as pltpu
from jax.sharding import PartitionSpec as P

HD = 128
ROT = 32
STREAMS = 4
LANES = 128
GROUP = 16

HIGHEST = lax.Precision.HIGHEST
EPS_NORM = 1e-05
EPS_RMS = 1e-06
ROPE_BASE = 10000.0
VMEM = 56 * 2**20
PLANE = ("hist", "mp")


def dot(left, right, contract):
    return lax.dot_general(
        left, right, (((contract[0],), (contract[1],)), ((), ())), preferred_element_type=jnp.float32
    )


def gelu_exact(value):
    return 0.5 * value * (1.0 + lax.erf(value * 0.7071067811865476))


def gelu_slope(value):
    return (
        0.5 * (1.0 + lax.erf(value * 0.7071067811865476))
        + value * jnp.exp(-0.5 * value * value) * 0.3989422804014327
    )


class Plane:
    def __init__(self):
        self.size = lax.axis_size("hist")
        self.cores = lax.axis_size("mp")
        self.bits = self.size.bit_length() - 1
        assert self.size == 1 << self.bits
        self.h = lax.axis_index("hist")
        self.m = lax.axis_index("mp")

    def turned(self, j):
        return sum(((j >> b) & 1) << (self.bits - 1 - b) for b in range(self.bits))

    def place(self, j):
        return jnp.where(self.m % 2 == 0, j, self.turned(j))

    def step(self, value, i):
        pairs = []
        for h in range(self.size):
            for m in range(self.cores):
                bit = 1 << (i if m % 2 == 0 else self.bits - 1 - i)
                pairs.append((h * self.cores + m, (h ^ bit) * self.cores + m))
        return lax.ppermute(value, PLANE, pairs)

    def gather(self, value):
        slots = [value]
        for i in range(self.bits):
            slots = slots + [self.step(s, i) for s in slots]
        return slots

    def scatter(self, held):
        for i in reversed(range(self.bits)):
            got = [self.step(x, i) for x in held[1 << i :]]
            held = [
                (x.astype(jnp.float32) + y.astype(jnp.float32)).astype(x.dtype)
                for x, y in zip(held[: 1 << i], got)
            ]
        return held[0]

    def ordered(self, slots):
        rows = slots[0].shape[0]
        out = jnp.zeros((self.size * rows,) + slots[0].shape[1:], slots[0].dtype)
        for j, slot in enumerate(slots):
            out = lax.dynamic_update_slice_in_dim(out, slot, (self.h ^ self.place(j)) * rows, 0)
        return out

    def trade(self, wide):
        cols = wide.shape[1] // self.size
        block = lambda r: lax.dynamic_slice_in_dim(wide, (self.h ^ r) * cols, cols, 1)
        return [block(0)] + [
            lax.ppermute(block(r), "hist", [(h, h ^ r) for h in range(self.size)]) for r in range(1, self.size)
        ]

    def trade_rows(self, tall):
        rows = tall.shape[0] // self.size
        block = lambda r: lax.dynamic_slice_in_dim(tall, (self.h ^ r) * rows, rows, 0)
        return [block(0)] + [
            lax.ppermute(block(r), "hist", [(h, h ^ r) for h in range(self.size)]) for r in range(1, self.size)
        ]

    def stacked(self, entries):
        rows = entries[0].shape[0]
        out = jnp.zeros((self.size * rows,) + entries[0].shape[1:], entries[0].dtype)
        for r, entry in enumerate(entries):
            out = lax.dynamic_update_slice_in_dim(out, entry, (self.h ^ r) * rows, 0)
        return out

    def swap(self, value):
        return lax.ppermute(value, "mp", [(m, m ^ 1) for m in range(self.cores)])

    def both(self, own, sibling, axis):
        first = self.m % 2 == 0
        return jnp.stack([jnp.where(first, own, sibling), jnp.where(first, sibling, own)], axis)


def forward_kernel(count, pick, *refs):
    slots = refs[:count]
    in_ref, out_ref, bias_ref, gain_ref = refs[count : count + 4]
    normed = refs[count + 4 : count + 4 + STREAMS]
    mix_ref, pre_ref, stat_ref, last_ref = refs[count + 4 + STREAMS :]
    for j in range(count):

        @pl.when(pick[0] == j)
        def _(j=j):
            last_ref[...] = slots[j][...]

    tile = last_ref.shape[0]
    last = last_ref[...].astype(jnp.float32)
    inverse = lax.rsqrt(jnp.mean(last * last, -1, keepdims=True) + EPS_RMS)
    unit = (last * inverse).astype(jnp.bfloat16)
    pre = jnp.dot(unit, in_ref[...], preferred_element_type=jnp.float32)
    pre_ref[...] = pre
    hidden = gelu_exact(pre).astype(jnp.bfloat16)
    mix_ref[...] = (
        jnp.dot(hidden, out_ref[...], preferred_element_type=jnp.float32) + bias_ref[...]
    )
    lane = lax.broadcasted_iota(jnp.int32, (GROUP, LANES), 1)

    def group(g, carry):
        rows = pl.ds(pl.multiple_of(g * GROUP, GROUP), GROUP)
        mix = mix_ref[rows, :]
        parts = [s[rows, :].astype(jnp.float32) for s in slots]
        stat = jnp.zeros((GROUP, LANES), jnp.float32)
        for c in range(STREAMS):
            stream = mix[:, c * count : c * count + 1] * parts[0]
            for j in range(1, count):
                stream = stream + mix[:, c * count + j : c * count + j + 1] * parts[j]
            centered = stream - jnp.mean(stream, -1, keepdims=True)
            scale = lax.rsqrt(jnp.mean(centered * centered, -1, keepdims=True) + EPS_NORM)
            normed[c][rows, :] = (centered * scale * gain_ref[c : c + 1, :]).astype(jnp.bfloat16)
            stat = jnp.where(lane == c, scale, stat)
        stat_ref[rows, :] = stat
        return carry

    lax.fori_loop(0, tile // GROUP, group, 0)


def forward_streams(slots, pick, mixer_in, mixer_out, bias, gain):
    count = len(slots)
    rows, width = slots[0].shape
    tile = min(128, rows)
    whole = lambda shape: pl.BlockSpec(shape, lambda i: (0,) * len(shape))
    by_row = lambda cols: pl.BlockSpec((tile, cols), lambda i: (i, 0))
    return pl.pallas_call(
        lambda *refs: forward_kernel(count, *refs),
        grid=(rows // tile,),
        in_specs=[pl.BlockSpec(memory_space=pltpu.SMEM)]
        + [by_row(width)] * count
        + [whole(mixer_in.shape), whole(mixer_out.shape), whole(bias.shape), whole(gain.shape)],
        out_specs=[by_row(width)] * STREAMS + [by_row(LANES)] * 3,
        out_shape=[jax.ShapeDtypeStruct((rows, width), jnp.bfloat16)] * STREAMS
        + [jax.ShapeDtypeStruct((rows, LANES), jnp.float32)] * 3,
        scratch_shapes=[pltpu.VMEM((tile, width), jnp.bfloat16)],
        compiler_params=pltpu.CompilerParams(vmem_limit_bytes=VMEM),
        cost_estimate=pl.CostEstimate(
            flops=rows * width * 80, bytes_accessed=rows * width * 2 * (count + STREAMS), transcendentals=0
        ),
        name="forward_streams",
    )(pick, *slots, mixer_in, mixer_out, bias, gain)


def split_dot(left, right, contract):
    high = right.astype(jnp.bfloat16)
    low = (right - high.astype(jnp.float32)).astype(jnp.bfloat16)
    return dot(left, high, contract) + dot(left, low, contract)


def backward_kernel(count, pick, *refs):
    slots, refs = refs[:count], refs[count:]
    mine, refs = refs[:STREAMS], refs[STREAMS:]
    theirs, refs = refs[:STREAMS], refs[STREAMS:]
    normed, refs = refs[:STREAMS], refs[STREAMS:]
    mix_ref, pre_ref, stat_ref, target_ref, scale_ref, refs = *refs[:5], refs[5:]
    in_ref, out_ref, gain_ref, inverse_gain_ref, refs = *refs[:4], refs[4:]
    grads, refs = refs[:count], refs[count:]
    gain_grad_ref, in_grad_ref, out_grad_ref, bias_grad_ref, last_ref, dmix_ref, gain_sum = refs
    tile = last_ref.shape[0]

    @pl.when(pl.program_id(0) == 0)
    def _():
        gain_sum[...] = jnp.zeros_like(gain_sum)
        in_grad_ref[...] = jnp.zeros_like(in_grad_ref)
        out_grad_ref[...] = jnp.zeros_like(out_grad_ref)
        bias_grad_ref[...] = jnp.zeros_like(bias_grad_ref)

    for j in range(count):

        @pl.when(pick[0] == j)
        def _(j=j):
            last_ref[...] = slots[j][...]

    lane = lax.broadcasted_iota(jnp.int32, (GROUP, LANES), 1)

    def group(g, carry):
        rows = pl.ds(pl.multiple_of(g * GROUP, GROUP), GROUP)
        mix = mix_ref[rows, :]
        stat = stat_ref[rows, :]
        dmix = jnp.zeros((GROUP, LANES), jnp.float32)
        grad = []
        for c in range(STREAMS):
            total = mine[c][rows, :].astype(jnp.float32) + theirs[c][rows, :].astype(jnp.float32)
            unit = normed[c][rows, :].astype(jnp.float32) * inverse_gain_ref[c : c + 1, :]
            product = total * unit
            gain_sum[c] += product[:8] + product[8:]
            scaled = total * gain_ref[c : c + 1, :]
            mean = jnp.mean(scaled, -1, keepdims=True)
            along = jnp.mean(product * gain_ref[c : c + 1, :], -1, keepdims=True)
            one = stat[:, c : c + 1] * (scaled - mean - unit * along)
            if c == STREAMS - 1:
                one = one + target_ref[rows, :].astype(jnp.float32) * scale_ref[rows, :1]
            grad.append(one)
        for j in range(count):
            part = slots[j][rows, :].astype(jnp.float32)
            total = mix[:, j : j + 1] * grad[0]
            for c in range(1, STREAMS):
                total = total + mix[:, c * count + j : c * count + j + 1] * grad[c]
            grads[j][rows, :] = total.astype(jnp.bfloat16)
            for c in range(STREAMS):
                value = jnp.sum(grad[c] * part, -1, keepdims=True)
                dmix = jnp.where(lane == c * count + j, value, dmix)
        dmix_ref[rows, :] = dmix
        return carry

    lax.fori_loop(0, tile // GROUP, group, 0)
    dmix = dmix_ref[...]
    last = last_ref[...].astype(jnp.float32)
    inverse = lax.rsqrt(jnp.mean(last * last, -1, keepdims=True) + EPS_RMS)
    unit = (last * inverse).astype(jnp.bfloat16)
    pre = pre_ref[...]
    hidden = gelu_exact(pre).astype(jnp.bfloat16)
    hidden_grad = lax.dot_general(
        dmix,
        out_ref[...].astype(jnp.float32),
        (((1,), (1,)), ((), ())),
        precision=HIGHEST,
        preferred_element_type=jnp.float32,
    )
    pre_grad = hidden_grad * gelu_slope(pre)
    in_grad_ref[...] += split_dot(unit, pre_grad, (0, 0))
    out_grad_ref[...] += split_dot(hidden, dmix, (0, 0))
    bias_grad_ref[...] += jnp.sum(dmix, 0, keepdims=True)
    high = pre_grad.astype(jnp.bfloat16)
    low = (pre_grad - high.astype(jnp.float32)).astype(jnp.bfloat16)
    unit_grad = dot(high, in_ref[...], (1, 1)) + dot(low, in_ref[...], (1, 1))
    cube = inverse * inverse * inverse * jnp.mean(unit_grad * last, -1, keepdims=True)
    extra = inverse * unit_grad - last * cube
    for j in range(count):

        @pl.when(pick[0] == j)
        def _(j=j):
            grads[j][...] = (grads[j][...].astype(jnp.float32) + extra).astype(jnp.bfloat16)

    @pl.when(pl.program_id(0) == pl.num_programs(0) - 1)
    def _():
        gain_grad_ref[...] = jnp.sum(gain_sum[...], 1)


def backward_streams(slots, mine, theirs, at, normed, mix, pre, stat, target, scale, pick, mixer_in, mixer_out, gain):
    count = len(slots)
    rows, width = slots[0].shape
    tile = min(128, rows)
    steps = rows // tile
    whole = lambda shape: pl.BlockSpec(shape, lambda i: (0,) * len(shape))
    by_row = lambda cols: pl.BlockSpec((tile, cols), lambda i: (i, 0))
    shifted = pl.BlockSpec((tile, width), lambda i: (at * steps + i, 0))
    hidden = mixer_in.shape[1]
    return pl.pallas_call(
        lambda *refs: backward_kernel(count, *refs),
        grid=(steps,),
        in_specs=[pl.BlockSpec(memory_space=pltpu.SMEM)]
        + [by_row(width)] * count
        + [shifted] * (2 * STREAMS)
        + [by_row(width)] * STREAMS
        + [by_row(LANES)] * 3
        + [by_row(width), by_row(LANES)]
        + [whole(mixer_in.shape), whole(mixer_out.shape), whole(gain.shape), whole(gain.shape)],
        out_specs=[by_row(width)] * count
        + [whole((STREAMS, width)), whole((width, hidden)), whole((hidden, LANES)), whole((1, LANES))],
        out_shape=[jax.ShapeDtypeStruct((rows, width), jnp.bfloat16)] * count
        + [
            jax.ShapeDtypeStruct((STREAMS, width), jnp.float32),
            jax.ShapeDtypeStruct((width, hidden), jnp.float32),
            jax.ShapeDtypeStruct((hidden, LANES), jnp.float32),
            jax.ShapeDtypeStruct((1, LANES), jnp.float32),
        ],
        scratch_shapes=[
            pltpu.VMEM((tile, width), jnp.bfloat16),
            pltpu.VMEM((tile, LANES), jnp.float32),
            pltpu.VMEM((STREAMS, 8, width), jnp.float32),
        ],
        compiler_params=pltpu.CompilerParams(vmem_limit_bytes=VMEM),
        cost_estimate=pl.CostEstimate(
            flops=rows * width * 160,
            bytes_accessed=rows * width * 2 * (2 * count + 3 * STREAMS),
            transcendentals=0,
        ),
        name="backward_streams",
    )(pick, *slots, *mine, *theirs, *normed, mix, pre, stat, target, scale, mixer_in, mixer_out, gain, 1.0 / gain)


def rope_tables(positions):
    side = ROT // 2
    freq = ROPE_BASE ** (-2.0 * jnp.arange(side, dtype=jnp.float32) / ROT)
    angle = positions.astype(jnp.float32)[:, None] * freq[None, :]
    cosine, sine = jnp.cos(angle), jnp.sin(angle)
    rest = HD - ROT
    return (
        jnp.pad(jnp.concatenate([cosine, cosine], 1), ((0, 0), (0, rest)), constant_values=1.0),
        jnp.pad(-sine, ((0, 0), (0, HD - side))),
        jnp.pad(sine, ((0, 0), (side, rest))),
    )


def turn(value, cosine, right, left, sign):
    side = ROT // 2
    moved = pltpu.roll(value, HD - side, 1) * right + pltpu.roll(value, side, 1) * left
    return value * cosine + moved * sign


def attention_kernel(count, half, heads, which, *refs):
    q_ref, k_ref, v_ref, g_ref, cos_ref, right_ref, left_ref = refs[:7]
    o_ref, dq_ref, dk_ref, dv_ref = refs[7:11]
    k_s, dk_s, dv_s, p_s, o_s, dq_s, top_s, sum_s = refs[11:]
    blocks = 2 * count
    scale = HD ** (-0.5)
    bf16, f32 = jnp.bfloat16, jnp.float32
    m = which[0]

    def at(b):
        return pl.ds(pl.multiple_of(((lax.rem(b, 2) ^ m) * count + lax.div(b, 2)) * half, half), half)

    def cols(n):
        return slice(n * HD, (n + 1) * HD)

    def prepare(b, carry):
        rows = pl.ds(pl.multiple_of(b * half, half), half)
        for n in range(heads):
            k_s[rows, cols(n)] = turn(
                k_ref[rows, cols(n)], cos_ref[rows, :], right_ref[rows, :], left_ref[rows, :], 1.0
            ).astype(bf16)
        dk_s[rows, :] = jnp.zeros((half, heads * HD), f32)
        dv_s[rows, :] = jnp.zeros((half, heads * HD), f32)
        return carry

    lax.fori_loop(0, blocks, prepare, 0)
    later = lax.broadcasted_iota(jnp.int32, (half, half), 1) > lax.broadcasted_iota(jnp.int32, (half, half), 0)

    def lanes(value, op):
        parts = [value[:, i : i + LANES] for i in range(0, value.shape[1], LANES)]
        out = parts[0]
        for part in parts[1:]:
            out = op(out, part)
        return out

    def query_block(i, carry):
        here = at(i)
        queries = [
            turn(
                q_ref[here, cols(n)], cos_ref[here, :], right_ref[here, :], left_ref[here, :], 1.0
            ).astype(bf16)
            for n in range(heads)
        ]
        grads = [g_ref[here, cols(n)] for n in range(heads)]

        def scores(j, last):
            there = at(j)
            for n in range(heads):
                s = dot(queries[n], k_s[there, cols(n)], (1, 1)) * scale
                if last:
                    s = jnp.where(later, -1e30, s)
                p_s[n, :, pl.ds(pl.multiple_of(j * half, half), half)] = s
                top = lanes(s, jnp.maximum)
                top_s[n] = jnp.maximum(top_s[n], top)

        top_s[...] = jnp.full(top_s.shape, -1e30, f32)
        lax.fori_loop(0, i, lambda j, c: (scores(j, False), c)[1], 0)
        scores(i, True)
        tops = [jnp.max(top_s[n], -1, keepdims=True) for n in range(heads)]
        o_s[...] = jnp.zeros(o_s.shape, f32)
        dq_s[...] = jnp.zeros(dq_s.shape, f32)
        sum_s[...] = jnp.zeros(sum_s.shape, f32)

        def mixing(j, c):
            there = at(j)
            spot = pl.ds(pl.multiple_of(j * half, half), half)
            for n in range(heads):
                p = jnp.exp(p_s[n, :, spot] - tops[n])
                p_s[n, :, spot] = p
                sum_s[n] += lanes(p, jnp.add)
                o_s[n] += dot(p.astype(bf16), v_ref[there, cols(n)], (1, 0))
            return c

        lax.fori_loop(0, i + 1, mixing, 0)
        shares, deltas = [], []
        for n in range(heads):
            share = 1.0 / jnp.sum(sum_s[n], -1, keepdims=True)
            found = o_s[n] * share
            o_ref[here, cols(n)] = found.astype(bf16)
            shares.append(share)
            deltas.append(jnp.sum(found * grads[n].astype(f32), -1, keepdims=True))

        def back(j, c):
            there = at(j)
            spot = pl.ds(pl.multiple_of(j * half, half), half)
            for n in range(heads):
                p = p_s[n, :, spot] * shares[n]
                dp = dot(grads[n], v_ref[there, cols(n)], (1, 1))
                ds = (p * (dp - deltas[n])).astype(bf16)
                dq_s[n] += dot(ds, k_s[there, cols(n)], (1, 0))
                dk_s[there, cols(n)] += dot(ds, queries[n], (0, 0))
                dv_s[there, cols(n)] += dot(p.astype(bf16), grads[n], (0, 0))
            return c

        lax.fori_loop(0, i + 1, back, 0)
        for n in range(heads):
            dq_ref[here, cols(n)] = turn(
                dq_s[n] * scale, cos_ref[here, :], right_ref[here, :], left_ref[here, :], -1.0
            ).astype(bf16)
        return carry

    lax.fori_loop(0, blocks, query_block, 0)

    def finish(b, carry):
        rows = pl.ds(pl.multiple_of(b * half, half), half)
        for n in range(heads):
            dk_ref[rows, cols(n)] = turn(
                dk_s[rows, cols(n)] * scale, cos_ref[rows, :], right_ref[rows, :], left_ref[rows, :], -1.0
            ).astype(bf16)
        dv_ref[rows, :] = dv_s[rows, :].astype(bf16)
        return carry

    lax.fori_loop(0, blocks, finish, 0)


def attention(query, keys, values, grad, positions, which, count):
    rows, piece = query.shape
    heads, half = piece // HD, rows // (2 * count)
    vmem = pl.BlockSpec(memory_space=pltpu.VMEM)
    out = jax.ShapeDtypeStruct((rows, piece), jnp.bfloat16)
    wide = lambda *shape: pltpu.VMEM(shape, jnp.float32)
    return pl.pallas_call(
        lambda *refs: attention_kernel(count, half, heads, *refs),
        in_specs=[pl.BlockSpec(memory_space=pltpu.SMEM)] + [vmem] * 7,
        out_specs=[vmem] * 4,
        out_shape=[out] * 4,
        scratch_shapes=[
            pltpu.VMEM((rows, piece), jnp.bfloat16),
            wide(rows, piece),
            wide(rows, piece),
            wide(heads, half, rows),
            wide(heads, half, HD),
            wide(heads, half, HD),
            wide(heads, half, LANES),
            wide(heads, half, LANES),
        ],
        compiler_params=pltpu.CompilerParams(vmem_limit_bytes=VMEM),
        cost_estimate=pl.CostEstimate(
            flops=6 * rows * rows * piece, bytes_accessed=rows * piece * 20, transcendentals=rows * rows * heads // 2
        ),
        name="attention",
    )(which, query, keys, values, grad, *rope_tables(positions))


def total(value, plane):
    z, zs = lax.axis_index("dp"), lax.axis_size("dp")
    rows = value.shape[0]
    side = rows // plane.cores
    block = side // plane.size
    part = block // zs
    cut = lambda x, at, size: lax.dynamic_slice_in_dim(x, at * size, size, 0)
    value = cut(value, plane.m, side) + plane.swap(cut(value, 1 - plane.m, side))
    value = plane.scatter([cut(value, plane.h ^ plane.place(j), block) for j in range(plane.size)])
    ring = lambda x, k: lax.ppermute(x, "dp", [(i, (i + k) % zs) for i in range(zs)])
    mine = cut(value, z, part)
    for k in range(1, zs):
        mine = mine + ring(cut(value, (z + k) % zs, part), k)
    out = lax.dynamic_update_slice_in_dim(jnp.zeros((block,) + value.shape[1:], value.dtype), mine, z * part, 0)
    for k in range(1, zs):
        out = lax.dynamic_update_slice_in_dim(out, ring(mine, k), (z + zs - k) % zs * part, 0)
    out = plane.ordered(plane.gather(out))
    return plane.both(out, plane.swap(out), 0).reshape((rows,) + value.shape[1:])


def place_wide(entries, h, out_type, pieces, turned):
    count = len(entries)
    depth, cols = entries[0].shape
    size = cols // pieces

    def kernel(which, *refs):
        a = pl.program_id(0)
        for r in range(count):

            @pl.when((which[0] ^ a) == r)
            def _(r=r):
                for i in range(pieces):
                    block = refs[r][:, i * size : (i + 1) * size].astype(jnp.float32)
                    refs[count + i][...] = block.T if turned[i] else block

    return pl.pallas_call(
        kernel,
        grid=(count,),
        in_specs=[pl.BlockSpec(memory_space=pltpu.SMEM)] + [pl.BlockSpec((depth, cols), lambda a: (0, 0))] * count,
        out_specs=[
            pl.BlockSpec((size, depth), lambda a: (a, 0)) if t else pl.BlockSpec((depth, size), lambda a: (0, a))
            for t in turned
        ],
        out_shape=[
            jax.ShapeDtypeStruct((count * size, depth) if t else (depth, count * size), out_type) for t in turned
        ],
        compiler_params=pltpu.CompilerParams(vmem_limit_bytes=VMEM),
        name="place_wide",
    )(h, *entries)


def after(value, *others):
    return lax.optimization_barrier((value,) + others)[0]


def shards(
    history,
    mixer_in,
    mixer_out,
    mixer_bias,
    norm_gain,
    query_weight,
    key_weight,
    value_weight,
    out_weight,
    up_weight,
    down_weight,
    target,
    loss_count,
    domain,
    domain_scale,
):
    plane = Plane()
    count, cores, h, m = plane.size, plane.cores, plane.h, plane.m
    layers, group_rows, width = history.shape
    rows = target.shape[0]
    half = rows // cores
    depth = query_weight.shape[0]
    assert layers == 1 and cores == 2 and domain.shape[0] == 1 and group_rows == count * rows
    hidden_units = mixer_in.shape[1]
    bf16, f32 = jnp.bfloat16, jnp.float32

    near = count * half
    which_m = m.astype(jnp.int32).reshape(1)
    which_h = h.astype(jnp.int32).reshape(1)

    z, zs = lax.axis_index("dp"), lax.axis_size("dp")
    part = plane.ordered([x[None] for x in plane.gather(norm_gain)])
    gain = lax.dynamic_update_slice_in_dim(jnp.zeros((zs,) + part.shape, bf16), part[None], z, 0)
    for k in range(1, zs):
        came = lax.ppermute(part, "dp", [(i, (i + k) % zs) for i in range(zs)])
        gain = lax.dynamic_update_slice_in_dim(gain, came[None], (z + zs - k) % zs, 0)
    gain = gain.reshape(zs * count, STREAMS, -1).transpose(1, 0, 2).reshape(STREAMS, width).astype(f32)

    parted = history.reshape(count, cores, half, width)
    own_rows = [lax.dynamic_index_in_dim(parted[a], m, 0, keepdims=False) for a in range(count)]
    up_parts = plane.trade(up_weight)
    up_full = lax.all_gather(plane.stacked(up_parts), "dp", axis=0, tiled=True)
    slots, waited = [], up_parts[-1]
    marks = []
    for a in range(count):
        found = plane.gather(after(own_rows[a], waited))
        marks.append(found[1])
        slots.append(found)
    down_parts = plane.trade(after(down_weight, marks[0]).T)
    down_full = lax.all_gather(plane.stacked(down_parts), "dp", axis=0, tiled=True)
    packed = jnp.stack(
        [query_weight, key_weight, value_weight, after(out_weight, marks[min(1, count - 1)]).T], 0
    )
    packed = packed.reshape(4, depth, count, -1).transpose(1, 2, 0, 3).reshape(depth, -1)
    narrow_full = lax.all_gather(plane.stacked(plane.trade(packed)), "dp", axis=0, tiled=True)
    piece = narrow_full.shape[1] // 4
    query_full, key_full, value_full, out_full = (
        narrow_full[:, i * piece : (i + 1) * piece] for i in range(4)
    )

    layer_of = [h ^ plane.place(j) for j in range(count)]
    pick = sum(jnp.where(layer_of[j] == count - 1, j, 0) for j in range(count)).astype(jnp.int32).reshape(1)

    def to_slots(values):
        return jnp.stack(
            [sum(jnp.where(layer_of[j] == l, values[..., l], 0) for l in range(count)) for j in range(count)], -1
        )

    def from_slots(values):
        return jnp.stack(
            [sum(jnp.where(layer_of[j] == l, values[..., j], 0) for j in range(count)) for l in range(count)], -1
        )

    pairs = STREAMS * count
    in_wide = jnp.pad(mixer_in, ((0, 0), (0, LANES - hidden_units)))
    out_wide = jnp.pad(
        to_slots(mixer_out).reshape(hidden_units, pairs), ((0, LANES - hidden_units), (0, LANES - pairs))
    )
    bias_wide = jnp.pad(to_slots(mixer_bias).reshape(1, pairs), ((0, 0), (0, LANES - pairs)))

    normed, mixes, pres, stats, others = [], [], [], [], []
    for a in range(count):
        *one, mix, pre, stat = forward_streams(slots[a], pick, in_wide, out_wide, bias_wide, gain)
        normed.append(one)
        mixes.append(mix)
        pres.append(pre)
        stats.append(stat)
        others.append([plane.swap(x) for x in one])
    streams = [jnp.concatenate([x[c] for x in normed + others], 0) for c in range(STREAMS)]
    block = jnp.arange(count)[:, None] * rows + jnp.arange(half)[None, :]
    positions = jnp.concatenate([(block + m * half).reshape(-1), (block + (1 - m) * half).reshape(-1)])

    domain_one = jnp.sum(jnp.where(jnp.arange(domain_scale.shape[0]) == domain[0], domain_scale, 0.0))
    own_target = lax.dynamic_slice_in_dim(target, m * half, half, 0)
    own_scale = lax.dynamic_slice_in_dim(loss_count, m * half, half, 0).astype(f32) * domain_one
    branch_own = (own_target.astype(f32) * own_scale[:, None]).astype(bf16)
    branch_near = plane.ordered(plane.gather(after(branch_own, marks[-1])))
    branch_grad = jnp.concatenate([branch_near, plane.swap(branch_near)], 0)

    hidden_pre = dot(streams[3], up_full, (1, 0))
    hidden = gelu_exact(hidden_pre).astype(bf16)
    act_grad = dot(branch_grad, down_full, (1, 0))
    pre_grad = (act_grad * gelu_slope(hidden_pre)).astype(bf16)
    down_part = dot(branch_grad, hidden, (0, 0)).astype(bf16)
    up_part = dot(streams[3], pre_grad, (0, 0)).astype(bf16)

    streams[0], streams[1], streams[2] = lax.optimization_barrier(
        (streams[0], streams[1], streams[2], up_part, down_part)
    )[:3]
    query = dot(streams[0], query_full, (1, 0))
    keys = dot(streams[1], key_full, (1, 0))
    values = dot(streams[2], value_full, (1, 0)).astype(bf16)
    attended_grad = dot(branch_grad, out_full, (1, 0)).astype(bf16)
    attended, query_back, key_back, value_back = attention(
        query, keys, values, attended_grad, positions, which_m, count
    )

    branch_far = (
        dot(attended[near:], out_full, (1, 1)) + dot(hidden[near:], down_full, (1, 1))
    ).astype(bf16)
    query_back, key_back, value_back, branch_far = lax.optimization_barrier(
        (query_back, key_back, value_back, branch_far)
    )
    branch = dot(attended[:near], out_full, (1, 1)) + dot(hidden[:near], down_full, (1, 1))
    branch_sum = (branch + plane.swap(branch_far).astype(f32)).astype(bf16)
    branch_rows = plane.scatter(
        [lax.dynamic_slice_in_dim(branch_sum, layer_of[j] * half, half, 0) for j in range(count)]
    ).astype(f32)
    own_mix = lax.dynamic_index_in_dim(jnp.stack(mixes, 0), h, 0, keepdims=False)[:, :pairs]
    own_mix = own_mix.reshape(half, STREAMS, count)
    own_layers = [lax.dynamic_index_in_dim(jnp.stack([s[j] for s in slots], 0), h, 0, keepdims=False) for j in range(count)]
    residual = sum(own_mix[:, STREAMS - 1, j, None] * own_layers[j].astype(f32) for j in range(count))
    output_own = (residual + branch_rows).astype(bf16)
    output = plane.both(output_own, plane.swap(output_own), 0).reshape(rows, width)
    mix_own = from_slots(own_mix)
    mix_rows = plane.both(mix_own, plane.swap(mix_own), 0).reshape(rows, STREAMS, count)

    tails = [
        (query_back, query_full),
        (key_back, key_full),
        (value_back, value_full),
        (pre_grad, up_full),
    ]
    theirs = [plane.swap(dot(x[near:], w, (1, 1)).astype(bf16)) for x, w in tails]
    mine = [dot(x[:near], w, (1, 1)).astype(bf16) for x, w in tails]

    narrow_part = jnp.concatenate(
        [
            dot(streams[0], query_back, (0, 0)),
            dot(streams[1], key_back, (0, 0)),
            dot(streams[2], value_back, (0, 0)),
            dot(branch_grad, attended, (0, 0)),
        ],
        1,
    ).astype(bf16)

    def spread(part, turned):
        summed = lax.psum_scatter(part, "dp", scatter_dimension=0, tiled=True)
        return place_wide(plane.trade_rows(summed), which_h, f32, len(turned), turned)

    (up_grad,) = spread(up_part, (False,))
    (down_grad,) = spread(down_part, (True,))
    query_grad, key_grad, value_grad, out_grad = spread(narrow_part, (False, False, False, True))

    scale_wide = after(jnp.broadcast_to(own_scale[:, None], (half, LANES)), narrow_part, branch_sum)
    sums = None
    history_grad = jnp.zeros((group_rows, width), bf16)
    for a in range(count):
        scale = jnp.where(h == a, scale_wide, 0.0)
        found = backward_streams(
            slots[a], mine, theirs, a, normed[a], mixes[a], pres[a], stats[a], own_target, scale, pick, in_wide, out_wide, gain
        )
        held, rest = list(found[:count]), found[count:]
        sums = rest if sums is None else tuple(x + y for x, y in zip(sums, rest))
        final = plane.scatter(held)
        history_grad = lax.dynamic_update_slice_in_dim(history_grad, final, a * rows + m * half, 0)
        history_grad = lax.dynamic_update_slice_in_dim(history_grad, plane.swap(final), a * rows + (1 - m) * half, 0)
    history_grad = history_grad.reshape(history.shape)

    gain_sum, in_sum, out_sum, bias_sum = sums
    out_sum = from_slots(out_sum[:, :pairs].reshape(LANES, STREAMS, count)).reshape(LANES, pairs)
    bias_sum = from_slots(bias_sum[:, :pairs].reshape(1, STREAMS, count)).reshape(1, pairs)
    small = jnp.concatenate(
        [in_sum, gain_sum.T, jnp.pad(jnp.concatenate([out_sum, bias_sum], 0), ((0, width - LANES - 1), (0, 0)))], 1
    )
    small = total(small, plane)
    mixer_in_grad = small[:, :hidden_units]
    gain_all = small[:, LANES : LANES + STREAMS].T
    place = (lax.axis_index("dp") * count + h) * norm_gain.shape[1]
    norm_gain_grad = lax.dynamic_slice_in_dim(gain_all, place, norm_gain.shape[1], 1)
    tail = small[:, LANES + STREAMS :]
    mixer_out_grad = tail[:hidden_units].reshape(hidden_units, STREAMS, count)
    mixer_bias_grad = tail[LANES].reshape(STREAMS, count)
    return (
        output,
        mix_rows,
        history_grad,
        mixer_in_grad,
        mixer_out_grad,
        mixer_bias_grad,
        norm_gain_grad,
        query_grad,
        key_grad,
        value_grad,
        out_grad,
        up_grad,
        down_grad,
    )


def solution(mesh):
    in_specs = (
        P("hist", "dp", None),
        P(),
        P(),
        P(),
        P(None, ("dp", "hist")),
        P(("dp", "hist"), "mp"),
        P(("dp", "hist"), "mp"),
        P(("dp", "hist"), "mp"),
        P("mp", ("dp", "hist")),
        P(("dp", "hist"), "mp"),
        P("mp", ("dp", "hist")),
        P(("dp", "hist"), None),
        P(("dp", "hist")),
        P("dp"),
        P(),
    )
    out_specs = (
        P(("dp", "hist"), None),
        P(("dp", "hist"), None, None),
        P("hist", "dp", None),
        P(),
        P(),
        P(),
        P(None, ("dp", "hist")),
        P(("dp", "hist"), "mp"),
        P(("dp", "hist"), "mp"),
        P(("dp", "hist"), "mp"),
        P("mp", ("dp", "hist")),
        P(("dp", "hist"), "mp"),
        P("mp", ("dp", "hist")),
    )
    return jax.shard_map(shards, mesh=mesh, in_specs=in_specs, out_specs=out_specs, check_vma=False)
```

```python
import jax
import jax.numpy as jnp
from jax import lax
from jax.experimental import pallas as pl
from jax.experimental.pallas import tpu as pltpu
from jax.sharding import PartitionSpec as P

HD = 128
ROT = 32
STREAMS = 4
LANES = 128
GROUP = 16
UNROLL = 1

HIGHEST = lax.Precision.HIGHEST
EPS_NORM = 1e-05
EPS_RMS = 1e-06
ROPE_BASE = 10000.0
VMEM = 56 * 2**20
PLANE = ("hist", "mp")


def dot(left, right, contract):
    return lax.dot_general(
        left, right, (((contract[0],), (contract[1],)), ((), ())), preferred_element_type=jnp.float32
    )


def gelu_exact(value):
    return 0.5 * value * (1.0 + lax.erf(value * 0.7071067811865476))


def gelu_slope(value):
    return (
        0.5 * (1.0 + lax.erf(value * 0.7071067811865476))
        + value * jnp.exp(-0.5 * value * value) * 0.3989422804014327
    )


class Plane:
    def __init__(self):
        self.size = lax.axis_size("hist")
        self.cores = lax.axis_size("mp")
        self.bits = self.size.bit_length() - 1
        assert self.size == 1 << self.bits
        self.h = lax.axis_index("hist")
        self.m = lax.axis_index("mp")

    def turned(self, j):
        return sum(((j >> b) & 1) << (self.bits - 1 - b) for b in range(self.bits))

    def place(self, j):
        return jnp.where(self.m % 2 == 0, j, self.turned(j))

    def step(self, value, i):
        pairs = []
        for h in range(self.size):
            for m in range(self.cores):
                bit = 1 << (i if m % 2 == 0 else self.bits - 1 - i)
                pairs.append((h * self.cores + m, (h ^ bit) * self.cores + m))
        return lax.ppermute(value, PLANE, pairs)

    def gather(self, value):
        slots = [value]
        for i in range(self.bits):
            slots = slots + [self.step(s, i) for s in slots]
        return slots

    def scatter(self, held):
        for i in reversed(range(self.bits)):
            got = [self.step(x, i) for x in held[1 << i :]]
            held = [
                (x.astype(jnp.float32) + y.astype(jnp.float32)).astype(x.dtype)
                for x, y in zip(held[: 1 << i], got)
            ]
        return held[0]

    def scatter_packed(self, low, high):
        for i in reversed(range(self.bits)):
            got = self.step(high, i)
            if i == 0:
                return low, got
            total = (low.astype(jnp.float32) + got.astype(jnp.float32)).astype(low.dtype)
            side = total.shape[0] // 2
            low, high = total[:side], total[side:]

    def direct(self, value, j):
        pairs = []
        for h in range(self.size):
            for m in range(self.cores):
                place = j if m % 2 == 0 else self.turned(j)
                pairs.append((h * self.cores + m, (h ^ place) * self.cores + m))
        return lax.ppermute(value, PLANE, pairs)

    def ordered(self, slots):
        rows = slots[0].shape[0]
        out = jnp.zeros((self.size * rows,) + slots[0].shape[1:], slots[0].dtype)
        for j, slot in enumerate(slots):
            out = lax.dynamic_update_slice_in_dim(out, slot, (self.h ^ self.place(j)) * rows, 0)
        return out

    def trade(self, wide):
        cols = wide.shape[1] // self.size
        block = lambda r: lax.dynamic_slice_in_dim(wide, (self.h ^ r) * cols, cols, 1)
        return [block(0)] + [
            lax.ppermute(block(r), "hist", [(h, h ^ r) for h in range(self.size)]) for r in range(1, self.size)
        ]

    def trade_rows(self, tall):
        rows = tall.shape[0] // self.size
        block = lambda r: lax.dynamic_slice_in_dim(tall, (self.h ^ r) * rows, rows, 0)
        return [block(0)] + [
            lax.ppermute(block(r), "hist", [(h, h ^ r) for h in range(self.size)]) for r in range(1, self.size)
        ]

    def stacked(self, entries):
        rows = entries[0].shape[0]
        out = jnp.zeros((self.size * rows,) + entries[0].shape[1:], entries[0].dtype)
        for r, entry in enumerate(entries):
            out = lax.dynamic_update_slice_in_dim(out, entry, (self.h ^ r) * rows, 0)
        return out

    def swap(self, value):
        return lax.ppermute(value, "mp", [(m, m ^ 1) for m in range(self.cores)])

    def both(self, own, sibling, axis):
        first = self.m % 2 == 0
        return jnp.stack([jnp.where(first, own, sibling), jnp.where(first, sibling, own)], axis)


def forward_kernel(count, pick, *refs):
    slots = refs[:count]
    in_ref, out_ref, bias_ref, gain_ref = refs[count : count + 4]
    normed = refs[count + 4 : count + 4 + STREAMS]
    mix_ref, pre_ref, stat_ref, last_ref = refs[count + 4 + STREAMS :]
    for j in range(count):

        @pl.when(pick[0] == j)
        def _(j=j):
            last_ref[...] = slots[j][...]

    tile = last_ref.shape[0]
    last = last_ref[...].astype(jnp.float32)
    inverse = lax.rsqrt(jnp.mean(last * last, -1, keepdims=True) + EPS_RMS)
    unit = (last * inverse).astype(jnp.bfloat16)
    pre = jnp.dot(unit, in_ref[...], preferred_element_type=jnp.float32)
    pre_ref[...] = pre
    hidden = gelu_exact(pre).astype(jnp.bfloat16)
    mix_ref[...] = (
        jnp.dot(hidden, out_ref[...], preferred_element_type=jnp.float32) + bias_ref[...]
    )
    lane = lax.broadcasted_iota(jnp.int32, (GROUP, LANES), 1)

    def group(g, carry):
        rows = pl.ds(pl.multiple_of(g * GROUP, GROUP), GROUP)
        mix = mix_ref[rows, :]
        parts = [s[rows, :].astype(jnp.float32) for s in slots]
        stat = jnp.zeros((GROUP, LANES), jnp.float32)
        for c in range(STREAMS):
            stream = mix[:, c * count : c * count + 1] * parts[0]
            for j in range(1, count):
                stream = stream + mix[:, c * count + j : c * count + j + 1] * parts[j]
            centered = stream - jnp.mean(stream, -1, keepdims=True)
            scale = lax.rsqrt(jnp.mean(centered * centered, -1, keepdims=True) + EPS_NORM)
            normed[c][rows, :] = (centered * scale * gain_ref[c : c + 1, :]).astype(jnp.bfloat16)
            stat = jnp.where(lane == c, scale, stat)
        stat_ref[rows, :] = stat
        return carry

    lax.fori_loop(0, tile // GROUP, group, 0, unroll=UNROLL)


def forward_streams(slots, at, blocks, before, pick, mixer_in, mixer_out, bias, gain):
    count = len(slots)
    rows, width = slots[0].shape
    tile = min(128, rows)
    steps = rows // tile
    whole = lambda shape: pl.BlockSpec(shape, lambda i: (0,) * len(shape))
    by_row = lambda cols: pl.BlockSpec((tile, cols), lambda i: (i, 0))
    shifted = lambda cols: pl.BlockSpec((tile, cols), lambda i: (at * steps + i, 0))
    given = 1 + count + 4
    return pl.pallas_call(
        lambda *refs: forward_kernel(count, *refs[:given], *refs[given + len(before) :]),
        grid=(steps,),
        in_specs=[pl.BlockSpec(memory_space=pltpu.SMEM)]
        + [by_row(width)] * count
        + [whole(mixer_in.shape), whole(mixer_out.shape), whole(bias.shape), whole(gain.shape)]
        + [pl.BlockSpec(memory_space=pl.ANY)] * len(before),
        out_specs=[shifted(width)] * STREAMS + [shifted(LANES)] * 3,
        out_shape=[jax.ShapeDtypeStruct((blocks * rows, width), jnp.bfloat16)] * STREAMS
        + [jax.ShapeDtypeStruct((blocks * rows, LANES), jnp.float32)] * 3,
        input_output_aliases={given + i: i for i in range(len(before))},
        scratch_shapes=[pltpu.VMEM((tile, width), jnp.bfloat16)],
        compiler_params=pltpu.CompilerParams(vmem_limit_bytes=VMEM),
        cost_estimate=pl.CostEstimate(
            flops=rows * width * 80, bytes_accessed=rows * width * 2 * (count + STREAMS), transcendentals=0
        ),
        name="forward_streams",
    )(pick, *slots, mixer_in, mixer_out, bias, gain, *before)


def split_dot(left, right, contract):
    high = right.astype(jnp.bfloat16)
    low = (right - high.astype(jnp.float32)).astype(jnp.bfloat16)
    return dot(left, high, contract) + dot(left, low, contract)


def backward_kernel(count, half, pick, order, *refs):
    slots, refs = refs[:count], refs[count:]
    mine, refs = refs[:STREAMS], refs[STREAMS:]
    theirs, refs = refs[:STREAMS], refs[STREAMS:]
    normed, refs = refs[:STREAMS], refs[STREAMS:]
    mix_ref, pre_ref, stat_ref, target_ref, scale_ref, refs = *refs[:5], refs[5:]
    in_ref, out_ref, gain_ref, inverse_gain_ref, refs = *refs[:4], refs[4:]
    grads_ref, refs = refs[0], refs[1:]
    gain_grad_ref, in_grad_ref, out_grad_ref, bias_grad_ref, last_ref, dmix_ref, gain_sum = refs
    tile = last_ref.shape[0]

    @pl.when(pl.program_id(0) == 0)
    def _():
        gain_sum[...] = jnp.zeros_like(gain_sum)
        in_grad_ref[...] = jnp.zeros_like(in_grad_ref)
        out_grad_ref[...] = jnp.zeros_like(out_grad_ref)
        bias_grad_ref[...] = jnp.zeros_like(bias_grad_ref)

    for j in range(count):

        @pl.when(pick[0] == j)
        def _(j=j):
            last_ref[...] = slots[j][...]

    lane = lax.broadcasted_iota(jnp.int32, (GROUP, LANES), 1)

    def placed(j, start, size):
        return pl.ds(pl.multiple_of(order[j] * half + pl.program_id(0) * tile + start, GROUP), size)

    def group(g, carry):
        rows = pl.ds(pl.multiple_of(g * GROUP, GROUP), GROUP)
        mix = mix_ref[rows, :]
        stat = stat_ref[rows, :]
        dmix = jnp.zeros((GROUP, LANES), jnp.float32)
        grad = []
        for c in range(STREAMS):
            total = mine[c][rows, :].astype(jnp.float32) + theirs[c][rows, :].astype(jnp.float32)
            unit = normed[c][rows, :].astype(jnp.float32) * inverse_gain_ref[c : c + 1, :]
            product = total * unit
            gain_sum[c] += product[:8] + product[8:]
            scaled = total * gain_ref[c : c + 1, :]
            mean = jnp.mean(scaled, -1, keepdims=True)
            along = jnp.mean(product * gain_ref[c : c + 1, :], -1, keepdims=True)
            one = stat[:, c : c + 1] * (scaled - mean - unit * along)
            if c == STREAMS - 1:
                one = one + target_ref[rows, :].astype(jnp.float32) * scale_ref[rows, :1]
            grad.append(one)
        for j in range(count):
            part = slots[j][rows, :].astype(jnp.float32)
            total = mix[:, j : j + 1] * grad[0]
            for c in range(1, STREAMS):
                total = total + mix[:, c * count + j : c * count + j + 1] * grad[c]
            grads_ref[placed(j, g * GROUP, GROUP), :] = total.astype(jnp.bfloat16)
            for c in range(STREAMS):
                value = jnp.sum(grad[c] * part, -1, keepdims=True)
                dmix = jnp.where(lane == c * count + j, value, dmix)
        dmix_ref[rows, :] = dmix
        return carry

    lax.fori_loop(0, tile // GROUP, group, 0, unroll=UNROLL)
    dmix = dmix_ref[...]
    last = last_ref[...].astype(jnp.float32)
    inverse = lax.rsqrt(jnp.mean(last * last, -1, keepdims=True) + EPS_RMS)
    unit = (last * inverse).astype(jnp.bfloat16)
    pre = pre_ref[...]
    hidden = gelu_exact(pre).astype(jnp.bfloat16)
    hidden_grad = lax.dot_general(
        dmix,
        out_ref[...].astype(jnp.float32),
        (((1,), (1,)), ((), ())),
        precision=HIGHEST,
        preferred_element_type=jnp.float32,
    )
    pre_grad = hidden_grad * gelu_slope(pre)
    in_grad_ref[...] += split_dot(unit, pre_grad, (0, 0))
    out_grad_ref[...] += split_dot(hidden, dmix, (0, 0))
    bias_grad_ref[...] += jnp.sum(dmix, 0, keepdims=True)
    high = pre_grad.astype(jnp.bfloat16)
    low = (pre_grad - high.astype(jnp.float32)).astype(jnp.bfloat16)
    unit_grad = dot(high, in_ref[...], (1, 1)) + dot(low, in_ref[...], (1, 1))
    cube = inverse * inverse * inverse * jnp.mean(unit_grad * last, -1, keepdims=True)
    extra = inverse * unit_grad - last * cube
    for j in range(count):

        @pl.when(pick[0] == j)
        def _(j=j):
            place = placed(j, 0, tile)
            grads_ref[place, :] = (grads_ref[place, :].astype(jnp.float32) + extra).astype(jnp.bfloat16)

    @pl.when(pl.program_id(0) == pl.num_programs(0) - 1)
    def _():
        gain_grad_ref[...] = jnp.sum(gain_sum[...], 1)


def backward_streams(slots, start, half, mine, theirs, at, normed, mix, pre, stat, target, scale, pick, order, mixer_in, mixer_out, gain):
    count = len(slots)
    rows, width = half, slots[0].shape[1]
    tile = min(128, rows)
    steps = rows // tile
    whole = lambda shape: pl.BlockSpec(shape, lambda i: (0,) * len(shape))
    by_row = lambda cols: pl.BlockSpec((tile, cols), lambda i: (i, 0))
    shifted = lambda cols: pl.BlockSpec((tile, cols), lambda i: (at * steps + i, 0))
    within = pl.BlockSpec((tile, width), lambda i: (start // tile + i, 0))
    hidden = mixer_in.shape[1]
    return pl.pallas_call(
        lambda *refs: backward_kernel(count, half, *refs),
        grid=(steps,),
        in_specs=[pl.BlockSpec(memory_space=pltpu.SMEM)] * 2
        + [within] * count
        + [pl.BlockSpec((tile, width), lambda i, c=c: (at * steps + i, c)) for _, c in mine + theirs]
        + [shifted(width)] * STREAMS
        + [shifted(LANES)] * 3
        + [by_row(width), by_row(LANES)]
        + [whole(mixer_in.shape), whole(mixer_out.shape), whole(gain.shape), whole(gain.shape)],
        out_specs=[whole((count * half, width))]
        + [whole((STREAMS, width)), whole((width, hidden)), whole((hidden, LANES)), whole((1, LANES))],
        out_shape=[jax.ShapeDtypeStruct((count * half, width), jnp.bfloat16)]
        + [
            jax.ShapeDtypeStruct((STREAMS, width), jnp.float32),
            jax.ShapeDtypeStruct((width, hidden), jnp.float32),
            jax.ShapeDtypeStruct((hidden, LANES), jnp.float32),
            jax.ShapeDtypeStruct((1, LANES), jnp.float32),
        ],
        scratch_shapes=[
            pltpu.VMEM((tile, width), jnp.bfloat16),
            pltpu.VMEM((tile, LANES), jnp.float32),
            pltpu.VMEM((STREAMS, 8, width), jnp.float32),
        ],
        compiler_params=pltpu.CompilerParams(vmem_limit_bytes=VMEM),
        cost_estimate=pl.CostEstimate(
            flops=rows * width * 160,
            bytes_accessed=rows * width * 2 * (2 * count + 3 * STREAMS),
            transcendentals=0,
        ),
        name="backward_streams",
    )(pick, order, *slots, *(x for x, _ in mine + theirs), *normed, mix, pre, stat, target, scale, mixer_in, mixer_out, gain, 1.0 / gain)


def rope_tables(positions):
    side = ROT // 2
    freq = ROPE_BASE ** (-2.0 * jnp.arange(side, dtype=jnp.float32) / ROT)
    angle = positions.astype(jnp.float32)[:, None] * freq[None, :]
    cosine, sine = jnp.cos(angle), jnp.sin(angle)
    rest = HD - ROT
    return (
        jnp.pad(jnp.concatenate([cosine, cosine], 1), ((0, 0), (0, rest)), constant_values=1.0),
        jnp.pad(-sine, ((0, 0), (0, HD - side))),
        jnp.pad(sine, ((0, 0), (side, rest))),
    )


def turn(value, cosine, right, left, sign):
    side = ROT // 2
    moved = pltpu.roll(value, HD - side, 1) * right + pltpu.roll(value, side, 1) * left
    return value * cosine + moved * sign


def attention_kernel(count, half, heads, which, *refs):
    near, far, (cos_ref, right_ref, left_ref) = refs[:4], refs[4:8], refs[8:11]
    o_ref, dq_ref, dk_ref, dv_ref, all_ref = refs[11:16]
    q_s, k_s, v_s, g_s, dk_s, dv_s, p_s, o_s, dq_s, top_s, sum_s = refs[16:]
    piece = heads * HD
    blocks = 2 * count
    scale = HD ** (-0.5)
    bf16, f32 = jnp.bfloat16, jnp.float32
    m = which[0]

    def at(b):
        return pl.ds(pl.multiple_of(((lax.rem(b, 2) ^ m) * count + lax.div(b, 2)) * half, half), half)

    def by_owner(a, side):
        return pl.ds(pl.multiple_of((2 * a + side) * half, half), half)

    def cols(n):
        return slice(n * HD, (n + 1) * HD)

    for side, (q_ref, k_ref, v_ref, g_ref) in enumerate((near, far)):

        def prepare(a, carry, side=side, q_ref=q_ref, k_ref=k_ref, v_ref=v_ref, g_ref=g_ref):
            rows = pl.ds(pl.multiple_of(a * half, half), half)
            here = pl.ds(pl.multiple_of((side * count + a) * half, half), half)
            for n in range(heads):
                for given, kept in ((q_ref, q_s), (k_ref, k_s)):
                    kept[here, cols(n)] = turn(
                        given[rows, cols(n)], cos_ref[here, :], right_ref[here, :], left_ref[here, :], 1.0
                    ).astype(bf16)
            v_s[here, :] = v_ref[rows, :]
            g_s[here, :] = g_ref[rows, :]
            dk_s[here, :] = jnp.zeros((half, heads * HD), f32)
            dv_s[here, :] = jnp.zeros((half, heads * HD), f32)
            return carry

        lax.fori_loop(0, count, prepare, 0)
    later = lax.broadcasted_iota(jnp.int32, (half, half), 1) > lax.broadcasted_iota(jnp.int32, (half, half), 0)

    def lanes(value, op):
        parts = [value[:, i : i + LANES] for i in range(0, value.shape[1], LANES)]
        out = parts[0]
        for part in parts[1:]:
            out = op(out, part)
        return out

    def query_block(i, carry):
        here = at(i)
        queries = [q_s[here, cols(n)] for n in range(heads)]
        grads = [g_s[here, cols(n)] for n in range(heads)]

        def scores(j, last):
            there = at(j)
            for n in range(heads):
                s = dot(queries[n], k_s[there, cols(n)], (1, 1)) * scale
                if last:
                    s = jnp.where(later, -1e30, s)
                p_s[n, :, pl.ds(pl.multiple_of(j * half, half), half)] = s
                top = lanes(s, jnp.maximum)
                top_s[n] = jnp.maximum(top_s[n], top)

        top_s[...] = jnp.full(top_s.shape, -1e30, f32)
        lax.fori_loop(0, i, lambda j, c: (scores(j, False), c)[1], 0)
        scores(i, True)
        tops = [jnp.max(top_s[n], -1, keepdims=True) for n in range(heads)]
        o_s[...] = jnp.zeros(o_s.shape, f32)
        dq_s[...] = jnp.zeros(dq_s.shape, f32)
        sum_s[...] = jnp.zeros(sum_s.shape, f32)

        def mixing(j, c):
            there = at(j)
            spot = pl.ds(pl.multiple_of(j * half, half), half)
            for n in range(heads):
                p = jnp.exp(p_s[n, :, spot] - tops[n])
                p_s[n, :, spot] = p
                sum_s[n] += lanes(p, jnp.add)
                o_s[n] += dot(p.astype(bf16), v_s[there, cols(n)], (1, 0))
            return c

        lax.fori_loop(0, i + 1, mixing, 0)
        shares, deltas = [], []
        for n in range(heads):
            share = 1.0 / jnp.sum(sum_s[n], -1, keepdims=True)
            found = o_s[n] * share
            o_ref[here, cols(n)] = found.astype(bf16)
            shares.append(share)
            deltas.append(jnp.sum(found * grads[n].astype(f32), -1, keepdims=True))

        def back(j, c):
            there = at(j)
            spot = pl.ds(pl.multiple_of(j * half, half), half)
            for n in range(heads):
                p = p_s[n, :, spot] * shares[n]
                dp = dot(grads[n], v_s[there, cols(n)], (1, 1))
                ds = (p * (dp - deltas[n])).astype(bf16)
                dq_s[n] += dot(ds, k_s[there, cols(n)], (1, 0))
                dk_s[there, cols(n)] += dot(ds, queries[n], (0, 0))
                dv_s[there, cols(n)] += dot(p.astype(bf16), grads[n], (0, 0))
            return c

        lax.fori_loop(0, i + 1, back, 0)
        place = by_owner(lax.div(i, 2), lax.rem(i, 2) ^ m)
        for n in range(heads):
            found = turn(dq_s[n] * scale, cos_ref[here, :], right_ref[here, :], left_ref[here, :], -1.0).astype(bf16)
            dq_ref[here, cols(n)] = found
            all_ref[place, cols(n)] = found
        return carry

    lax.fori_loop(0, blocks, query_block, 0)

    def finish(b, carry):
        rows = pl.ds(pl.multiple_of(b * half, half), half)
        place = by_owner(lax.rem(b, count), lax.div(b, count))
        for n in range(heads):
            found = turn(
                dk_s[rows, cols(n)] * scale, cos_ref[rows, :], right_ref[rows, :], left_ref[rows, :], -1.0
            ).astype(bf16)
            dk_ref[rows, cols(n)] = found
            all_ref[place, cols(heads + n)] = found
        found = dv_s[rows, :].astype(bf16)
        dv_ref[rows, :] = found
        all_ref[place, 2 * piece : 3 * piece] = found
        return carry

    lax.fori_loop(0, blocks, finish, 0)


def attention(near, far, positions, which, count):
    rows, piece = 2 * near[0].shape[0], near[0].shape[1]
    heads, half = piece // HD, rows // (2 * count)
    vmem = pl.BlockSpec(memory_space=pltpu.VMEM)
    out = jax.ShapeDtypeStruct((rows, piece), jnp.bfloat16)
    wide = lambda *shape: pltpu.VMEM(shape, jnp.float32)
    return pl.pallas_call(
        lambda *refs: attention_kernel(count, half, heads, *refs),
        in_specs=[pl.BlockSpec(memory_space=pltpu.SMEM)] + [vmem] * 11,
        out_specs=[vmem] * 5,
        out_shape=[out] * 4 + [jax.ShapeDtypeStruct((rows, 3 * piece), jnp.bfloat16)],
        scratch_shapes=[pltpu.VMEM((rows, piece), jnp.bfloat16)] * 4
        + [
            wide(rows, piece),
            wide(rows, piece),
            wide(heads, half, rows),
            wide(heads, half, HD),
            wide(heads, half, HD),
            wide(heads, half, LANES),
            wide(heads, half, LANES),
        ],
        compiler_params=pltpu.CompilerParams(vmem_limit_bytes=VMEM),
        cost_estimate=pl.CostEstimate(
            flops=40 * rows * rows * piece, bytes_accessed=rows * piece * 20, transcendentals=rows * rows * heads // 2
        ),
        name="attention",
    )(which, *near, *far, *rope_tables(positions))


def project(streams, weights, types):
    rows, width = streams[0].shape
    count = len(streams)
    piece = weights.shape[1] // count
    tile = min(256, rows)

    def kernel(*refs):
        for c in range(count):
            found = dot(refs[c][...], refs[count][:, c * piece : (c + 1) * piece], (1, 0))
            refs[count + 1 + c][...] = found.astype(types[c])

    return pl.pallas_call(
        kernel,
        grid=(rows // tile,),
        in_specs=[pl.BlockSpec((tile, width), lambda i: (i, 0))] * count
        + [pl.BlockSpec(weights.shape, lambda i: (0, 0))],
        out_specs=[pl.BlockSpec((tile, piece), lambda i: (i, 0))] * count,
        out_shape=[jax.ShapeDtypeStruct((rows, piece), t) for t in types],
        compiler_params=pltpu.CompilerParams(vmem_limit_bytes=VMEM),
        cost_estimate=pl.CostEstimate(
            flops=2 * rows * width * piece * count, bytes_accessed=2 * rows * width * count, transcendentals=0
        ),
        name="project",
    )(*streams, weights)


def project_back(entries, weights):
    count = len(entries)
    rows, piece = entries[0].shape[0], entries[0].shape[1] // 3
    width = weights[0].shape[0]
    side = rows // 2

    def kernel(*refs):
        found = dot(refs[0][...], refs[count][...], (1, 1))
        for j in range(1, count):
            found = found + dot(refs[j][...], refs[count + j][...], (1, 1))
        refs[2 * count][...] = found[:side].astype(jnp.bfloat16)
        refs[2 * count + 1][...] = found[side:].astype(jnp.bfloat16)

    return pl.pallas_call(
        kernel,
        grid=(3, 2),
        in_specs=[pl.BlockSpec((rows, piece), lambda c, i: (0, c))] * count
        + [pl.BlockSpec((width // 2, piece), lambda c, i: (i, c))] * count,
        out_specs=[pl.BlockSpec((side, width // 2), lambda c, i: (0, 2 * c + i))] * 2,
        out_shape=[jax.ShapeDtypeStruct((side, 3 * width), jnp.bfloat16)] * 2,
        compiler_params=pltpu.CompilerParams(vmem_limit_bytes=VMEM),
        name="project_back",
    )(*entries, *weights)


def add_in_slots(near, far, order, count):
    rows, width = near.shape
    block = rows // count
    tile = min(128, block)
    steps = block // tile
    side = count // 2

    def kernel(order, a, b, c, d, low, high):
        low[...] = (a[...].astype(jnp.float32) + b[...].astype(jnp.float32)).astype(jnp.bfloat16)
        high[...] = (c[...].astype(jnp.float32) + d[...].astype(jnp.float32)).astype(jnp.bfloat16)

    def spec(shift):
        return pl.BlockSpec((tile, width), lambda j, i, order: (order[shift + j] * steps + i, 0))

    out = pl.BlockSpec((tile, width), lambda j, i, order: (j * steps + i, 0))
    return pl.pallas_call(
        kernel,
        grid_spec=pltpu.PrefetchScalarGridSpec(
            num_scalar_prefetch=1,
            grid=(side, steps),
            in_specs=[spec(0), spec(0), spec(side), spec(side)],
            out_specs=[out, out],
        ),
        out_shape=[jax.ShapeDtypeStruct((rows // 2, width), jnp.bfloat16)] * 2,
        compiler_params=pltpu.CompilerParams(vmem_limit_bytes=VMEM),
        name="add_in_slots",
    )(order, near, far, near, far)


def outer(groups):
    pieces = len(groups[0][0])
    rows = min(a.shape[0] for a, _ in groups[0][0])
    width = groups[0][0][0][0].shape[1]
    tile = min(256, width)
    sizes = [right[0][0].shape[1] for _, right in groups]
    specs, arrays = [], []
    for left, right in groups:
        for a, k in left:
            specs.append(pl.BlockSpec((rows, tile), lambda i, k=k: (k, i)))
            arrays.append(a)
        for b, k in right:
            specs.append(pl.BlockSpec((rows, b.shape[1]), lambda i, k=k: (k, 0)))
            arrays.append(b)

    def kernel(*refs):
        out, at = refs[-1], 0
        for g, size in enumerate(sizes):
            mine = refs[2 * pieces * g : 2 * pieces * (g + 1)]
            found = dot(mine[0][...], mine[pieces][...], (0, 0))
            for p in range(1, pieces):
                found = found + dot(mine[p][...], mine[pieces + p][...], (0, 0))
            out[:, at : at + size] = found.astype(jnp.bfloat16)
            at += size

    total_rows = rows * pieces
    return pl.pallas_call(
        kernel,
        grid=(width // tile,),
        in_specs=specs,
        out_specs=pl.BlockSpec((tile, sum(sizes)), lambda i: (i, 0)),
        out_shape=jax.ShapeDtypeStruct((width, sum(sizes)), jnp.bfloat16),
        compiler_params=pltpu.CompilerParams(vmem_limit_bytes=VMEM),
        cost_estimate=pl.CostEstimate(
            flops=2 * total_rows * width * sum(sizes),
            bytes_accessed=2 * total_rows * (width * len(groups) + sum(sizes)) + 2 * width * sum(sizes),
            transcendentals=0,
        ),
        name="outer",
    )(*arrays)


def total_over_dp(value, plane):
    z, zs = lax.axis_index("dp"), lax.axis_size("dp")
    rows = value.shape[0]
    side = rows // plane.cores
    cut = lambda x, at, size: lax.dynamic_slice_in_dim(x, at * size, size, 0)
    put = lambda out, x, at: lax.dynamic_update_slice_in_dim(out, x, at * x.shape[0], 0)
    value = cut(value, plane.m, side) + plane.swap(cut(value, 1 - plane.m, side))
    over_dp = lambda x, k: lax.ppermute(x, "dp", [(i, (i + k) % zs) for i in range(zs)])
    part = side // zs
    mine = cut(value, z, part)
    for k in range(1, zs):
        mine = mine + over_dp(cut(value, (z + k) % zs, part), k)
    out = put(jnp.zeros_like(value), mine, z)
    for k in range(1, zs):
        out = put(out, over_dp(mine, k), (z + zs - k) % zs)
    return out


def total_over_plane(out, plane):
    side = out.shape[0]
    cut = lambda x, at, size: lax.dynamic_slice_in_dim(x, at * size, size, 0)
    block = side // plane.size
    mine = cut(out, plane.h, block)
    for j in range(1, plane.size):
        mine = mine + plane.direct(cut(out, plane.h ^ plane.place(j), block), j)
    out = plane.ordered([mine] + [plane.direct(mine, j) for j in range(1, plane.size)])
    return plane.both(out, plane.swap(out), 0).reshape((2 * side,) + out.shape[1:])


def interleave(own, sibling, m, half):
    rows, width = own.shape
    count = rows // half

    def kernel(which, own_ref, sibling_ref, out):
        at = lambda side: pl.ds(pl.multiple_of(side * half, half), half)
        out[at(which[0]), :] = own_ref[...]
        out[at(1 - which[0]), :] = sibling_ref[...]

    block = pl.BlockSpec((half, width), lambda a: (a, 0))
    return pl.pallas_call(
        kernel,
        grid=(count,),
        in_specs=[pl.BlockSpec(memory_space=pltpu.SMEM), block, block],
        out_specs=pl.BlockSpec((2 * half, width), lambda a: (a, 0)),
        out_shape=jax.ShapeDtypeStruct((2 * rows, width), own.dtype),
        compiler_params=pltpu.CompilerParams(vmem_limit_bytes=VMEM),
        name="interleave",
    )(m, own, sibling)


def place_wide(entries, h, out_type, pieces, turned):
    count = len(entries)
    depth, cols = entries[0].shape
    size = cols // pieces

    def kernel(which, *refs):
        a = pl.program_id(0)
        for r in range(count):

            @pl.when((which[0] ^ a) == r)
            def _(r=r):
                for i in range(pieces):
                    block = refs[r][:, i * size : (i + 1) * size].astype(jnp.float32)
                    refs[count + i][...] = block.T if turned[i] else block

    return pl.pallas_call(
        kernel,
        grid=(count,),
        in_specs=[pl.BlockSpec(memory_space=pltpu.SMEM)] + [pl.BlockSpec((depth, cols), lambda a: (0, 0))] * count,
        out_specs=[
            pl.BlockSpec((size, depth), lambda a: (a, 0)) if t else pl.BlockSpec((depth, size), lambda a: (0, a))
            for t in turned
        ],
        out_shape=[
            jax.ShapeDtypeStruct((count * size, depth) if t else (depth, count * size), out_type) for t in turned
        ],
        compiler_params=pltpu.CompilerParams(vmem_limit_bytes=VMEM),
        name="place_wide",
    )(h, *entries)


def after(value, *others):
    return lax.optimization_barrier((value,) + others)[0]


def shards(
    history,
    mixer_in,
    mixer_out,
    mixer_bias,
    norm_gain,
    query_weight,
    key_weight,
    value_weight,
    out_weight,
    up_weight,
    down_weight,
    target,
    loss_count,
    domain,
    domain_scale,
):
    plane = Plane()
    count, cores, h, m = plane.size, plane.cores, plane.h, plane.m
    layers, group_rows, width = history.shape
    rows = target.shape[0]
    half = rows // cores
    depth = query_weight.shape[0]
    assert layers == 1 and cores == 2 and domain.shape[0] == 1 and group_rows == count * rows
    hidden_units = mixer_in.shape[1]
    bf16, f32 = jnp.bfloat16, jnp.float32

    near = count * half
    which_m = m.astype(jnp.int32).reshape(1)
    which_h = h.astype(jnp.int32).reshape(1)

    z, zs = lax.axis_index("dp"), lax.axis_size("dp")
    part = plane.ordered([x[None] for x in plane.gather(norm_gain)])
    gain = lax.dynamic_update_slice_in_dim(jnp.zeros((zs,) + part.shape, bf16), part[None], z, 0)
    for k in range(1, zs):
        came = lax.ppermute(part, "dp", [(i, (i + k) % zs) for i in range(zs)])
        gain = lax.dynamic_update_slice_in_dim(gain, came[None], (z + zs - k) % zs, 0)
    gain = gain.reshape(zs * count, STREAMS, -1).transpose(1, 0, 2).reshape(STREAMS, width).astype(f32)

    parts = 2 if count % 2 == 0 else 1
    per = count // parts
    parted = history.reshape(parts, per, cores, half, width)
    own_rows = [
        lax.dynamic_index_in_dim(parted[g], m, 1, keepdims=False).reshape(per * half, width) for g in range(parts)
    ]
    swap_columns = lambda x: lax.all_to_all(x, "hist", 1, 0, tiled=True)
    slots = [plane.gather(after(own_rows[0], part))]
    up_mine = swap_columns(after(up_weight, part))
    up_full = lax.all_gather(up_mine, "dp", axis=0, tiled=True)
    for g in range(1, parts):
        slots.append(plane.gather(after(own_rows[g], slots[-1][1])))
    down_mine = swap_columns(after(down_weight.T, up_mine, gain, slots[-1][1]))
    down_full = lax.all_gather(down_mine, "dp", axis=0, tiled=True)
    layer_of = [h ^ plane.place(j) for j in range(count)]
    order = jnp.stack(layer_of).astype(jnp.int32)
    pick = sum(jnp.where(layer_of[j] == count - 1, j, 0) for j in range(count)).astype(jnp.int32).reshape(1)

    def to_slots(values):
        return jnp.stack(
            [sum(jnp.where(layer_of[j] == l, values[..., l], 0) for l in range(count)) for j in range(count)], -1
        )

    def from_slots(values):
        return jnp.stack(
            [sum(jnp.where(layer_of[j] == l, values[..., j], 0) for j in range(count)) for l in range(count)], -1
        )

    pairs = STREAMS * count
    in_wide = jnp.pad(mixer_in, ((0, 0), (0, LANES - hidden_units)))
    out_wide = jnp.pad(
        to_slots(mixer_out).reshape(hidden_units, pairs), ((0, LANES - hidden_units), (0, LANES - pairs))
    )
    bias_wide = jnp.pad(to_slots(mixer_bias).reshape(1, pairs), ((0, 0), (0, LANES - pairs)))

    found = []
    for g in range(parts):
        found = forward_streams(slots[g], g, parts, found, pick, in_wide, out_wide, bias_wide, gain)
        if g == 0:
            packed = jnp.stack([query_weight, key_weight, value_weight, out_weight.T], 0)
            packed = packed.reshape(4, depth, count, -1).transpose(1, 2, 0, 3).reshape(depth, -1)
            packed, *found = lax.optimization_barrier((packed, *found))
    narrow_mine = swap_columns(packed)
    narrow_full = lax.all_gather(narrow_mine, "dp", axis=0, tiled=True)
    piece = narrow_full.shape[1] // 4
    out_full = narrow_full[:, 3 * piece :]
    all_weights = plane.gather(narrow_full[:, : 3 * piece])
    near_streams, (mixes, pres, stats) = list(found[:STREAMS]), found[STREAMS:]
    far_streams = [None] * STREAMS
    for c in reversed(range(STREAMS)):
        far_streams[c] = plane.swap(near_streams[c])
    block = jnp.arange(count)[:, None] * rows + jnp.arange(half)[None, :]
    positions = jnp.concatenate([(block + m * half).reshape(-1), (block + (1 - m) * half).reshape(-1)])

    domain_one = jnp.sum(jnp.where(jnp.arange(domain_scale.shape[0]) == domain[0], domain_scale, 0.0))
    own_target = lax.dynamic_slice_in_dim(target, m * half, half, 0)
    own_scale = lax.dynamic_slice_in_dim(loss_count, m * half, half, 0).astype(f32) * domain_one
    branch_own = (own_target.astype(f32) * own_scale[:, None]).astype(bf16)
    near_grad = plane.ordered(plane.gather(after(branch_own, slots[-1][1])))
    far_grad = plane.swap(near_grad)

    def mlp(stream, grad):
        before = dot(stream, up_full, (1, 0))
        back = dot(grad, down_full, (1, 0)) * gelu_slope(before)
        return gelu_exact(before).astype(bf16), back.astype(bf16)

    near_hidden, near_back = mlp(near_streams[3], near_grad)
    far_hidden, far_back = mlp(far_streams[3], far_grad)
    both = lambda near_one, far_one: [(near_one, 0), (far_one, 0)]
    local = lambda one: [(one, 0), (one, 1)]
    grads = both(near_grad, far_grad)
    down_part = outer([(grads, both(near_hidden, far_hidden))])
    down_sum = lax.psum_scatter(down_part, "dp", scatter_dimension=0, tiled=True)
    up_part = outer([(both(near_streams[3], far_streams[3]), both(near_back, far_back))])
    up_sum = lax.psum_scatter(up_part, "dp", scatter_dimension=0, tiled=True)

    near_given, far_given, _, _ = lax.optimization_barrier(
        (near_streams[:3] + [near_grad], far_streams[:3] + [far_grad], up_part, down_part)
    )

    types = (f32, f32, bf16, bf16)
    attended, query_back, key_back, value_back, backs = attention(
        project(near_given, narrow_full, types), project(far_given, narrow_full, types), positions, which_m, count
    )

    def owned(near_one, far_one):
        return plane.scatter_packed(*add_in_slots(near_one, plane.swap(far_one), order, count))

    near_back, far_back, up_part = lax.optimization_barrier((near_back, far_back, up_part))
    far_mlp = dot(far_back, up_full, (1, 1)).astype(bf16)
    near_mlp = dot(near_back, up_full, (1, 1)).astype(bf16)
    owned_mlp = owned(near_mlp, far_mlp)
    backs, attended, _, down_sum, all_weights = lax.optimization_barrier(
        (backs, attended, owned_mlp, down_sum, all_weights)
    )
    own_backs = [lax.dynamic_slice_in_dim(backs, layer_of[j] * rows, rows, 0) for j in range(count)]
    own_backs = own_backs[:1] + [plane.direct(own_backs[j], j) for j in range(1, count)]
    narrow_part = outer(
        [
            (both(near_streams[0], far_streams[0]), local(query_back)),
            (both(near_streams[1], far_streams[1]), local(key_back)),
            (both(near_streams[2], far_streams[2]), local(value_back)),
            (grads, local(attended)),
        ]
    )
    narrow_sum = lax.psum_scatter(narrow_part, "dp", scatter_dimension=0, tiled=True)
    own_backs[0] = after(own_backs[0], narrow_part)
    near_backs, far_backs = project_back(own_backs, all_weights)
    far_backs = plane.swap(far_backs)

    attended = after(attended, near_backs)
    branch_far = (dot(attended[near:], out_full, (1, 1)) + dot(far_hidden, down_full, (1, 1))).astype(bf16)
    branch = (dot(attended[:near], out_full, (1, 1)) + dot(near_hidden, down_full, (1, 1))).astype(bf16)
    branch_low, branch_high = owned(branch, branch_far)
    own_mix = lax.dynamic_slice_in_dim(mixes, h * half, half, 0)[:, :pairs].reshape(half, STREAMS, count)

    def own_block(j):
        found = lax.dynamic_slice_in_dim(slots[0][j], h % per * half, half, 0)
        for g in range(1, parts):
            found = jnp.where(h // per == g, lax.dynamic_slice_in_dim(slots[g][j], h % per * half, half, 0), found)
        return found

    own_layers = [own_block(j) for j in range(count)]
    mix_own = from_slots(own_mix)
    mix_rows = plane.both(mix_own, plane.swap(mix_own), 0).reshape(rows, STREAMS, count)

    def spread(summed, turned):
        return place_wide(plane.trade_rows(summed), which_h, f32, len(turned), turned)

    wide_sum = jnp.concatenate([up_sum, down_sum], 1)

    scale_wide = jnp.broadcast_to(own_scale[:, None], (half, LANES))
    own_part = lambda x: lax.dynamic_slice_in_dim(x, h * half, half, 0)
    found = backward_streams(
        own_layers,
        0,
        half,
        [(near_backs, 0), (near_backs, 1), (near_backs, 2), (owned_mlp[0], 0)],
        [(far_backs, 0), (far_backs, 1), (far_backs, 2), (owned_mlp[1], 0)],
        0,
        [own_part(x) for x in near_streams],
        own_part(mixes),
        own_part(pres),
        own_part(stats),
        own_target,
        scale_wide,
        pick,
        order,
        in_wide,
        out_wide,
        gain,
    )
    layer_grads, sums = found[0], found[1:]
    layer_grads, branch_low, wide_sum = lax.optimization_barrier((layer_grads, branch_low, wide_sum))
    branch_rows = branch_low.astype(f32) + branch_high.astype(f32)
    residual = sum(own_mix[:, STREAMS - 1, j, None] * own_layers[j].astype(f32) for j in range(count))
    output_own = (residual + branch_rows).astype(bf16)
    output = plane.both(output_own, plane.swap(output_own), 0).reshape(rows, width)
    came = lax.all_to_all(layer_grads, "hist", 0, 0, tiled=True)
    gain_sum, in_sum, out_sum, bias_sum = sums
    out_sum = from_slots(out_sum[:, :pairs].reshape(LANES, STREAMS, count)).reshape(LANES, pairs)
    bias_sum = from_slots(bias_sum[:, :pairs].reshape(1, STREAMS, count)).reshape(1, pairs)
    spare = LANES - hidden_units - STREAMS
    spare -= spare % 8
    packed_sum = jnp.concatenate([out_sum, bias_sum], 0).reshape(-1)
    packed_sum = jnp.pad(packed_sum, (0, width * spare - packed_sum.shape[0])).reshape(width, spare)
    small = jnp.concatenate([in_sum[:, :hidden_units], gain_sum.T, packed_sum], 1)
    small = total_over_dp(jnp.pad(small, ((0, 0), (0, LANES - small.shape[1]))), plane)
    came, small, narrow_sum, wide_sum = lax.optimization_barrier((came, small, narrow_sum, wide_sum))
    up_grad, down_grad = spread(wide_sum, (False, True))
    history_grad = interleave(came, plane.swap(came), which_m, half).reshape(history.shape)
    query_grad, key_grad, value_grad, out_grad = spread(narrow_sum, (False, False, False, True))
    small = total_over_plane(small, plane)
    mixer_in_grad = small[:, :hidden_units]
    gain_all = small[:, hidden_units : hidden_units + STREAMS].T
    place = (z * count + h) * norm_gain.shape[1]
    norm_gain_grad = lax.dynamic_slice_in_dim(gain_all, place, norm_gain.shape[1], 1)
    tail = small[:, hidden_units + STREAMS : hidden_units + STREAMS + spare].reshape(-1)[: (LANES + 1) * pairs]
    tail = tail.reshape(LANES + 1, STREAMS, count)
    mixer_out_grad = tail[:hidden_units]
    mixer_bias_grad = tail[LANES]
    return (
        output,
        mix_rows,
        history_grad,
        mixer_in_grad,
        mixer_out_grad,
        mixer_bias_grad,
        norm_gain_grad,
        query_grad,
        key_grad,
        value_grad,
        out_grad,
        up_grad,
        down_grad,
    )


def solution(mesh):
    in_specs = (
        P("hist", "dp", None),
        P(),
        P(),
        P(),
        P(None, ("dp", "hist")),
        P(("dp", "hist"), "mp"),
        P(("dp", "hist"), "mp"),
        P(("dp", "hist"), "mp"),
        P("mp", ("dp", "hist")),
        P(("dp", "hist"), "mp"),
        P("mp", ("dp", "hist")),
        P(("dp", "hist"), None),
        P(("dp", "hist")),
        P("dp"),
        P(),
    )
    out_specs = (
        P(("dp", "hist"), None),
        P(("dp", "hist"), None, None),
        P("hist", "dp", None),
        P(),
        P(),
        P(),
        P(None, ("dp", "hist")),
        P(("dp", "hist"), "mp"),
        P(("dp", "hist"), "mp"),
        P(("dp", "hist"), "mp"),
        P("mp", ("dp", "hist")),
        P(("dp", "hist"), "mp"),
        P("mp", ("dp", "hist")),
    )
    return jax.shard_map(shards, mesh=mesh, in_specs=in_specs, out_specs=out_specs, check_vma=False)
```

```python
import jax
import jax.numpy as jnp
from jax import lax
from jax.experimental import pallas as pl
from jax.experimental.pallas import tpu as pltpu
from jax.sharding import PartitionSpec as P

HD = 128
ROT = 32
STREAMS = 4
LANES = 128
GROUP = 16
UNROLL = 1

HIGHEST = lax.Precision.HIGHEST
EPS_NORM = 1e-05
EPS_RMS = 1e-06
ROPE_BASE = 10000.0
VMEM = 56 * 2**20
PLANE = ("hist", "mp")


def dot(left, right, contract):
    return lax.dot_general(
        left, right, (((contract[0],), (contract[1],)), ((), ())), preferred_element_type=jnp.float32
    )


def gelu_exact(value):
    return 0.5 * value * (1.0 + lax.erf(value * 0.7071067811865476))


def gelu_slope(value):
    return (
        0.5 * (1.0 + lax.erf(value * 0.7071067811865476))
        + value * jnp.exp(-0.5 * value * value) * 0.3989422804014327
    )


class Plane:
    def __init__(self):
        self.size = lax.axis_size("hist")
        self.cores = lax.axis_size("mp")
        self.bits = self.size.bit_length() - 1
        assert self.size == 1 << self.bits
        self.h = lax.axis_index("hist")
        self.m = lax.axis_index("mp")

    def turned(self, j):
        return sum(((j >> b) & 1) << (self.bits - 1 - b) for b in range(self.bits))

    def place(self, j):
        return jnp.where(self.m % 2 == 0, j, self.turned(j))

    def step(self, value, i):
        pairs = []
        for h in range(self.size):
            for m in range(self.cores):
                bit = 1 << (i if m % 2 == 0 else self.bits - 1 - i)
                pairs.append((h * self.cores + m, (h ^ bit) * self.cores + m))
        return lax.ppermute(value, PLANE, pairs)

    def gather(self, value):
        slots = [value]
        for i in range(self.bits):
            slots = slots + [self.step(s, i) for s in slots]
        return slots

    def scatter(self, held):
        for i in reversed(range(self.bits)):
            got = [self.step(x, i) for x in held[1 << i :]]
            held = [
                (x.astype(jnp.float32) + y.astype(jnp.float32)).astype(x.dtype)
                for x, y in zip(held[: 1 << i], got)
            ]
        return held[0]

    def scatter_packed(self, low, high):
        for i in reversed(range(self.bits)):
            got = self.step(high, i)
            if i == 0:
                return low, got
            total = (low.astype(jnp.float32) + got.astype(jnp.float32)).astype(low.dtype)
            side = total.shape[0] // 2
            low, high = total[:side], total[side:]

    def direct(self, value, j):
        pairs = []
        for h in range(self.size):
            for m in range(self.cores):
                place = j if m % 2 == 0 else self.turned(j)
                pairs.append((h * self.cores + m, (h ^ place) * self.cores + m))
        return lax.ppermute(value, PLANE, pairs)

    def ordered(self, slots):
        rows = slots[0].shape[0]
        out = jnp.zeros((self.size * rows,) + slots[0].shape[1:], slots[0].dtype)
        for j, slot in enumerate(slots):
            out = lax.dynamic_update_slice_in_dim(out, slot, (self.h ^ self.place(j)) * rows, 0)
        return out

    def trade(self, wide):
        cols = wide.shape[1] // self.size
        block = lambda r: lax.dynamic_slice_in_dim(wide, (self.h ^ r) * cols, cols, 1)
        return [block(0)] + [
            lax.ppermute(block(r), "hist", [(h, h ^ r) for h in range(self.size)]) for r in range(1, self.size)
        ]

    def trade_rows(self, tall):
        rows = tall.shape[0] // self.size
        block = lambda r: lax.dynamic_slice_in_dim(tall, (self.h ^ r) * rows, rows, 0)
        return [block(0)] + [
            lax.ppermute(block(r), "hist", [(h, h ^ r) for h in range(self.size)]) for r in range(1, self.size)
        ]

    def stacked(self, entries):
        rows = entries[0].shape[0]
        out = jnp.zeros((self.size * rows,) + entries[0].shape[1:], entries[0].dtype)
        for r, entry in enumerate(entries):
            out = lax.dynamic_update_slice_in_dim(out, entry, (self.h ^ r) * rows, 0)
        return out

    def swap(self, value):
        return lax.ppermute(value, "mp", [(m, m ^ 1) for m in range(self.cores)])

    def both(self, own, sibling, axis):
        first = self.m % 2 == 0
        return jnp.stack([jnp.where(first, own, sibling), jnp.where(first, sibling, own)], axis)


def forward_kernel(count, pick, *refs):
    slots = refs[:count]
    in_ref, out_ref, bias_ref, gain_ref = refs[count : count + 4]
    normed = refs[count + 4 : count + 4 + STREAMS]
    mix_ref, pre_ref, stat_ref, last_ref = refs[count + 4 + STREAMS :]
    for j in range(count):

        @pl.when(pick[0] == j)
        def _(j=j):
            last_ref[...] = slots[j][...]

    tile = last_ref.shape[0]
    last = last_ref[...].astype(jnp.float32)
    inverse = lax.rsqrt(jnp.mean(last * last, -1, keepdims=True) + EPS_RMS)
    unit = (last * inverse).astype(jnp.bfloat16)
    pre = jnp.dot(unit, in_ref[...], preferred_element_type=jnp.float32)
    pre_ref[...] = pre
    hidden = gelu_exact(pre).astype(jnp.bfloat16)
    mix_ref[...] = (
        jnp.dot(hidden, out_ref[...], preferred_element_type=jnp.float32) + bias_ref[...]
    )
    lane = lax.broadcasted_iota(jnp.int32, (GROUP, LANES), 1)

    def group(g, carry):
        rows = pl.ds(pl.multiple_of(g * GROUP, GROUP), GROUP)
        mix = mix_ref[rows, :]
        parts = [s[rows, :].astype(jnp.float32) for s in slots]
        stat = jnp.zeros((GROUP, LANES), jnp.float32)
        for c in range(STREAMS):
            stream = mix[:, c * count : c * count + 1] * parts[0]
            for j in range(1, count):
                stream = stream + mix[:, c * count + j : c * count + j + 1] * parts[j]
            centered = stream - jnp.mean(stream, -1, keepdims=True)
            scale = lax.rsqrt(jnp.mean(centered * centered, -1, keepdims=True) + EPS_NORM)
            normed[c][rows, :] = (centered * scale * gain_ref[c : c + 1, :]).astype(jnp.bfloat16)
            stat = jnp.where(lane == c, scale, stat)
        stat_ref[rows, :] = stat
        return carry

    lax.fori_loop(0, tile // GROUP, group, 0, unroll=UNROLL)


def forward_streams(slots, at, blocks, before, pick, mixer_in, mixer_out, bias, gain):
    count = len(slots)
    rows, width = slots[0].shape
    tile = min(128, rows)
    steps = rows // tile
    whole = lambda shape: pl.BlockSpec(shape, lambda i: (0,) * len(shape))
    by_row = lambda cols: pl.BlockSpec((tile, cols), lambda i: (i, 0))
    shifted = lambda cols: pl.BlockSpec((tile, cols), lambda i: (at * steps + i, 0))
    given = 1 + count + 4
    return pl.pallas_call(
        lambda *refs: forward_kernel(count, *refs[:given], *refs[given + len(before) :]),
        grid=(steps,),
        in_specs=[pl.BlockSpec(memory_space=pltpu.SMEM)]
        + [by_row(width)] * count
        + [whole(mixer_in.shape), whole(mixer_out.shape), whole(bias.shape), whole(gain.shape)]
        + [pl.BlockSpec(memory_space=pl.ANY)] * len(before),
        out_specs=[shifted(width)] * STREAMS + [shifted(LANES)] * 3,
        out_shape=[jax.ShapeDtypeStruct((blocks * rows, width), jnp.bfloat16)] * STREAMS
        + [jax.ShapeDtypeStruct((blocks * rows, LANES), jnp.float32)] * 3,
        input_output_aliases={given + i: i for i in range(len(before))},
        scratch_shapes=[pltpu.VMEM((tile, width), jnp.bfloat16)],
        compiler_params=pltpu.CompilerParams(vmem_limit_bytes=VMEM),
        cost_estimate=pl.CostEstimate(
            flops=rows * width * 80, bytes_accessed=rows * width * 2 * (count + STREAMS), transcendentals=0
        ),
        name="forward_streams",
    )(pick, *slots, mixer_in, mixer_out, bias, gain, *before)


def split_dot(left, right, contract):
    high = right.astype(jnp.bfloat16)
    low = (right - high.astype(jnp.float32)).astype(jnp.bfloat16)
    return dot(left, high, contract) + dot(left, low, contract)


def backward_kernel(count, half, pick, order, *refs):
    slots, refs = refs[:count], refs[count:]
    mine, refs = refs[:STREAMS], refs[STREAMS:]
    theirs, refs = refs[:STREAMS], refs[STREAMS:]
    normed, refs = refs[:STREAMS], refs[STREAMS:]
    mix_ref, pre_ref, stat_ref, target_ref, scale_ref, refs = *refs[:5], refs[5:]
    in_ref, out_ref, gain_ref, inverse_gain_ref, refs = *refs[:4], refs[4:]
    grads_ref, refs = refs[0], refs[1:]
    gain_grad_ref, in_grad_ref, out_grad_ref, bias_grad_ref, last_ref, dmix_ref, gain_sum = refs
    tile = last_ref.shape[0]

    @pl.when(pl.program_id(0) == 0)
    def _():
        gain_sum[...] = jnp.zeros_like(gain_sum)
        in_grad_ref[...] = jnp.zeros_like(in_grad_ref)
        out_grad_ref[...] = jnp.zeros_like(out_grad_ref)
        bias_grad_ref[...] = jnp.zeros_like(bias_grad_ref)

    for j in range(count):

        @pl.when(pick[0] == j)
        def _(j=j):
            last_ref[...] = slots[j][...]

    lane = lax.broadcasted_iota(jnp.int32, (GROUP, LANES), 1)

    def placed(j, start, size):
        return pl.ds(pl.multiple_of(order[j] * half + pl.program_id(0) * tile + start, GROUP), size)

    def group(g, carry):
        rows = pl.ds(pl.multiple_of(g * GROUP, GROUP), GROUP)
        mix = mix_ref[rows, :]
        stat = stat_ref[rows, :]
        dmix = jnp.zeros((GROUP, LANES), jnp.float32)
        grad = []
        for c in range(STREAMS):
            total = mine[c][rows, :].astype(jnp.float32) + theirs[c][rows, :].astype(jnp.float32)
            unit = normed[c][rows, :].astype(jnp.float32) * inverse_gain_ref[c : c + 1, :]
            product = total * unit
            gain_sum[c] += product[:8] + product[8:]
            scaled = total * gain_ref[c : c + 1, :]
            mean = jnp.mean(scaled, -1, keepdims=True)
            along = jnp.mean(product * gain_ref[c : c + 1, :], -1, keepdims=True)
            one = stat[:, c : c + 1] * (scaled - mean - unit * along)
            if c == STREAMS - 1:
                one = one + target_ref[rows, :].astype(jnp.float32) * scale_ref[rows, :1]
            grad.append(one)
        for j in range(count):
            part = slots[j][rows, :].astype(jnp.float32)
            total = mix[:, j : j + 1] * grad[0]
            for c in range(1, STREAMS):
                total = total + mix[:, c * count + j : c * count + j + 1] * grad[c]
            grads_ref[placed(j, g * GROUP, GROUP), :] = total.astype(jnp.bfloat16)
            for c in range(STREAMS):
                value = jnp.sum(grad[c] * part, -1, keepdims=True)
                dmix = jnp.where(lane == c * count + j, value, dmix)
        dmix_ref[rows, :] = dmix
        return carry

    lax.fori_loop(0, tile // GROUP, group, 0, unroll=UNROLL)
    dmix = dmix_ref[...]
    last = last_ref[...].astype(jnp.float32)
    inverse = lax.rsqrt(jnp.mean(last * last, -1, keepdims=True) + EPS_RMS)
    unit = (last * inverse).astype(jnp.bfloat16)
    pre = pre_ref[...]
    hidden = gelu_exact(pre).astype(jnp.bfloat16)
    hidden_grad = lax.dot_general(
        dmix,
        out_ref[...].astype(jnp.float32),
        (((1,), (1,)), ((), ())),
        precision=HIGHEST,
        preferred_element_type=jnp.float32,
    )
    pre_grad = hidden_grad * gelu_slope(pre)
    in_grad_ref[...] += split_dot(unit, pre_grad, (0, 0))
    out_grad_ref[...] += split_dot(hidden, dmix, (0, 0))
    bias_grad_ref[...] += jnp.sum(dmix, 0, keepdims=True)
    high = pre_grad.astype(jnp.bfloat16)
    low = (pre_grad - high.astype(jnp.float32)).astype(jnp.bfloat16)
    unit_grad = dot(high, in_ref[...], (1, 1)) + dot(low, in_ref[...], (1, 1))
    cube = inverse * inverse * inverse * jnp.mean(unit_grad * last, -1, keepdims=True)
    extra = inverse * unit_grad - last * cube
    for j in range(count):

        @pl.when(pick[0] == j)
        def _(j=j):
            place = placed(j, 0, tile)
            grads_ref[place, :] = (grads_ref[place, :].astype(jnp.float32) + extra).astype(jnp.bfloat16)

    @pl.when(pl.program_id(0) == pl.num_programs(0) - 1)
    def _():
        gain_grad_ref[...] = jnp.sum(gain_sum[...], 1)


def backward_streams(slots, start, half, mine, theirs, at, normed, mix, pre, stat, target, scale, pick, order, mixer_in, mixer_out, gain):
    count = len(slots)
    rows, width = half, slots[0].shape[1]
    tile = min(128, rows)
    steps = rows // tile
    whole = lambda shape: pl.BlockSpec(shape, lambda i: (0,) * len(shape))
    by_row = lambda cols: pl.BlockSpec((tile, cols), lambda i: (i, 0))
    shifted = lambda cols: pl.BlockSpec((tile, cols), lambda i: (at * steps + i, 0))
    within = pl.BlockSpec((tile, width), lambda i: (start // tile + i, 0))
    hidden = mixer_in.shape[1]
    return pl.pallas_call(
        lambda *refs: backward_kernel(count, half, *refs),
        grid=(steps,),
        in_specs=[pl.BlockSpec(memory_space=pltpu.SMEM)] * 2
        + [within] * count
        + [pl.BlockSpec((tile, width), lambda i, c=c: (at * steps + i, c)) for _, c in mine + theirs]
        + [shifted(width)] * STREAMS
        + [shifted(LANES)] * 3
        + [by_row(width), by_row(LANES)]
        + [whole(mixer_in.shape), whole(mixer_out.shape), whole(gain.shape), whole(gain.shape)],
        out_specs=[whole((count * half, width))]
        + [whole((STREAMS, width)), whole((width, hidden)), whole((hidden, LANES)), whole((1, LANES))],
        out_shape=[jax.ShapeDtypeStruct((count * half, width), jnp.bfloat16)]
        + [
            jax.ShapeDtypeStruct((STREAMS, width), jnp.float32),
            jax.ShapeDtypeStruct((width, hidden), jnp.float32),
            jax.ShapeDtypeStruct((hidden, LANES), jnp.float32),
            jax.ShapeDtypeStruct((1, LANES), jnp.float32),
        ],
        scratch_shapes=[
            pltpu.VMEM((tile, width), jnp.bfloat16),
            pltpu.VMEM((tile, LANES), jnp.float32),
            pltpu.VMEM((STREAMS, 8, width), jnp.float32),
        ],
        compiler_params=pltpu.CompilerParams(vmem_limit_bytes=VMEM),
        cost_estimate=pl.CostEstimate(
            flops=rows * width * 160,
            bytes_accessed=rows * width * 2 * (2 * count + 3 * STREAMS),
            transcendentals=0,
        ),
        name="backward_streams",
    )(pick, order, *slots, *(x for x, _ in mine + theirs), *normed, mix, pre, stat, target, scale, mixer_in, mixer_out, gain, 1.0 / gain)


def rope_tables(positions):
    side = ROT // 2
    freq = ROPE_BASE ** (-2.0 * jnp.arange(side, dtype=jnp.float32) / ROT)
    angle = positions.astype(jnp.float32)[:, None] * freq[None, :]
    cosine, sine = jnp.cos(angle), jnp.sin(angle)
    rest = HD - ROT
    return (
        jnp.pad(jnp.concatenate([cosine, cosine], 1), ((0, 0), (0, rest)), constant_values=1.0),
        jnp.pad(-sine, ((0, 0), (0, HD - side))),
        jnp.pad(sine, ((0, 0), (side, rest))),
    )


def turn(value, cosine, right, left, sign):
    side = ROT // 2
    moved = pltpu.roll(value, HD - side, 1) * right + pltpu.roll(value, side, 1) * left
    return value * cosine + moved * sign


def attention_kernel(count, half, heads, which, *refs):
    near, far, (cos_ref, right_ref, left_ref) = refs[:4], refs[4:8], refs[8:11]
    o_ref, dq_ref, dk_ref, dv_ref, all_ref = refs[11:16]
    q_s, k_s, v_s, g_s, k_t, v_t, g_t, dk_s, dv_s, p_s, o_s, dq_s = refs[16:]
    piece = heads * HD
    block = 2 * half
    scale = HD ** (-0.5)
    bf16, f32 = jnp.bfloat16, jnp.float32
    m = which[0]

    def cols(n):
        return slice(n * HD, (n + 1) * HD)

    def part(b):
        return pl.ds(pl.multiple_of(b * half, half), half)

    def span(j):
        return pl.ds(pl.multiple_of(j * block, block), block)

    def turned(value, here, sign):
        return turn(value, cos_ref[here, :], right_ref[here, :], left_ref[here, :], sign)

    for side, (q_ref, k_ref, v_ref, g_ref) in enumerate((near, far)):

        def prepare(a, carry, side=side, q_ref=q_ref, k_ref=k_ref, v_ref=v_ref, g_ref=g_ref):
            rows, here, there = part(a), part(side * count + a), part(2 * a + (side ^ m))
            for n in range(heads):
                q_s[there, cols(n)] = turned(q_ref[rows, cols(n)], here, 1.0).astype(bf16)
                keys = turned(k_ref[rows, cols(n)], here, 1.0)
                k_s[there, cols(n)] = keys.astype(bf16)
                k_t[cols(n), there] = keys.T.astype(bf16)
                v_t[cols(n), there] = v_ref[rows, cols(n)].astype(f32).T.astype(bf16)
                g_t[cols(n), there] = g_ref[rows, cols(n)].astype(f32).T.astype(bf16)
            v_s[there, :] = v_ref[rows, :]
            g_s[there, :] = g_ref[rows, :]
            dk_s[there, :] = jnp.zeros((half, piece), f32)
            dv_s[there, :] = jnp.zeros((half, piece), f32)
            return carry

        lax.fori_loop(0, count, prepare, 0)
    later = lax.broadcasted_iota(jnp.int32, (block, block), 0) > lax.broadcasted_iota(jnp.int32, (block, block), 1)

    def rows_of_eight(value, op):
        out = value[:8]
        for at in range(8, value.shape[0], 8):
            out = op(out, value[at : at + 8])
        return out

    def query_block(i, carry):
        here = span(i)
        queries = [q_s[here, cols(n)] for n in range(heads)]
        grads = [g_s[here, cols(n)] for n in range(heads)]

        def scores(j, tops, last=False):
            there = span(j)
            out = []
            for n in range(heads):
                s = dot(k_s[there, cols(n)], queries[n], (1, 1)) * (scale * 1.4426950408889634)
                if last:
                    s = jnp.where(later, -1e30, s)
                p_s[n, there, :] = s
                out.append(jnp.maximum(tops[n], rows_of_eight(s, jnp.maximum)))
            return tuple(out)

        tops = lax.fori_loop(0, i, scores, tuple(jnp.full((8, block), -1e30, f32) for _ in range(heads)))
        tops = [jnp.max(x, 0, keepdims=True) for x in scores(i, tops, True)]
        o_s[...] = jnp.zeros(o_s.shape, f32)
        dq_s[...] = jnp.zeros(dq_s.shape, f32)

        def mixing(j, sums):
            there = span(j)
            out = []
            for n in range(heads):
                p = jnp.exp2(p_s[n, there, :] - tops[n])
                p_s[n, there, :] = p
                out.append(sums[n] + rows_of_eight(p, jnp.add))
                o_s[n] += dot(v_t[cols(n), there], p.astype(bf16), (1, 0))
            return tuple(out)

        sums = lax.fori_loop(0, i + 1, mixing, tuple(jnp.zeros((8, block), f32) for _ in range(heads)))
        shares, deltas = [], []
        for n in range(heads):
            share = 1.0 / jnp.sum(sums[n], 0, keepdims=True)
            found = o_s[n] * share
            deltas.append(jnp.sum(found * g_t[cols(n), here].astype(f32), 0, keepdims=True))
            found = found.T.astype(bf16)
            for b in range(2):
                o_ref[part((b ^ m) * count + i), cols(n)] = found[b * half : (b + 1) * half]
            shares.append(share)

        def back(j, c):
            there = span(j)
            for n in range(heads):
                p = p_s[n, there, :] * shares[n]
                dp = dot(v_s[there, cols(n)], grads[n], (1, 1))
                ds = (p * (dp - deltas[n])).astype(bf16)
                dq_s[n] += dot(k_t[cols(n), there], ds, (1, 0))
                dk_s[there, cols(n)] += dot(ds, queries[n], (1, 0))
                dv_s[there, cols(n)] += dot(p.astype(bf16), grads[n], (1, 0))
            return c

        lax.fori_loop(0, i + 1, back, 0)
        for n in range(heads):
            found = dq_s[n].T * scale
            for b in range(2):
                rows = part((b ^ m) * count + i)
                value = turned(found[b * half : (b + 1) * half], rows, -1.0).astype(bf16)
                dq_ref[rows, cols(n)] = value
                all_ref[part(2 * i + (b ^ m)), cols(n)] = value
        return carry

    lax.fori_loop(0, count, query_block, 0)
    for side in range(2):

        def finish(a, carry, side=side):
            here, there, place = part(side * count + a), part(2 * a + (side ^ m)), part(2 * a + side)
            for n in range(heads):
                found = turned(dk_s[there, cols(n)] * scale, here, -1.0).astype(bf16)
                dk_ref[here, cols(n)] = found
                all_ref[place, cols(heads + n)] = found
            found = dv_s[there, :].astype(bf16)
            dv_ref[here, :] = found
            all_ref[place, 2 * piece : 3 * piece] = found
            return carry

        lax.fori_loop(0, count, finish, 0)


def attention(near, far, positions, which, count):
    rows, piece = 2 * near[0].shape[0], near[0].shape[1]
    heads, half = piece // HD, rows // (2 * count)
    vmem = pl.BlockSpec(memory_space=pltpu.VMEM)
    out = jax.ShapeDtypeStruct((rows, piece), jnp.bfloat16)
    wide = lambda *shape: pltpu.VMEM(shape, jnp.float32)
    return pl.pallas_call(
        lambda *refs: attention_kernel(count, half, heads, *refs),
        in_specs=[pl.BlockSpec(memory_space=pltpu.SMEM)] + [vmem] * 11,
        out_specs=[vmem] * 5,
        out_shape=[out] * 4 + [jax.ShapeDtypeStruct((rows, 3 * piece), jnp.bfloat16)],
        scratch_shapes=[pltpu.VMEM((rows, piece), jnp.bfloat16)] * 4
        + [pltpu.VMEM((piece, rows), jnp.bfloat16)] * 3
        + [
            wide(rows, piece),
            wide(rows, piece),
            wide(heads, rows, 2 * half),
            wide(heads, HD, 2 * half),
            wide(heads, HD, 2 * half),
        ],
        compiler_params=pltpu.CompilerParams(vmem_limit_bytes=VMEM),
        cost_estimate=pl.CostEstimate(
            flops=18 * rows * rows * piece, bytes_accessed=rows * piece * 20, transcendentals=rows * rows * heads // 2
        ),
        name="attention",
    )(which, *near, *far, *rope_tables(positions))


def project(streams, weights, types):
    rows, width = streams[0].shape
    count = len(streams)
    piece = weights.shape[1] // count
    tile = min(512, rows)

    def kernel(*refs):
        for c in range(count):
            found = dot(refs[c][...], refs[count][:, c * piece : (c + 1) * piece], (1, 0))
            refs[count + 1 + c][...] = found.astype(types[c])

    return pl.pallas_call(
        kernel,
        grid=(rows // tile,),
        in_specs=[pl.BlockSpec((tile, width), lambda i: (i, 0))] * count
        + [pl.BlockSpec(weights.shape, lambda i: (0, 0))],
        out_specs=[pl.BlockSpec((tile, piece), lambda i: (i, 0))] * count,
        out_shape=[jax.ShapeDtypeStruct((rows, piece), t) for t in types],
        compiler_params=pltpu.CompilerParams(vmem_limit_bytes=VMEM),
        cost_estimate=pl.CostEstimate(
            flops=2 * rows * width * piece * count, bytes_accessed=2 * rows * width * count, transcendentals=0
        ),
        name="project",
    )(*streams, weights)


def project_back(entries, weights):
    count = len(entries)
    rows, piece = entries[0].shape[0], entries[0].shape[1] // 3
    width = weights[0].shape[0]
    side = rows // 2

    def kernel(*refs):
        found = dot(refs[0][...], refs[count][...], (1, 1))
        for j in range(1, count):
            found = found + dot(refs[j][...], refs[count + j][...], (1, 1))
        refs[2 * count][...] = found[:side].astype(jnp.bfloat16)
        refs[2 * count + 1][...] = found[side:].astype(jnp.bfloat16)

    return pl.pallas_call(
        kernel,
        grid=(3, 2),
        in_specs=[pl.BlockSpec((rows, piece), lambda c, i: (0, c))] * count
        + [pl.BlockSpec((width // 2, piece), lambda c, i: (i, c))] * count,
        out_specs=[pl.BlockSpec((side, width // 2), lambda c, i: (0, 2 * c + i))] * 2,
        out_shape=[jax.ShapeDtypeStruct((side, 3 * width), jnp.bfloat16)] * 2,
        compiler_params=pltpu.CompilerParams(vmem_limit_bytes=VMEM),
        name="project_back",
    )(*entries, *weights)


def add_in_slots(near, far, order, count):
    rows, width = near.shape
    block = rows // count
    tile = min(256, block)
    steps = block // tile
    side = count // 2

    def kernel(order, a, b, c, d, low, high):
        low[...] = (a[...].astype(jnp.float32) + b[...].astype(jnp.float32)).astype(jnp.bfloat16)
        high[...] = (c[...].astype(jnp.float32) + d[...].astype(jnp.float32)).astype(jnp.bfloat16)

    def spec(shift):
        return pl.BlockSpec((tile, width), lambda j, i, order: (order[shift + j] * steps + i, 0))

    out = pl.BlockSpec((tile, width), lambda j, i, order: (j * steps + i, 0))
    return pl.pallas_call(
        kernel,
        grid_spec=pltpu.PrefetchScalarGridSpec(
            num_scalar_prefetch=1,
            grid=(side, steps),
            in_specs=[spec(0), spec(0), spec(side), spec(side)],
            out_specs=[out, out],
        ),
        out_shape=[jax.ShapeDtypeStruct((rows // 2, width), jnp.bfloat16)] * 2,
        compiler_params=pltpu.CompilerParams(vmem_limit_bytes=VMEM),
        name="add_in_slots",
    )(order, near, far, near, far)


def outer(groups):
    pieces = len(groups[0][0])
    rows = min(a.shape[0] for a, _ in groups[0][0])
    width = groups[0][0][0][0].shape[1]
    tile = min(512, width)
    sizes = [right[0][0].shape[1] for _, right in groups]
    specs, arrays = [], []
    for left, right in groups:
        for a, k in left:
            specs.append(pl.BlockSpec((rows, tile), lambda i, k=k: (k, i)))
            arrays.append(a)
        for b, k in right:
            specs.append(pl.BlockSpec((rows, b.shape[1]), lambda i, k=k: (k, 0)))
            arrays.append(b)

    def kernel(*refs):
        out, at = refs[-1], 0
        for g, size in enumerate(sizes):
            mine = refs[2 * pieces * g : 2 * pieces * (g + 1)]
            found = dot(mine[0][...], mine[pieces][...], (0, 0))
            for p in range(1, pieces):
                found = found + dot(mine[p][...], mine[pieces + p][...], (0, 0))
            out[:, at : at + size] = found.astype(jnp.bfloat16)
            at += size

    total_rows = rows * pieces
    return pl.pallas_call(
        kernel,
        grid=(width // tile,),
        in_specs=specs,
        out_specs=pl.BlockSpec((tile, sum(sizes)), lambda i: (i, 0)),
        out_shape=jax.ShapeDtypeStruct((width, sum(sizes)), jnp.bfloat16),
        compiler_params=pltpu.CompilerParams(vmem_limit_bytes=VMEM),
        cost_estimate=pl.CostEstimate(
            flops=2 * total_rows * width * sum(sizes),
            bytes_accessed=2 * total_rows * (width * len(groups) + sum(sizes)) + 2 * width * sum(sizes),
            transcendentals=0,
        ),
        name="outer",
    )(*arrays)


def total_over_dp(value, plane):
    z, zs = lax.axis_index("dp"), lax.axis_size("dp")
    rows = value.shape[0]
    side = rows // plane.cores
    cut = lambda x, at, size: lax.dynamic_slice_in_dim(x, at * size, size, 0)
    put = lambda out, x, at: lax.dynamic_update_slice_in_dim(out, x, at * x.shape[0], 0)
    value = cut(value, plane.m, side) + plane.swap(cut(value, 1 - plane.m, side))
    over_dp = lambda x, k: lax.ppermute(x, "dp", [(i, (i + k) % zs) for i in range(zs)])
    part = side // zs
    mine = cut(value, z, part)
    for k in range(1, zs):
        mine = mine + over_dp(cut(value, (z + k) % zs, part), k)
    out = put(jnp.zeros_like(value), mine, z)
    for k in range(1, zs):
        out = put(out, over_dp(mine, k), (z + zs - k) % zs)
    return out


def total_over_plane(out, plane):
    side = out.shape[0]
    cut = lambda x, at, size: lax.dynamic_slice_in_dim(x, at * size, size, 0)
    block = side // plane.size
    mine = cut(out, plane.h, block)
    for j in range(1, plane.size):
        mine = mine + plane.direct(cut(out, plane.h ^ plane.place(j), block), j)
    out = plane.ordered([mine] + [plane.direct(mine, j) for j in range(1, plane.size)])
    return plane.both(out, plane.swap(out), 0).reshape((2 * side,) + out.shape[1:])


def interleave(own, sibling, m, half):
    rows, width = own.shape
    count = rows // half

    def kernel(which, own_ref, sibling_ref, out):
        at = lambda side: pl.ds(pl.multiple_of(side * half, half), half)
        out[at(which[0]), :] = own_ref[...]
        out[at(1 - which[0]), :] = sibling_ref[...]

    block = pl.BlockSpec((half, width), lambda a: (a, 0))
    return pl.pallas_call(
        kernel,
        grid=(count,),
        in_specs=[pl.BlockSpec(memory_space=pltpu.SMEM), block, block],
        out_specs=pl.BlockSpec((2 * half, width), lambda a: (a, 0)),
        out_shape=jax.ShapeDtypeStruct((2 * rows, width), own.dtype),
        compiler_params=pltpu.CompilerParams(vmem_limit_bytes=VMEM),
        name="interleave",
    )(m, own, sibling)


def place_wide(blocks, count, pieces, turned):
    depth, cols = blocks.shape[0] // count, blocks.shape[1]
    size = cols // pieces

    def kernel(*refs):
        for i in range(pieces):
            block = refs[0][:, i * size : (i + 1) * size].astype(jnp.float32)
            refs[1 + i][...] = block.T if turned[i] else block

    return pl.pallas_call(
        kernel,
        grid=(count,),
        in_specs=[pl.BlockSpec((depth, cols), lambda a: (a, 0))],
        out_specs=[
            pl.BlockSpec((size, depth), lambda a: (a, 0)) if t else pl.BlockSpec((depth, size), lambda a: (0, a))
            for t in turned
        ],
        out_shape=[
            jax.ShapeDtypeStruct((count * size, depth) if t else (depth, count * size), jnp.float32) for t in turned
        ],
        compiler_params=pltpu.CompilerParams(vmem_limit_bytes=VMEM),
        name="place_wide",
    )(blocks)


def after(value, *others):
    return lax.optimization_barrier((value,) + others)[0]


def shards(
    history,
    mixer_in,
    mixer_out,
    mixer_bias,
    norm_gain,
    query_weight,
    key_weight,
    value_weight,
    out_weight,
    up_weight,
    down_weight,
    target,
    loss_count,
    domain,
    domain_scale,
):
    plane = Plane()
    count, cores, h, m = plane.size, plane.cores, plane.h, plane.m
    layers, group_rows, width = history.shape
    rows = target.shape[0]
    half = rows // cores
    depth = query_weight.shape[0]
    assert layers == 1 and cores == 2 and domain.shape[0] == 1 and group_rows == count * rows
    hidden_units = mixer_in.shape[1]
    bf16, f32 = jnp.bfloat16, jnp.float32

    near = count * half
    which_m = m.astype(jnp.int32).reshape(1)
    which_h = h.astype(jnp.int32).reshape(1)

    z, zs = lax.axis_index("dp"), lax.axis_size("dp")
    part = plane.ordered([x[None] for x in plane.gather(norm_gain)])
    gain = lax.dynamic_update_slice_in_dim(jnp.zeros((zs,) + part.shape, bf16), part[None], z, 0)
    for k in range(1, zs):
        came = lax.ppermute(part, "dp", [(i, (i + k) % zs) for i in range(zs)])
        gain = lax.dynamic_update_slice_in_dim(gain, came[None], (z + zs - k) % zs, 0)
    gain = gain.reshape(zs * count, STREAMS, -1).transpose(1, 0, 2).reshape(STREAMS, width).astype(f32)

    parts = 2 if count % 2 == 0 else 1
    per = count // parts
    parted = history.reshape(parts, per, cores, half, width)
    own_rows = [
        lax.dynamic_index_in_dim(parted[g], m, 1, keepdims=False).reshape(per * half, width) for g in range(parts)
    ]
    swap_columns = lambda x: lax.all_to_all(x, "hist", 1, 0, tiled=True)
    slots = [plane.gather(after(own_rows[0], part))]
    up_mine = swap_columns(after(up_weight, part))
    up_full = lax.all_gather(up_mine, "dp", axis=0, tiled=True)
    for g in range(1, parts):
        slots.append(plane.gather(after(own_rows[g], slots[-1][1])))
    packed = jnp.stack([query_weight, key_weight, value_weight, out_weight.T], 0)
    packed = packed.reshape(4, depth, count, -1).transpose(1, 2, 0, 3).reshape(depth, -1)
    narrow_mine = swap_columns(after(packed, up_mine, gain, slots[-1][1]))
    narrow_full = lax.all_gather(narrow_mine, "dp", axis=0, tiled=True)
    piece = narrow_full.shape[1] // 4
    out_full = narrow_full[:, 3 * piece :]

    layer_of = [h ^ plane.place(j) for j in range(count)]
    order = jnp.stack(layer_of).astype(jnp.int32)
    pick = sum(jnp.where(layer_of[j] == count - 1, j, 0) for j in range(count)).astype(jnp.int32).reshape(1)

    def to_slots(values):
        return jnp.stack(
            [sum(jnp.where(layer_of[j] == l, values[..., l], 0) for l in range(count)) for j in range(count)], -1
        )

    def from_slots(values):
        return jnp.stack(
            [sum(jnp.where(layer_of[j] == l, values[..., j], 0) for j in range(count)) for l in range(count)], -1
        )

    pairs = STREAMS * count
    in_wide = jnp.pad(mixer_in, ((0, 0), (0, LANES - hidden_units)))
    out_wide = jnp.pad(
        to_slots(mixer_out).reshape(hidden_units, pairs), ((0, LANES - hidden_units), (0, LANES - pairs))
    )
    bias_wide = jnp.pad(to_slots(mixer_bias).reshape(1, pairs), ((0, 0), (0, LANES - pairs)))

    found = []
    for g in range(parts):
        found = forward_streams(slots[g], g, parts, found, pick, in_wide, out_wide, bias_wide, gain)
        if g == 0:
            down_turned, *found = lax.optimization_barrier((down_weight.T, *found))
    down_mine = swap_columns(down_turned)
    down_full = lax.all_gather(down_mine, "dp", axis=0, tiled=True)
    all_weights = plane.gather(narrow_full[:, : 3 * piece])
    near_streams, (mixes, pres, stats) = list(found[:STREAMS]), found[STREAMS:]
    far_streams = [None] * STREAMS
    for c in reversed(range(STREAMS)):
        far_streams[c] = plane.swap(near_streams[c])
    block = jnp.arange(count)[:, None] * rows + jnp.arange(half)[None, :]
    positions = jnp.concatenate([(block + m * half).reshape(-1), (block + (1 - m) * half).reshape(-1)])

    domain_one = jnp.sum(jnp.where(jnp.arange(domain_scale.shape[0]) == domain[0], domain_scale, 0.0))
    own_target = lax.dynamic_slice_in_dim(target, m * half, half, 0)
    own_scale = lax.dynamic_slice_in_dim(loss_count, m * half, half, 0).astype(f32) * domain_one
    branch_own = (own_target.astype(f32) * own_scale[:, None]).astype(bf16)
    near_grad = plane.ordered(plane.gather(after(branch_own, slots[-1][1])))
    far_grad = plane.swap(near_grad)

    def mlp(stream, grad):
        before = dot(stream, up_full, (1, 0))
        back = dot(grad, down_full, (1, 0)) * gelu_slope(before)
        return gelu_exact(before).astype(bf16), back.astype(bf16)

    near_hidden, near_back = mlp(near_streams[3], near_grad)
    far_hidden, far_back = mlp(far_streams[3], far_grad)
    both = lambda near_one, far_one: [(near_one, 0), (far_one, 0)]
    local = lambda one: [(one, 0), (one, 1)]
    grads = both(near_grad, far_grad)
    down_part = outer([(grads, both(near_hidden, far_hidden))])
    down_sum = lax.psum_scatter(down_part, "dp", scatter_dimension=0, tiled=True)
    near_back, far_back, all_weights[1], *far_streams = lax.optimization_barrier(
        (near_back, far_back, all_weights[1], *far_streams)
    )
    up_part = outer([(both(near_streams[3], far_streams[3]), both(near_back, far_back))])
    up_sum = lax.psum_scatter(up_part, "dp", scatter_dimension=0, tiled=True)

    own_mix = lax.dynamic_slice_in_dim(mixes, h * half, half, 0)[:, :pairs].reshape(half, STREAMS, count)

    def own_block(j):
        found = lax.dynamic_slice_in_dim(slots[0][j], h % per * half, half, 0)
        for g in range(1, parts):
            found = jnp.where(h // per == g, lax.dynamic_slice_in_dim(slots[g][j], h % per * half, half, 0), found)
        return found

    own_layers = [own_block(j) for j in range(count)]
    own_part = lambda x: lax.dynamic_slice_in_dim(x, h * half, half, 0)
    own_given = [own_part(x) for x in near_streams], own_part(mixes), own_part(pres), own_part(stats)
    near_given, far_given, _, _, own_given, own_layers, all_weights[2] = lax.optimization_barrier(
        (near_streams[:3] + [near_grad], far_streams[:3] + [far_grad], up_part, down_part, own_given, own_layers, all_weights[2])
    )

    types = (f32, f32, bf16, bf16)
    attended, query_back, key_back, value_back, backs = attention(
        project(near_given, narrow_full, types), project(far_given, narrow_full, types), positions, which_m, count
    )

    def owned(near_one, far_one):
        return plane.scatter_packed(*add_in_slots(near_one, plane.swap(far_one), order, count))

    near_back, far_back, up_part = lax.optimization_barrier((near_back, far_back, up_part))
    far_mlp = dot(far_back, up_full, (1, 1)).astype(bf16)
    near_mlp = dot(near_back, up_full, (1, 1)).astype(bf16)
    owned_mlp = owned(near_mlp, far_mlp)
    backs, attended, _, down_sum, all_weights = lax.optimization_barrier(
        (backs, attended, owned_mlp, down_sum, all_weights)
    )
    own_backs = [lax.dynamic_slice_in_dim(backs, layer_of[j] * rows, rows, 0) for j in range(count)]
    own_backs = own_backs[:1] + [plane.direct(own_backs[j], j) for j in range(1, count)]
    narrow_part = outer(
        [
            (both(near_streams[0], far_streams[0]), local(query_back)),
            (both(near_streams[1], far_streams[1]), local(key_back)),
            (both(near_streams[2], far_streams[2]), local(value_back)),
            (grads, local(attended)),
        ]
    )
    narrow_sum = lax.psum_scatter(narrow_part, "dp", scatter_dimension=0, tiled=True)
    own_backs, wide_sum, _ = lax.optimization_barrier((own_backs, jnp.concatenate([up_sum, down_sum], 1), narrow_part))
    near_backs, far_backs = project_back(own_backs, all_weights)
    far_backs = plane.swap(far_backs)

    attended = after(attended, near_backs)
    branch_far = (dot(attended[near:], out_full, (1, 1)) + dot(far_hidden, down_full, (1, 1))).astype(bf16)
    branch = (dot(attended[:near], out_full, (1, 1)) + dot(near_hidden, down_full, (1, 1))).astype(bf16)
    branch_low, branch_high = owned(branch, branch_far)
    mix_own = from_slots(own_mix)
    mix_rows = plane.both(mix_own, plane.swap(mix_own), 0).reshape(rows, STREAMS, count)

    def spread(summed):
        return lax.all_to_all(summed, "hist", 0, 0, tiled=True)

    wide_sum = spread(wide_sum)

    scale_wide = jnp.broadcast_to(own_scale[:, None], (half, LANES))
    found = backward_streams(
        own_layers,
        0,
        half,
        [(near_backs, 0), (near_backs, 1), (near_backs, 2), (owned_mlp[0], 0)],
        [(far_backs, 0), (far_backs, 1), (far_backs, 2), (owned_mlp[1], 0)],
        0,
        *own_given,
        own_target,
        scale_wide,
        pick,
        order,
        in_wide,
        out_wide,
        gain,
    )
    layer_grads, sums = found[0], found[1:]
    layer_grads, branch_low, wide_sum = lax.optimization_barrier((layer_grads, branch_low, wide_sum))
    branch_rows = branch_low.astype(f32) + branch_high.astype(f32)
    residual = sum(own_mix[:, STREAMS - 1, j, None] * own_layers[j].astype(f32) for j in range(count))
    output_own = (residual + branch_rows).astype(bf16)
    output = plane.both(output_own, plane.swap(output_own), 0).reshape(rows, width)
    came = lax.all_to_all(layer_grads, "hist", 0, 0, tiled=True)
    gain_sum, in_sum, out_sum, bias_sum = sums
    out_sum = from_slots(out_sum[:, :pairs].reshape(LANES, STREAMS, count)).reshape(LANES, pairs)
    bias_sum = from_slots(bias_sum[:, :pairs].reshape(1, STREAMS, count)).reshape(1, pairs)
    spare = LANES - hidden_units - STREAMS
    spare -= spare % 8
    packed_sum = jnp.concatenate([out_sum, bias_sum], 0).reshape(-1)
    packed_sum = jnp.pad(packed_sum, (0, width * spare - packed_sum.shape[0])).reshape(width, spare)
    small = jnp.concatenate([in_sum[:, :hidden_units], gain_sum.T, packed_sum], 1)
    small = total_over_dp(jnp.pad(small, ((0, 0), (0, LANES - small.shape[1]))), plane)
    came, small, narrow_sum, wide_sum = lax.optimization_barrier((came, small, narrow_sum, wide_sum))
    up_grad, down_grad = place_wide(wide_sum, count, 2, (False, True))
    history_grad = interleave(came, plane.swap(came), which_m, half).reshape(history.shape)
    query_grad, key_grad, value_grad, out_grad = place_wide(spread(narrow_sum), count, 4, (False, False, False, True))
    small = total_over_plane(small, plane)
    mixer_in_grad = small[:, :hidden_units]
    gain_all = small[:, hidden_units : hidden_units + STREAMS].T
    place = (z * count + h) * norm_gain.shape[1]
    norm_gain_grad = lax.dynamic_slice_in_dim(gain_all, place, norm_gain.shape[1], 1)
    tail = small[:, hidden_units + STREAMS : hidden_units + STREAMS + spare].reshape(-1)[: (LANES + 1) * pairs]
    tail = tail.reshape(LANES + 1, STREAMS, count)
    mixer_out_grad = tail[:hidden_units]
    mixer_bias_grad = tail[LANES]
    return (
        output,
        mix_rows,
        history_grad,
        mixer_in_grad,
        mixer_out_grad,
        mixer_bias_grad,
        norm_gain_grad,
        query_grad,
        key_grad,
        value_grad,
        out_grad,
        up_grad,
        down_grad,
    )


def solution(mesh):
    in_specs = (
        P("hist", "dp", None),
        P(),
        P(),
        P(),
        P(None, ("dp", "hist")),
        P(("dp", "hist"), "mp"),
        P(("dp", "hist"), "mp"),
        P(("dp", "hist"), "mp"),
        P("mp", ("dp", "hist")),
        P(("dp", "hist"), "mp"),
        P("mp", ("dp", "hist")),
        P(("dp", "hist"), None),
        P(("dp", "hist")),
        P("dp"),
        P(),
    )
    out_specs = (
        P(("dp", "hist"), None),
        P(("dp", "hist"), None, None),
        P("hist", "dp", None),
        P(),
        P(),
        P(),
        P(None, ("dp", "hist")),
        P(("dp", "hist"), "mp"),
        P(("dp", "hist"), "mp"),
        P(("dp", "hist"), "mp"),
        P("mp", ("dp", "hist")),
        P(("dp", "hist"), "mp"),
        P("mp", ("dp", "hist")),
    )
    return jax.shard_map(shards, mesh=mesh, in_specs=in_specs, out_specs=out_specs, check_vma=False)
```

```python
import jax
import jax.numpy as jnp
from jax import lax
from jax.experimental import pallas as pl
from jax.experimental.pallas import tpu as pltpu
from jax.sharding import PartitionSpec as P

HD = 128
ROT = 32
STREAMS = 4
LANES = 128
GROUP = 16
UNROLL = 1

HIGHEST = lax.Precision.HIGHEST
EPS_NORM = 1e-05
EPS_RMS = 1e-06
ROPE_BASE = 10000.0
VMEM = 56 * 2**20
PLANE = ("hist", "mp")


def dot(left, right, contract):
    return lax.dot_general(
        left, right, (((contract[0],), (contract[1],)), ((), ())), preferred_element_type=jnp.float32
    )


def gelu_exact(value):
    return 0.5 * value * (1.0 + lax.erf(value * 0.7071067811865476))


def gelu_slope(value):
    return (
        0.5 * (1.0 + lax.erf(value * 0.7071067811865476))
        + value * jnp.exp(-0.5 * value * value) * 0.3989422804014327
    )


class Plane:
    def __init__(self):
        self.size = lax.axis_size("hist")
        self.cores = lax.axis_size("mp")
        self.bits = self.size.bit_length() - 1
        assert self.size == 1 << self.bits
        self.h = lax.axis_index("hist")
        self.m = lax.axis_index("mp")

    def turned(self, j):
        return sum(((j >> b) & 1) << (self.bits - 1 - b) for b in range(self.bits))

    def place(self, j):
        return jnp.where(self.m % 2 == 0, j, self.turned(j))

    def step(self, value, i):
        pairs = []
        for h in range(self.size):
            for m in range(self.cores):
                bit = 1 << (i if m % 2 == 0 else self.bits - 1 - i)
                pairs.append((h * self.cores + m, (h ^ bit) * self.cores + m))
        return lax.ppermute(value, PLANE, pairs)

    def gather(self, value):
        slots = [value]
        for i in range(self.bits):
            slots = slots + [self.step(s, i) for s in slots]
        return slots

    def scatter(self, held):
        for i in reversed(range(self.bits)):
            got = [self.step(x, i) for x in held[1 << i :]]
            held = [
                (x.astype(jnp.float32) + y.astype(jnp.float32)).astype(x.dtype)
                for x, y in zip(held[: 1 << i], got)
            ]
        return held[0]

    def scatter_packed(self, low, high):
        for i in reversed(range(self.bits)):
            got = self.step(high, i)
            if i == 0:
                return low, got
            total = (low.astype(jnp.float32) + got.astype(jnp.float32)).astype(low.dtype)
            side = total.shape[0] // 2
            low, high = total[:side], total[side:]

    def direct(self, value, j):
        pairs = []
        for h in range(self.size):
            for m in range(self.cores):
                place = j if m % 2 == 0 else self.turned(j)
                pairs.append((h * self.cores + m, (h ^ place) * self.cores + m))
        return lax.ppermute(value, PLANE, pairs)

    def ordered(self, slots):
        rows = slots[0].shape[0]
        out = jnp.zeros((self.size * rows,) + slots[0].shape[1:], slots[0].dtype)
        for j, slot in enumerate(slots):
            out = lax.dynamic_update_slice_in_dim(out, slot, (self.h ^ self.place(j)) * rows, 0)
        return out

    def trade(self, wide):
        cols = wide.shape[1] // self.size
        block = lambda r: lax.dynamic_slice_in_dim(wide, (self.h ^ r) * cols, cols, 1)
        return [block(0)] + [
            lax.ppermute(block(r), "hist", [(h, h ^ r) for h in range(self.size)]) for r in range(1, self.size)
        ]

    def trade_rows(self, tall):
        rows = tall.shape[0] // self.size
        block = lambda r: lax.dynamic_slice_in_dim(tall, (self.h ^ r) * rows, rows, 0)
        return [block(0)] + [
            lax.ppermute(block(r), "hist", [(h, h ^ r) for h in range(self.size)]) for r in range(1, self.size)
        ]

    def stacked(self, entries):
        rows = entries[0].shape[0]
        out = jnp.zeros((self.size * rows,) + entries[0].shape[1:], entries[0].dtype)
        for r, entry in enumerate(entries):
            out = lax.dynamic_update_slice_in_dim(out, entry, (self.h ^ r) * rows, 0)
        return out

    def swap(self, value):
        return lax.ppermute(value, "mp", [(m, m ^ 1) for m in range(self.cores)])

    def both(self, own, sibling, axis):
        first = self.m % 2 == 0
        return jnp.stack([jnp.where(first, own, sibling), jnp.where(first, sibling, own)], axis)


def forward_kernel(count, pick, *refs):
    slots = refs[:count]
    in_ref, out_ref, bias_ref, gain_ref = refs[count : count + 4]
    normed = refs[count + 4 : count + 4 + STREAMS]
    mix_ref, pre_ref, stat_ref, last_ref = refs[count + 4 + STREAMS :]
    for j in range(count):

        @pl.when(pick[0] == j)
        def _(j=j):
            last_ref[...] = slots[j][...]

    tile = last_ref.shape[0]
    last = last_ref[...].astype(jnp.float32)
    inverse = lax.rsqrt(jnp.mean(last * last, -1, keepdims=True) + EPS_RMS)
    unit = (last * inverse).astype(jnp.bfloat16)
    pre = jnp.dot(unit, in_ref[...], preferred_element_type=jnp.float32)
    pre_ref[...] = pre
    hidden = gelu_exact(pre).astype(jnp.bfloat16)
    mix_ref[...] = (
        jnp.dot(hidden, out_ref[...], preferred_element_type=jnp.float32) + bias_ref[...]
    )
    lane = lax.broadcasted_iota(jnp.int32, (GROUP, LANES), 1)

    def group(g, carry):
        rows = pl.ds(pl.multiple_of(g * GROUP, GROUP), GROUP)
        mix = mix_ref[rows, :]
        parts = [s[rows, :].astype(jnp.float32) for s in slots]
        stat = jnp.zeros((GROUP, LANES), jnp.float32)
        for c in range(STREAMS):
            stream = mix[:, c * count : c * count + 1] * parts[0]
            for j in range(1, count):
                stream = stream + mix[:, c * count + j : c * count + j + 1] * parts[j]
            centered = stream - jnp.mean(stream, -1, keepdims=True)
            scale = lax.rsqrt(jnp.mean(centered * centered, -1, keepdims=True) + EPS_NORM)
            normed[c][rows, :] = (centered * scale * gain_ref[c : c + 1, :]).astype(jnp.bfloat16)
            stat = jnp.where(lane == c, scale, stat)
        stat_ref[rows, :] = stat
        return carry

    lax.fori_loop(0, tile // GROUP, group, 0, unroll=UNROLL)


def forward_streams(slots, at, blocks, before, pick, mixer_in, mixer_out, bias, gain):
    count = len(slots)
    rows, width = slots[0].shape
    tile = min(128, rows)
    steps = rows // tile
    whole = lambda shape: pl.BlockSpec(shape, lambda i: (0,) * len(shape))
    by_row = lambda cols: pl.BlockSpec((tile, cols), lambda i: (i, 0))
    shifted = lambda cols: pl.BlockSpec((tile, cols), lambda i: (at * steps + i, 0))
    given = 1 + count + 4
    return pl.pallas_call(
        lambda *refs: forward_kernel(count, *refs[:given], *refs[given + len(before) :]),
        grid=(steps,),
        in_specs=[pl.BlockSpec(memory_space=pltpu.SMEM)]
        + [by_row(width)] * count
        + [whole(mixer_in.shape), whole(mixer_out.shape), whole(bias.shape), whole(gain.shape)]
        + [pl.BlockSpec(memory_space=pl.ANY)] * len(before),
        out_specs=[shifted(width)] * STREAMS + [shifted(LANES)] * 3,
        out_shape=[jax.ShapeDtypeStruct((blocks * rows, width), jnp.bfloat16)] * STREAMS
        + [jax.ShapeDtypeStruct((blocks * rows, LANES), jnp.float32)] * 3,
        input_output_aliases={given + i: i for i in range(len(before))},
        scratch_shapes=[pltpu.VMEM((tile, width), jnp.bfloat16)],
        compiler_params=pltpu.CompilerParams(vmem_limit_bytes=VMEM),
        cost_estimate=pl.CostEstimate(
            flops=rows * width * 80, bytes_accessed=rows * width * 2 * (count + STREAMS), transcendentals=0
        ),
        name="forward_streams",
    )(pick, *slots, mixer_in, mixer_out, bias, gain, *before)


def split_dot(left, right, contract):
    high = right.astype(jnp.bfloat16)
    low = (right - high.astype(jnp.float32)).astype(jnp.bfloat16)
    return dot(left, high, contract) + dot(left, low, contract)


def backward_kernel(count, half, pick, order, *refs):
    slots, refs = refs[:count], refs[count:]
    mine, refs = refs[:STREAMS], refs[STREAMS:]
    theirs, refs = refs[:STREAMS], refs[STREAMS:]
    normed, refs = refs[:STREAMS], refs[STREAMS:]
    mix_ref, pre_ref, stat_ref, target_ref, scale_ref, refs = *refs[:5], refs[5:]
    in_ref, out_ref, gain_ref, inverse_gain_ref, refs = *refs[:4], refs[4:]
    grads_ref, refs = refs[0], refs[1:]
    gain_grad_ref, in_grad_ref, out_grad_ref, bias_grad_ref, last_ref, dmix_ref, gain_sum = refs
    tile = last_ref.shape[0]

    @pl.when(pl.program_id(0) == 0)
    def _():
        gain_sum[...] = jnp.zeros_like(gain_sum)
        in_grad_ref[...] = jnp.zeros_like(in_grad_ref)
        out_grad_ref[...] = jnp.zeros_like(out_grad_ref)
        bias_grad_ref[...] = jnp.zeros_like(bias_grad_ref)

    for j in range(count):

        @pl.when(pick[0] == j)
        def _(j=j):
            last_ref[...] = slots[j][...]

    lane = lax.broadcasted_iota(jnp.int32, (GROUP, LANES), 1)

    def placed(j, start, size):
        return pl.ds(pl.multiple_of(order[j] * half + pl.program_id(0) * tile + start, GROUP), size)

    def group(g, carry):
        rows = pl.ds(pl.multiple_of(g * GROUP, GROUP), GROUP)
        mix = mix_ref[rows, :]
        stat = stat_ref[rows, :]
        dmix = jnp.zeros((GROUP, LANES), jnp.float32)
        grad = []
        for c in range(STREAMS):
            total = mine[c][rows, :].astype(jnp.float32) + theirs[c][rows, :].astype(jnp.float32)
            unit = normed[c][rows, :].astype(jnp.float32) * inverse_gain_ref[c : c + 1, :]
            product = total * unit
            gain_sum[c] += product[:8] + product[8:]
            scaled = total * gain_ref[c : c + 1, :]
            mean = jnp.mean(scaled, -1, keepdims=True)
            along = jnp.mean(product * gain_ref[c : c + 1, :], -1, keepdims=True)
            one = stat[:, c : c + 1] * (scaled - mean - unit * along)
            if c == STREAMS - 1:
                one = one + target_ref[rows, :].astype(jnp.float32) * scale_ref[rows, :1]
            grad.append(one)
        for j in range(count):
            part = slots[j][rows, :].astype(jnp.float32)
            total = mix[:, j : j + 1] * grad[0]
            for c in range(1, STREAMS):
                total = total + mix[:, c * count + j : c * count + j + 1] * grad[c]
            grads_ref[placed(j, g * GROUP, GROUP), :] = total.astype(jnp.bfloat16)
            for c in range(STREAMS):
                value = jnp.sum(grad[c] * part, -1, keepdims=True)
                dmix = jnp.where(lane == c * count + j, value, dmix)
        dmix_ref[rows, :] = dmix
        return carry

    lax.fori_loop(0, tile // GROUP, group, 0, unroll=UNROLL)
    dmix = dmix_ref[...]
    last = last_ref[...].astype(jnp.float32)
    inverse = lax.rsqrt(jnp.mean(last * last, -1, keepdims=True) + EPS_RMS)
    unit = (last * inverse).astype(jnp.bfloat16)
    pre = pre_ref[...]
    hidden = gelu_exact(pre).astype(jnp.bfloat16)
    hidden_grad = lax.dot_general(
        dmix,
        out_ref[...].astype(jnp.float32),
        (((1,), (1,)), ((), ())),
        precision=HIGHEST,
        preferred_element_type=jnp.float32,
    )
    pre_grad = hidden_grad * gelu_slope(pre)
    in_grad_ref[...] += split_dot(unit, pre_grad, (0, 0))
    out_grad_ref[...] += split_dot(hidden, dmix, (0, 0))
    bias_grad_ref[...] += jnp.sum(dmix, 0, keepdims=True)
    high = pre_grad.astype(jnp.bfloat16)
    low = (pre_grad - high.astype(jnp.float32)).astype(jnp.bfloat16)
    unit_grad = dot(high, in_ref[...], (1, 1)) + dot(low, in_ref[...], (1, 1))
    cube = inverse * inverse * inverse * jnp.mean(unit_grad * last, -1, keepdims=True)
    extra = inverse * unit_grad - last * cube
    for j in range(count):

        @pl.when(pick[0] == j)
        def _(j=j):
            place = placed(j, 0, tile)
            grads_ref[place, :] = (grads_ref[place, :].astype(jnp.float32) + extra).astype(jnp.bfloat16)

    @pl.when(pl.program_id(0) == pl.num_programs(0) - 1)
    def _():
        gain_grad_ref[...] = jnp.sum(gain_sum[...], 1)


def backward_streams(slots, start, half, mine, theirs, at, normed, mix, pre, stat, target, scale, pick, order, mixer_in, mixer_out, gain):
    count = len(slots)
    rows, width = half, slots[0].shape[1]
    tile = min(128, rows)
    steps = rows // tile
    whole = lambda shape: pl.BlockSpec(shape, lambda i: (0,) * len(shape))
    by_row = lambda cols: pl.BlockSpec((tile, cols), lambda i: (i, 0))
    shifted = lambda cols: pl.BlockSpec((tile, cols), lambda i: (at * steps + i, 0))
    within = pl.BlockSpec((tile, width), lambda i: (start // tile + i, 0))
    hidden = mixer_in.shape[1]
    return pl.pallas_call(
        lambda *refs: backward_kernel(count, half, *refs),
        grid=(steps,),
        in_specs=[pl.BlockSpec(memory_space=pltpu.SMEM)] * 2
        + [within] * count
        + [pl.BlockSpec((tile, width), lambda i, c=c: (at * steps + i, c)) for _, c in mine + theirs]
        + [shifted(width)] * STREAMS
        + [shifted(LANES)] * 3
        + [by_row(width), by_row(LANES)]
        + [whole(mixer_in.shape), whole(mixer_out.shape), whole(gain.shape), whole(gain.shape)],
        out_specs=[whole((count * half, width))]
        + [whole((STREAMS, width)), whole((width, hidden)), whole((hidden, LANES)), whole((1, LANES))],
        out_shape=[jax.ShapeDtypeStruct((count * half, width), jnp.bfloat16)]
        + [
            jax.ShapeDtypeStruct((STREAMS, width), jnp.float32),
            jax.ShapeDtypeStruct((width, hidden), jnp.float32),
            jax.ShapeDtypeStruct((hidden, LANES), jnp.float32),
            jax.ShapeDtypeStruct((1, LANES), jnp.float32),
        ],
        scratch_shapes=[
            pltpu.VMEM((tile, width), jnp.bfloat16),
            pltpu.VMEM((tile, LANES), jnp.float32),
            pltpu.VMEM((STREAMS, 8, width), jnp.float32),
        ],
        compiler_params=pltpu.CompilerParams(vmem_limit_bytes=VMEM),
        cost_estimate=pl.CostEstimate(
            flops=rows * width * 160,
            bytes_accessed=rows * width * 2 * (2 * count + 3 * STREAMS),
            transcendentals=0,
        ),
        name="backward_streams",
    )(pick, order, *slots, *(x for x, _ in mine + theirs), *normed, mix, pre, stat, target, scale, mixer_in, mixer_out, gain, 1.0 / gain)


def rope_tables(positions):
    side = ROT // 2
    freq = ROPE_BASE ** (-2.0 * jnp.arange(side, dtype=jnp.float32) / ROT)
    angle = positions.astype(jnp.float32)[:, None] * freq[None, :]
    cosine, sine = jnp.cos(angle), jnp.sin(angle)
    rest = HD - ROT
    return (
        jnp.pad(jnp.concatenate([cosine, cosine], 1), ((0, 0), (0, rest)), constant_values=1.0),
        jnp.pad(-sine, ((0, 0), (0, HD - side))),
        jnp.pad(sine, ((0, 0), (side, rest))),
    )


def turn(value, cosine, right, left, sign):
    side = ROT // 2
    moved = pltpu.roll(value, HD - side, 1) * right + pltpu.roll(value, side, 1) * left
    return value * cosine + moved * sign


def attention_kernel(count, half, heads, which, *refs):
    near, far, (cos_ref, right_ref, left_ref) = refs[:4], refs[4:8], refs[8:11]
    o_ref, dq_ref, dk_ref, dv_ref, all_ref = refs[11:16]
    q_s, k_s, v_s, g_s, k_t, v_t, g_t, dk_s, dv_s, p_s, o_s, dq_s = refs[16:]
    piece = heads * HD
    block = 2 * half
    scale = HD ** (-0.5)
    bf16, f32 = jnp.bfloat16, jnp.float32
    m = which[0]

    def cols(n):
        return slice(n * HD, (n + 1) * HD)

    def part(b):
        return pl.ds(pl.multiple_of(b * half, half), half)

    def span(j):
        return pl.ds(pl.multiple_of(j * block, block), block)

    def turned(value, here, sign):
        return turn(value, cos_ref[here, :], right_ref[here, :], left_ref[here, :], sign)

    for side, (q_ref, k_ref, v_ref, g_ref) in enumerate((near, far)):

        def prepare(a, carry, side=side, q_ref=q_ref, k_ref=k_ref, v_ref=v_ref, g_ref=g_ref):
            rows, here, there = part(a), part(side * count + a), part(2 * a + (side ^ m))
            for n in range(heads):
                q_s[there, cols(n)] = turned(q_ref[rows, cols(n)], here, 1.0).astype(bf16)
                keys = turned(k_ref[rows, cols(n)], here, 1.0)
                k_s[there, cols(n)] = keys.astype(bf16)
                k_t[cols(n), there] = keys.T.astype(bf16)
                v_t[cols(n), there] = v_ref[rows, cols(n)].astype(f32).T.astype(bf16)
                g_t[cols(n), there] = g_ref[rows, cols(n)].astype(f32).T.astype(bf16)
            v_s[there, :] = v_ref[rows, :]
            g_s[there, :] = g_ref[rows, :]
            dk_s[there, :] = jnp.zeros((half, piece), f32)
            dv_s[there, :] = jnp.zeros((half, piece), f32)
            return carry

        lax.fori_loop(0, count, prepare, 0)
    later = lax.broadcasted_iota(jnp.int32, (block, block), 0) > lax.broadcasted_iota(jnp.int32, (block, block), 1)

    def rows_of_eight(value, op):
        out = value[:8]
        for at in range(8, value.shape[0], 8):
            out = op(out, value[at : at + 8])
        return out

    def query_block(i, carry):
        here = span(i)
        queries = [q_s[here, cols(n)] for n in range(heads)]
        grads = [g_s[here, cols(n)] for n in range(heads)]

        def scores(j, tops, last=False):
            there = span(j)
            out = []
            for n in range(heads):
                s = dot(k_s[there, cols(n)], queries[n], (1, 1)) * (scale * 1.4426950408889634)
                if last:
                    s = jnp.where(later, -1e30, s)
                p_s[n, there, :] = s
                out.append(jnp.maximum(tops[n], rows_of_eight(s, jnp.maximum)))
            return tuple(out)

        tops = lax.fori_loop(0, i, scores, tuple(jnp.full((8, block), -1e30, f32) for _ in range(heads)))
        tops = [jnp.max(x, 0, keepdims=True) for x in scores(i, tops, True)]
        o_s[...] = jnp.zeros(o_s.shape, f32)
        dq_s[...] = jnp.zeros(dq_s.shape, f32)

        def mixing(j, sums):
            there = span(j)
            out = []
            for n in range(heads):
                p = jnp.exp2(p_s[n, there, :] - tops[n])
                p_s[n, there, :] = p
                out.append(sums[n] + rows_of_eight(p, jnp.add))
                o_s[n] += dot(v_t[cols(n), there], p.astype(bf16), (1, 0))
            return tuple(out)

        sums = lax.fori_loop(0, i + 1, mixing, tuple(jnp.zeros((8, block), f32) for _ in range(heads)))
        shares, deltas = [], []
        for n in range(heads):
            share = 1.0 / jnp.sum(sums[n], 0, keepdims=True)
            found = o_s[n] * share
            deltas.append(jnp.sum(found * g_t[cols(n), here].astype(f32), 0, keepdims=True))
            found = found.T.astype(bf16)
            for b in range(2):
                o_ref[part((b ^ m) * count + i), cols(n)] = found[b * half : (b + 1) * half]
            shares.append(share)

        def back(j, c):
            there = span(j)
            for n in range(heads):
                p = p_s[n, there, :] * shares[n]
                dp = dot(v_s[there, cols(n)], grads[n], (1, 1))
                ds = (p * (dp - deltas[n])).astype(bf16)
                dq_s[n] += dot(k_t[cols(n), there], ds, (1, 0))
                dk_s[there, cols(n)] += dot(ds, queries[n], (1, 0))
                dv_s[there, cols(n)] += dot(p.astype(bf16), grads[n], (1, 0))
            return c

        lax.fori_loop(0, i + 1, back, 0)
        for n in range(heads):
            found = dq_s[n].T * scale
            for b in range(2):
                rows = part((b ^ m) * count + i)
                value = turned(found[b * half : (b + 1) * half], rows, -1.0).astype(bf16)
                dq_ref[rows, cols(n)] = value
                all_ref[part(2 * i + (b ^ m)), cols(n)] = value
        return carry

    lax.fori_loop(0, count, query_block, 0)
    for side in range(2):

        def finish(a, carry, side=side):
            here, there, place = part(side * count + a), part(2 * a + (side ^ m)), part(2 * a + side)
            for n in range(heads):
                found = turned(dk_s[there, cols(n)] * scale, here, -1.0).astype(bf16)
                dk_ref[here, cols(n)] = found
                all_ref[place, cols(heads + n)] = found
            found = dv_s[there, :].astype(bf16)
            dv_ref[here, :] = found
            all_ref[place, 2 * piece : 3 * piece] = found
            return carry

        lax.fori_loop(0, count, finish, 0)


def attention(near, far, positions, which, count):
    rows, piece = 2 * near[0].shape[0], near[0].shape[1]
    heads, half = piece // HD, rows // (2 * count)
    vmem = pl.BlockSpec(memory_space=pltpu.VMEM)
    out = jax.ShapeDtypeStruct((rows, piece), jnp.bfloat16)
    wide = lambda *shape: pltpu.VMEM(shape, jnp.float32)
    return pl.pallas_call(
        lambda *refs: attention_kernel(count, half, heads, *refs),
        in_specs=[pl.BlockSpec(memory_space=pltpu.SMEM)] + [vmem] * 11,
        out_specs=[vmem] * 5,
        out_shape=[out] * 4 + [jax.ShapeDtypeStruct((rows, 3 * piece), jnp.bfloat16)],
        scratch_shapes=[pltpu.VMEM((rows, piece), jnp.bfloat16)] * 4
        + [pltpu.VMEM((piece, rows), jnp.bfloat16)] * 3
        + [
            wide(rows, piece),
            wide(rows, piece),
            wide(heads, rows, 2 * half),
            wide(heads, HD, 2 * half),
            wide(heads, HD, 2 * half),
        ],
        compiler_params=pltpu.CompilerParams(vmem_limit_bytes=VMEM),
        cost_estimate=pl.CostEstimate(
            flops=18 * rows * rows * piece, bytes_accessed=rows * piece * 20, transcendentals=rows * rows * heads // 2
        ),
        name="attention",
    )(which, *near, *far, *rope_tables(positions))


def project(streams, weights, types):
    rows, width = streams[0].shape
    count = len(streams)
    piece = weights.shape[1] // count
    tile = min(512, rows)

    def kernel(*refs):
        for c in range(count):
            found = dot(refs[c][...], refs[count][:, c * piece : (c + 1) * piece], (1, 0))
            refs[count + 1 + c][...] = found.astype(types[c])

    return pl.pallas_call(
        kernel,
        grid=(rows // tile,),
        in_specs=[pl.BlockSpec((tile, width), lambda i: (i, 0))] * count
        + [pl.BlockSpec(weights.shape, lambda i: (0, 0))],
        out_specs=[pl.BlockSpec((tile, piece), lambda i: (i, 0))] * count,
        out_shape=[jax.ShapeDtypeStruct((rows, piece), t) for t in types],
        compiler_params=pltpu.CompilerParams(vmem_limit_bytes=VMEM),
        cost_estimate=pl.CostEstimate(
            flops=2 * rows * width * piece * count, bytes_accessed=2 * rows * width * count, transcendentals=0
        ),
        name="project",
    )(*streams, weights)


def project_back(entries, weights):
    count = len(entries)
    rows, piece = entries[0].shape[0], entries[0].shape[1] // 3
    width = weights[0].shape[0]
    side = rows // 2

    def kernel(*refs):
        found = dot(refs[0][...], refs[count][...], (1, 1))
        for j in range(1, count):
            found = found + dot(refs[j][...], refs[count + j][...], (1, 1))
        refs[2 * count][...] = found[:side].astype(jnp.bfloat16)
        refs[2 * count + 1][...] = found[side:].astype(jnp.bfloat16)

    return pl.pallas_call(
        kernel,
        grid=(3, 2),
        in_specs=[pl.BlockSpec((rows, piece), lambda c, i: (0, c))] * count
        + [pl.BlockSpec((width // 2, piece), lambda c, i: (i, c))] * count,
        out_specs=[pl.BlockSpec((side, width // 2), lambda c, i: (0, 2 * c + i))] * 2,
        out_shape=[jax.ShapeDtypeStruct((side, 3 * width), jnp.bfloat16)] * 2,
        compiler_params=pltpu.CompilerParams(vmem_limit_bytes=VMEM),
        name="project_back",
    )(*entries, *weights)


def add_in_slots(near, far, order, count):
    rows, width = near.shape
    block = rows // count
    tile = min(256, block)
    steps = block // tile
    side = count // 2

    def kernel(order, a, b, c, d, low, high):
        low[...] = (a[...].astype(jnp.float32) + b[...].astype(jnp.float32)).astype(jnp.bfloat16)
        high[...] = (c[...].astype(jnp.float32) + d[...].astype(jnp.float32)).astype(jnp.bfloat16)

    def spec(shift):
        return pl.BlockSpec((tile, width), lambda j, i, order: (order[shift + j] * steps + i, 0))

    out = pl.BlockSpec((tile, width), lambda j, i, order: (j * steps + i, 0))
    return pl.pallas_call(
        kernel,
        grid_spec=pltpu.PrefetchScalarGridSpec(
            num_scalar_prefetch=1,
            grid=(side, steps),
            in_specs=[spec(0), spec(0), spec(side), spec(side)],
            out_specs=[out, out],
        ),
        out_shape=[jax.ShapeDtypeStruct((rows // 2, width), jnp.bfloat16)] * 2,
        compiler_params=pltpu.CompilerParams(vmem_limit_bytes=VMEM),
        name="add_in_slots",
    )(order, near, far, near, far)


def outer(groups):
    pieces = len(groups[0][0])
    rows = min(a.shape[0] for a, _ in groups[0][0])
    width = groups[0][0][0][0].shape[1]
    tile = min(512, width)
    sizes = [right[0][0].shape[1] for _, right in groups]
    specs, arrays = [], []
    for left, right in groups:
        for a, k in left:
            specs.append(pl.BlockSpec((rows, tile), lambda i, k=k: (k, i)))
            arrays.append(a)
        for b, k in right:
            specs.append(pl.BlockSpec((rows, b.shape[1]), lambda i, k=k: (k, 0)))
            arrays.append(b)

    def kernel(*refs):
        out, at = refs[-1], 0
        for g, size in enumerate(sizes):
            mine = refs[2 * pieces * g : 2 * pieces * (g + 1)]
            found = dot(mine[0][...], mine[pieces][...], (0, 0))
            for p in range(1, pieces):
                found = found + dot(mine[p][...], mine[pieces + p][...], (0, 0))
            out[:, at : at + size] = found.astype(jnp.bfloat16)
            at += size

    total_rows = rows * pieces
    return pl.pallas_call(
        kernel,
        grid=(width // tile,),
        in_specs=specs,
        out_specs=pl.BlockSpec((tile, sum(sizes)), lambda i: (i, 0)),
        out_shape=jax.ShapeDtypeStruct((width, sum(sizes)), jnp.bfloat16),
        compiler_params=pltpu.CompilerParams(vmem_limit_bytes=VMEM),
        cost_estimate=pl.CostEstimate(
            flops=2 * total_rows * width * sum(sizes),
            bytes_accessed=2 * total_rows * (width * len(groups) + sum(sizes)) + 2 * width * sum(sizes),
            transcendentals=0,
        ),
        name="outer",
    )(*arrays)


def total_over_dp(value, plane):
    z, zs = lax.axis_index("dp"), lax.axis_size("dp")
    rows = value.shape[0]
    side = rows // plane.cores
    cut = lambda x, at, size: lax.dynamic_slice_in_dim(x, at * size, size, 0)
    put = lambda out, x, at: lax.dynamic_update_slice_in_dim(out, x, at * x.shape[0], 0)
    value = cut(value, plane.m, side) + plane.swap(cut(value, 1 - plane.m, side))
    over_dp = lambda x, k: lax.ppermute(x, "dp", [(i, (i + k) % zs) for i in range(zs)])
    part = side // zs
    mine = cut(value, z, part)
    for k in range(1, zs):
        mine = mine + over_dp(cut(value, (z + k) % zs, part), k)
    out = put(jnp.zeros_like(value), mine, z)
    for k in range(1, zs):
        out = put(out, over_dp(mine, k), (z + zs - k) % zs)
    return out


def total_over_hist(out, plane):
    block = out.shape[0] // plane.size
    cut = lambda x, at: lax.dynamic_slice_in_dim(x, at * block, block, 0)
    mine = cut(out, plane.h)
    for j in range(1, plane.size):
        mine = mine + plane.direct(cut(out, plane.h ^ plane.place(j)), j)
    return mine


def over_plane(mine, plane):
    out = plane.ordered([mine] + [plane.direct(mine, j) for j in range(1, plane.size)])
    return plane.both(out, plane.swap(out), 0).reshape((2 * out.shape[0],) + out.shape[1:])


def interleave(own, sibling, m, half):
    rows, width = own.shape
    count = rows // half

    def kernel(which, own_ref, sibling_ref, out):
        at = lambda side: pl.ds(pl.multiple_of(side * half, half), half)
        out[at(which[0]), :] = own_ref[...]
        out[at(1 - which[0]), :] = sibling_ref[...]

    block = pl.BlockSpec((half, width), lambda a: (a, 0))
    return pl.pallas_call(
        kernel,
        grid=(count,),
        in_specs=[pl.BlockSpec(memory_space=pltpu.SMEM), block, block],
        out_specs=pl.BlockSpec((2 * half, width), lambda a: (a, 0)),
        out_shape=jax.ShapeDtypeStruct((2 * rows, width), own.dtype),
        compiler_params=pltpu.CompilerParams(vmem_limit_bytes=VMEM),
        name="interleave",
    )(m, own, sibling)


def place_wide(blocks, count, pieces, turned):
    depth, cols = blocks.shape[0] // count, blocks.shape[1]
    size = cols // pieces

    def kernel(*refs):
        for i in range(pieces):
            block = refs[0][:, i * size : (i + 1) * size].astype(jnp.float32)
            refs[1 + i][...] = block.T if turned[i] else block

    return pl.pallas_call(
        kernel,
        grid=(count,),
        in_specs=[pl.BlockSpec((depth, cols), lambda a: (a, 0))],
        out_specs=[
            pl.BlockSpec((size, depth), lambda a: (a, 0)) if t else pl.BlockSpec((depth, size), lambda a: (0, a))
            for t in turned
        ],
        out_shape=[
            jax.ShapeDtypeStruct((count * size, depth) if t else (depth, count * size), jnp.float32) for t in turned
        ],
        compiler_params=pltpu.CompilerParams(vmem_limit_bytes=VMEM),
        name="place_wide",
    )(blocks)


def after(value, *others):
    return lax.optimization_barrier((value,) + others)[0]


tie = lax.optimization_barrier


def shards(
    history,
    mixer_in,
    mixer_out,
    mixer_bias,
    norm_gain,
    query_weight,
    key_weight,
    value_weight,
    out_weight,
    up_weight,
    down_weight,
    target,
    loss_count,
    domain,
    domain_scale,
):
    plane = Plane()
    count, cores, h, m = plane.size, plane.cores, plane.h, plane.m
    layers, group_rows, width = history.shape
    rows = target.shape[0]
    half = rows // cores
    depth = query_weight.shape[0]
    assert layers == 1 and cores == 2 and domain.shape[0] == 1 and group_rows == count * rows
    hidden_units = mixer_in.shape[1]
    bf16, f32 = jnp.bfloat16, jnp.float32

    near = count * half
    which_m = m.astype(jnp.int32).reshape(1)
    which_h = h.astype(jnp.int32).reshape(1)

    z, zs = lax.axis_index("dp"), lax.axis_size("dp")
    part = plane.ordered([x[None] for x in plane.gather(norm_gain)])
    gain = lax.dynamic_update_slice_in_dim(jnp.zeros((zs,) + part.shape, bf16), part[None], z, 0)
    for k in range(1, zs):
        came = lax.ppermute(part, "dp", [(i, (i + k) % zs) for i in range(zs)])
        gain = lax.dynamic_update_slice_in_dim(gain, came[None], (z + zs - k) % zs, 0)
    gain = gain.reshape(zs * count, STREAMS, -1).transpose(1, 0, 2).reshape(STREAMS, width).astype(f32)

    parts = 2 if count % 2 == 0 else 1
    per = count // parts
    parted = history.reshape(parts, per, cores, half, width)
    own_rows = [
        lax.dynamic_index_in_dim(parted[g], m, 1, keepdims=False).reshape(per * half, width) for g in range(parts)
    ]
    swap_columns = lambda x: lax.all_to_all(x, "hist", 1, 0, tiled=True)
    slots = [plane.gather(after(own_rows[0], part))]
    up_mine = swap_columns(after(up_weight, part))
    up_full = lax.all_gather(up_mine, "dp", axis=0, tiled=True)
    for g in range(1, parts):
        slots.append(plane.gather(after(own_rows[g], slots[-1][1])))
    packed = jnp.stack([query_weight, key_weight, value_weight, out_weight.T], 0)
    packed = packed.reshape(4, depth, count, -1).transpose(1, 2, 0, 3).reshape(depth, -1)
    narrow_mine = swap_columns(after(packed, up_mine, gain, slots[-1][1]))
    narrow_full = lax.all_gather(narrow_mine, "dp", axis=0, tiled=True)
    piece = narrow_full.shape[1] // 4
    out_full = narrow_full[:, 3 * piece :]

    layer_of = [h ^ plane.place(j) for j in range(count)]
    order = jnp.stack(layer_of).astype(jnp.int32)
    pick = sum(jnp.where(layer_of[j] == count - 1, j, 0) for j in range(count)).astype(jnp.int32).reshape(1)

    def to_slots(values):
        return jnp.stack(
            [sum(jnp.where(layer_of[j] == l, values[..., l], 0) for l in range(count)) for j in range(count)], -1
        )

    def from_slots(values):
        return jnp.stack(
            [sum(jnp.where(layer_of[j] == l, values[..., j], 0) for j in range(count)) for l in range(count)], -1
        )

    pairs = STREAMS * count
    in_wide = jnp.pad(mixer_in, ((0, 0), (0, LANES - hidden_units)))
    out_wide = jnp.pad(
        to_slots(mixer_out).reshape(hidden_units, pairs), ((0, LANES - hidden_units), (0, LANES - pairs))
    )
    bias_wide = jnp.pad(to_slots(mixer_bias).reshape(1, pairs), ((0, 0), (0, LANES - pairs)))

    found = []
    for g in range(parts):
        found = forward_streams(slots[g], g, parts, found, pick, in_wide, out_wide, bias_wide, gain)
        if g == 0:
            down_turned, *found = lax.optimization_barrier((down_weight.T, *found))
    down_mine = swap_columns(down_turned)
    down_full = lax.all_gather(down_mine, "dp", axis=0, tiled=True)
    all_weights = plane.gather(narrow_full[:, : 3 * piece])
    near_streams, (mixes, pres, stats) = list(found[:STREAMS]), found[STREAMS:]
    far_streams = [None] * STREAMS
    for c in reversed(range(STREAMS)):
        far_streams[c] = plane.swap(near_streams[c])
    block = jnp.arange(count)[:, None] * rows + jnp.arange(half)[None, :]
    positions = jnp.concatenate([(block + m * half).reshape(-1), (block + (1 - m) * half).reshape(-1)])

    domain_one = jnp.sum(jnp.where(jnp.arange(domain_scale.shape[0]) == domain[0], domain_scale, 0.0))
    own_target = lax.dynamic_slice_in_dim(target, m * half, half, 0)
    own_scale = lax.dynamic_slice_in_dim(loss_count, m * half, half, 0).astype(f32) * domain_one
    branch_own = (own_target.astype(f32) * own_scale[:, None]).astype(bf16)
    near_grad = plane.ordered(plane.gather(after(branch_own, slots[-1][1])))
    far_grad = plane.swap(near_grad)

    def mlp(stream, grad):
        before = dot(stream, up_full, (1, 0))
        back = dot(grad, down_full, (1, 0)) * gelu_slope(before)
        return gelu_exact(before).astype(bf16), back.astype(bf16)

    near_hidden, near_back = mlp(near_streams[3], near_grad)
    far_hidden, far_back = mlp(far_streams[3], far_grad)
    both = lambda near_one, far_one: [(near_one, 0), (far_one, 0)]
    local = lambda one: [(one, 0), (one, 1)]
    grads = both(near_grad, far_grad)
    down_part = outer([(grads, both(near_hidden, far_hidden))])
    down_sum = lax.psum_scatter(down_part, "dp", scatter_dimension=0, tiled=True)
    near_back, far_back, all_weights[1], *far_streams = lax.optimization_barrier(
        (near_back, far_back, all_weights[1], *far_streams)
    )
    up_part = outer([(both(near_streams[3], far_streams[3]), both(near_back, far_back))])
    up_sum = lax.psum_scatter(up_part, "dp", scatter_dimension=0, tiled=True)

    own_mix = lax.dynamic_slice_in_dim(mixes, h * half, half, 0)[:, :pairs].reshape(half, STREAMS, count)

    def own_block(j):
        found = lax.dynamic_slice_in_dim(slots[0][j], h % per * half, half, 0)
        for g in range(1, parts):
            found = jnp.where(h // per == g, lax.dynamic_slice_in_dim(slots[g][j], h % per * half, half, 0), found)
        return found

    own_layers = [own_block(j) for j in range(count)]
    own_part = lambda x: lax.dynamic_slice_in_dim(x, h * half, half, 0)
    own_given = [own_part(x) for x in near_streams], own_part(mixes), own_part(pres), own_part(stats)
    near_given, far_given, _, _, own_given, own_layers, all_weights[2] = lax.optimization_barrier(
        (near_streams[:3] + [near_grad], far_streams[:3] + [far_grad], up_part, down_part, own_given, own_layers, all_weights[2])
    )

    types = (f32, f32, bf16, bf16)
    attended, query_back, key_back, value_back, backs = attention(
        project(near_given, narrow_full, types), project(far_given, narrow_full, types), positions, which_m, count
    )

    def owned(near_one, far_one):
        return plane.scatter_packed(*add_in_slots(near_one, plane.swap(far_one), order, count))

    near_back, far_back, up_part = lax.optimization_barrier((near_back, far_back, up_part))
    far_mlp = dot(far_back, up_full, (1, 1)).astype(bf16)
    near_mlp = dot(near_back, up_full, (1, 1)).astype(bf16)
    owned_mlp = owned(near_mlp, far_mlp)
    backs, attended, _, down_sum, all_weights = lax.optimization_barrier(
        (backs, attended, owned_mlp, down_sum, all_weights)
    )
    own_backs = [lax.dynamic_slice_in_dim(backs, layer_of[j] * rows, rows, 0) for j in range(count)]
    own_backs = own_backs[:1] + [plane.direct(own_backs[j], j) for j in range(1, count)]
    narrow_part = outer(
        [
            (both(near_streams[0], far_streams[0]), local(query_back)),
            (both(near_streams[1], far_streams[1]), local(key_back)),
            (both(near_streams[2], far_streams[2]), local(value_back)),
            (grads, local(attended)),
        ]
    )
    narrow_sum = lax.psum_scatter(narrow_part, "dp", scatter_dimension=0, tiled=True)
    own_backs, wide_sum, _ = lax.optimization_barrier((own_backs, jnp.concatenate([up_sum, down_sum], 1), narrow_part))
    near_backs, far_backs = project_back(own_backs, all_weights)
    far_backs = plane.swap(far_backs)

    attended = after(attended, near_backs)
    branch_far = (dot(attended[near:], out_full, (1, 1)) + dot(far_hidden, down_full, (1, 1))).astype(bf16)
    branch = (dot(attended[:near], out_full, (1, 1)) + dot(near_hidden, down_full, (1, 1))).astype(bf16)
    branch_slots = add_in_slots(branch, plane.swap(branch_far), order, count)
    branch_low, branch_high = plane.scatter_packed(*branch_slots)
    mix_own = from_slots(own_mix)
    mix_rows = plane.both(mix_own, plane.swap(mix_own), 0).reshape(rows, STREAMS, count)

    def spread(summed):
        return lax.all_to_all(summed, "hist", 0, 0, tiled=True)

    wide_sum = spread(wide_sum)

    scale_wide, _ = tie((jnp.broadcast_to(own_scale[:, None], (half, LANES)), branch_slots))
    found = backward_streams(
        own_layers,
        0,
        half,
        [(near_backs, 0), (near_backs, 1), (near_backs, 2), (owned_mlp[0], 0)],
        [(far_backs, 0), (far_backs, 1), (far_backs, 2), (owned_mlp[1], 0)],
        0,
        *own_given,
        own_target,
        scale_wide,
        pick,
        order,
        in_wide,
        out_wide,
        gain,
    )
    layer_grads, sums = found[0], found[1:]
    came = lax.all_to_all(layer_grads, "hist", 0, 0, tiled=True)
    gain_sum, in_sum, out_sum, bias_sum = sums
    out_sum = from_slots(out_sum[:, :pairs].reshape(LANES, STREAMS, count)).reshape(LANES, pairs)
    bias_sum = from_slots(bias_sum[:, :pairs].reshape(1, STREAMS, count)).reshape(1, pairs)
    spare = LANES - hidden_units - STREAMS
    spare -= spare % 8
    packed_sum = jnp.concatenate([out_sum, bias_sum], 0).reshape(-1)
    packed_sum = jnp.pad(packed_sum, (0, width * spare - packed_sum.shape[0])).reshape(width, spare)
    small = jnp.concatenate([in_sum[:, :hidden_units], gain_sum.T, packed_sum], 1)
    small = total_over_dp(jnp.pad(small, ((0, 0), (0, LANES - small.shape[1]))), plane)
    came, small, narrow_sum, wide_sum, branch_low = tie((came, small, narrow_sum, wide_sum, branch_low))
    swapped = plane.swap(came)
    narrow_sum = spread(narrow_sum)
    small = total_over_hist(small, plane)
    history_grad = interleave(came, swapped, which_m, half).reshape(history.shape)
    up_grad, down_grad = place_wide(wide_sum, count, 2, (False, True))
    history_grad, up_grad, down_grad, narrow_sum, small, branch_low, branch_high = tie(
        (history_grad, up_grad, down_grad, narrow_sum, small, branch_low, branch_high)
    )
    branch_rows = branch_low.astype(f32) + branch_high.astype(f32)
    residual = sum(own_mix[:, STREAMS - 1, j, None] * own_layers[j].astype(f32) for j in range(count))
    output_own = (residual + branch_rows).astype(bf16)
    output = plane.both(output_own, plane.swap(output_own), 0).reshape(rows, width)
    query_grad, key_grad, value_grad, out_grad = place_wide(narrow_sum, count, 4, (False, False, False, True))
    small = over_plane(small, plane)
    mixer_in_grad = small[:, :hidden_units]
    gain_all = small[:, hidden_units : hidden_units + STREAMS].T
    place = (z * count + h) * norm_gain.shape[1]
    norm_gain_grad = lax.dynamic_slice_in_dim(gain_all, place, norm_gain.shape[1], 1)
    tail = small[:, hidden_units + STREAMS : hidden_units + STREAMS + spare].reshape(-1)[: (LANES + 1) * pairs]
    tail = tail.reshape(LANES + 1, STREAMS, count)
    mixer_out_grad = tail[:hidden_units]
    mixer_bias_grad = tail[LANES]
    return (
        output,
        mix_rows,
        history_grad,
        mixer_in_grad,
        mixer_out_grad,
        mixer_bias_grad,
        norm_gain_grad,
        query_grad,
        key_grad,
        value_grad,
        out_grad,
        up_grad,
        down_grad,
    )


def solution(mesh):
    in_specs = (
        P("hist", "dp", None),
        P(),
        P(),
        P(),
        P(None, ("dp", "hist")),
        P(("dp", "hist"), "mp"),
        P(("dp", "hist"), "mp"),
        P(("dp", "hist"), "mp"),
        P("mp", ("dp", "hist")),
        P(("dp", "hist"), "mp"),
        P("mp", ("dp", "hist")),
        P(("dp", "hist"), None),
        P(("dp", "hist")),
        P("dp"),
        P(),
    )
    out_specs = (
        P(("dp", "hist"), None),
        P(("dp", "hist"), None, None),
        P("hist", "dp", None),
        P(),
        P(),
        P(),
        P(None, ("dp", "hist")),
        P(("dp", "hist"), "mp"),
        P(("dp", "hist"), "mp"),
        P(("dp", "hist"), "mp"),
        P("mp", ("dp", "hist")),
        P(("dp", "hist"), "mp"),
        P("mp", ("dp", "hist")),
    )
    return jax.shard_map(shards, mesh=mesh, in_specs=in_specs, out_specs=out_specs, check_vma=False)
```

```python
import jax
import jax.numpy as jnp
from jax import lax
from jax.experimental import pallas as pl
from jax.experimental.pallas import tpu as pltpu
from jax.sharding import PartitionSpec as P

HD = 128
ROT = 32
STREAMS = 4
LANES = 128
GROUP = 16
UNROLL = 1

HIGHEST = lax.Precision.HIGHEST
EPS_NORM = 1e-05
EPS_RMS = 1e-06
ROPE_BASE = 10000.0
VMEM = 56 * 2**20
PLANE = ("hist", "mp")


def dot(left, right, contract):
    return lax.dot_general(
        left, right, (((contract[0],), (contract[1],)), ((), ())), preferred_element_type=jnp.float32
    )


def gelu_exact(value):
    return 0.5 * value * (1.0 + lax.erf(value * 0.7071067811865476))


def gelu_slope(value):
    return (
        0.5 * (1.0 + lax.erf(value * 0.7071067811865476))
        + value * jnp.exp(-0.5 * value * value) * 0.3989422804014327
    )


class Plane:
    def __init__(self):
        self.size = lax.axis_size("hist")
        self.cores = lax.axis_size("mp")
        self.bits = self.size.bit_length() - 1
        assert self.size == 1 << self.bits
        self.h = lax.axis_index("hist")
        self.m = lax.axis_index("mp")

    def turned(self, j):
        return sum(((j >> b) & 1) << (self.bits - 1 - b) for b in range(self.bits))

    def place(self, j):
        return jnp.where(self.m % 2 == 0, j, self.turned(j))

    def step(self, value, i):
        pairs = []
        for h in range(self.size):
            for m in range(self.cores):
                bit = 1 << (i if m % 2 == 0 else self.bits - 1 - i)
                pairs.append((h * self.cores + m, (h ^ bit) * self.cores + m))
        return lax.ppermute(value, PLANE, pairs)

    def gather(self, value):
        slots = [value]
        for i in range(self.bits):
            slots = slots + [self.step(s, i) for s in slots]
        return slots

    def scatter(self, held):
        for i in reversed(range(self.bits)):
            got = [self.step(x, i) for x in held[1 << i :]]
            held = [
                (x.astype(jnp.float32) + y.astype(jnp.float32)).astype(x.dtype)
                for x, y in zip(held[: 1 << i], got)
            ]
        return held[0]

    def scatter_packed(self, low, high):
        for i in reversed(range(self.bits)):
            got = self.step(high, i)
            if i == 0:
                return low, got
            total = (low.astype(jnp.float32) + got.astype(jnp.float32)).astype(low.dtype)
            side = total.shape[0] // 2
            low, high = total[:side], total[side:]

    def direct(self, value, j):
        pairs = []
        for h in range(self.size):
            for m in range(self.cores):
                place = j if m % 2 == 0 else self.turned(j)
                pairs.append((h * self.cores + m, (h ^ place) * self.cores + m))
        return lax.ppermute(value, PLANE, pairs)

    def ordered(self, slots):
        rows = slots[0].shape[0]
        out = jnp.zeros((self.size * rows,) + slots[0].shape[1:], slots[0].dtype)
        for j, slot in enumerate(slots):
            out = lax.dynamic_update_slice_in_dim(out, slot, (self.h ^ self.place(j)) * rows, 0)
        return out

    def trade(self, wide):
        cols = wide.shape[1] // self.size
        block = lambda r: lax.dynamic_slice_in_dim(wide, (self.h ^ r) * cols, cols, 1)
        return [block(0)] + [
            lax.ppermute(block(r), "hist", [(h, h ^ r) for h in range(self.size)]) for r in range(1, self.size)
        ]

    def trade_rows(self, tall):
        rows = tall.shape[0] // self.size
        block = lambda r: lax.dynamic_slice_in_dim(tall, (self.h ^ r) * rows, rows, 0)
        return [block(0)] + [
            lax.ppermute(block(r), "hist", [(h, h ^ r) for h in range(self.size)]) for r in range(1, self.size)
        ]

    def stacked(self, entries):
        rows = entries[0].shape[0]
        out = jnp.zeros((self.size * rows,) + entries[0].shape[1:], entries[0].dtype)
        for r, entry in enumerate(entries):
            out = lax.dynamic_update_slice_in_dim(out, entry, (self.h ^ r) * rows, 0)
        return out

    def swap(self, value):
        return lax.ppermute(value, "mp", [(m, m ^ 1) for m in range(self.cores)])

    def both(self, own, sibling, axis):
        first = self.m % 2 == 0
        return jnp.stack([jnp.where(first, own, sibling), jnp.where(first, sibling, own)], axis)


def forward_kernel(count, pick, *refs):
    slots = refs[:count]
    in_ref, out_ref, bias_ref, gain_ref = refs[count : count + 4]
    normed = refs[count + 4 : count + 4 + STREAMS]
    mix_ref, pre_ref, stat_ref, last_ref = refs[count + 4 + STREAMS :]
    for j in range(count):

        @pl.when(pick[0] == j)
        def _(j=j):
            last_ref[...] = slots[j][...]

    tile = last_ref.shape[0]
    last = last_ref[...].astype(jnp.float32)
    inverse = lax.rsqrt(jnp.mean(last * last, -1, keepdims=True) + EPS_RMS)
    unit = (last * inverse).astype(jnp.bfloat16)
    pre = jnp.dot(unit, in_ref[...], preferred_element_type=jnp.float32)
    pre_ref[...] = pre
    hidden = gelu_exact(pre).astype(jnp.bfloat16)
    mix_ref[...] = (
        jnp.dot(hidden, out_ref[...], preferred_element_type=jnp.float32) + bias_ref[...]
    )
    lane = lax.broadcasted_iota(jnp.int32, (GROUP, LANES), 1)

    def group(g, carry):
        rows = pl.ds(pl.multiple_of(g * GROUP, GROUP), GROUP)
        mix = mix_ref[rows, :]
        parts = [s[rows, :].astype(jnp.float32) for s in slots]
        stat = jnp.zeros((GROUP, LANES), jnp.float32)
        for c in range(STREAMS):
            stream = mix[:, c * count : c * count + 1] * parts[0]
            for j in range(1, count):
                stream = stream + mix[:, c * count + j : c * count + j + 1] * parts[j]
            centered = stream - jnp.mean(stream, -1, keepdims=True)
            scale = lax.rsqrt(jnp.mean(centered * centered, -1, keepdims=True) + EPS_NORM)
            normed[c][rows, :] = (centered * scale * gain_ref[c : c + 1, :]).astype(jnp.bfloat16)
            stat = jnp.where(lane == c, scale, stat)
        stat_ref[rows, :] = stat
        return carry

    lax.fori_loop(0, tile // GROUP, group, 0, unroll=UNROLL)


def forward_streams(slots, at, blocks, before, pick, mixer_in, mixer_out, bias, gain):
    count = len(slots)
    rows, width = slots[0].shape
    tile = min(128, rows)
    steps = rows // tile
    whole = lambda shape: pl.BlockSpec(shape, lambda i: (0,) * len(shape))
    by_row = lambda cols: pl.BlockSpec((tile, cols), lambda i: (i, 0))
    shifted = lambda cols: pl.BlockSpec((tile, cols), lambda i: (at * steps + i, 0))
    given = 1 + count + 4
    return pl.pallas_call(
        lambda *refs: forward_kernel(count, *refs[:given], *refs[given + len(before) :]),
        grid=(steps,),
        in_specs=[pl.BlockSpec(memory_space=pltpu.SMEM)]
        + [by_row(width)] * count
        + [whole(mixer_in.shape), whole(mixer_out.shape), whole(bias.shape), whole(gain.shape)]
        + [pl.BlockSpec(memory_space=pl.ANY)] * len(before),
        out_specs=[shifted(width)] * STREAMS + [shifted(LANES)] * 3,
        out_shape=[jax.ShapeDtypeStruct((blocks * rows, width), jnp.bfloat16)] * STREAMS
        + [jax.ShapeDtypeStruct((blocks * rows, LANES), jnp.float32)] * 3,
        input_output_aliases={given + i: i for i in range(len(before))},
        scratch_shapes=[pltpu.VMEM((tile, width), jnp.bfloat16)],
        compiler_params=pltpu.CompilerParams(vmem_limit_bytes=VMEM),
        cost_estimate=pl.CostEstimate(
            flops=rows * width * 80, bytes_accessed=rows * width * 2 * (count + STREAMS), transcendentals=0
        ),
        name="forward_streams",
    )(pick, *slots, mixer_in, mixer_out, bias, gain, *before)


def split_dot(left, right, contract):
    high = right.astype(jnp.bfloat16)
    low = (right - high.astype(jnp.float32)).astype(jnp.bfloat16)
    return dot(left, high, contract) + dot(left, low, contract)


def backward_kernel(count, half, pick, order, *refs):
    slots, refs = refs[:count], refs[count:]
    mine, refs = refs[:STREAMS], refs[STREAMS:]
    theirs, refs = refs[:STREAMS], refs[STREAMS:]
    normed, refs = refs[:STREAMS], refs[STREAMS:]
    mix_ref, pre_ref, stat_ref, target_ref, scale_ref, refs = *refs[:5], refs[5:]
    in_ref, out_ref, gain_ref, inverse_gain_ref, refs = *refs[:4], refs[4:]
    grads_ref, refs = refs[0], refs[1:]
    gain_grad_ref, in_grad_ref, out_grad_ref, bias_grad_ref, last_ref, dmix_ref, gain_sum = refs
    tile = last_ref.shape[0]

    @pl.when(pl.program_id(0) == 0)
    def _():
        gain_sum[...] = jnp.zeros_like(gain_sum)
        in_grad_ref[...] = jnp.zeros_like(in_grad_ref)
        out_grad_ref[...] = jnp.zeros_like(out_grad_ref)
        bias_grad_ref[...] = jnp.zeros_like(bias_grad_ref)

    for j in range(count):

        @pl.when(pick[0] == j)
        def _(j=j):
            last_ref[...] = slots[j][...]

    lane = lax.broadcasted_iota(jnp.int32, (GROUP, LANES), 1)

    def placed(j, start, size):
        return pl.ds(pl.multiple_of(order[j] * half + pl.program_id(0) * tile + start, GROUP), size)

    def group(g, carry):
        rows = pl.ds(pl.multiple_of(g * GROUP, GROUP), GROUP)
        mix = mix_ref[rows, :]
        stat = stat_ref[rows, :]
        dmix = jnp.zeros((GROUP, LANES), jnp.float32)
        grad = []
        for c in range(STREAMS):
            total = mine[c][rows, :].astype(jnp.float32) + theirs[c][rows, :].astype(jnp.float32)
            unit = normed[c][rows, :].astype(jnp.float32) * inverse_gain_ref[c : c + 1, :]
            product = total * unit
            gain_sum[c] += product[:8] + product[8:]
            scaled = total * gain_ref[c : c + 1, :]
            mean = jnp.mean(scaled, -1, keepdims=True)
            along = jnp.mean(product * gain_ref[c : c + 1, :], -1, keepdims=True)
            one = stat[:, c : c + 1] * (scaled - mean - unit * along)
            if c == STREAMS - 1:
                one = one + target_ref[rows, :].astype(jnp.float32) * scale_ref[rows, :1]
            grad.append(one)
        for j in range(count):
            part = slots[j][rows, :].astype(jnp.float32)
            total = mix[:, j : j + 1] * grad[0]
            for c in range(1, STREAMS):
                total = total + mix[:, c * count + j : c * count + j + 1] * grad[c]
            grads_ref[placed(j, g * GROUP, GROUP), :] = total.astype(jnp.bfloat16)
            for c in range(STREAMS):
                value = jnp.sum(grad[c] * part, -1, keepdims=True)
                dmix = jnp.where(lane == c * count + j, value, dmix)
        dmix_ref[rows, :] = dmix
        return carry

    lax.fori_loop(0, tile // GROUP, group, 0, unroll=UNROLL)
    dmix = dmix_ref[...]
    last = last_ref[...].astype(jnp.float32)
    inverse = lax.rsqrt(jnp.mean(last * last, -1, keepdims=True) + EPS_RMS)
    unit = (last * inverse).astype(jnp.bfloat16)
    pre = pre_ref[...]
    hidden = gelu_exact(pre).astype(jnp.bfloat16)
    hidden_grad = lax.dot_general(
        dmix,
        out_ref[...].astype(jnp.float32),
        (((1,), (1,)), ((), ())),
        precision=HIGHEST,
        preferred_element_type=jnp.float32,
    )
    pre_grad = hidden_grad * gelu_slope(pre)
    in_grad_ref[...] += split_dot(unit, pre_grad, (0, 0))
    out_grad_ref[...] += split_dot(hidden, dmix, (0, 0))
    bias_grad_ref[...] += jnp.sum(dmix, 0, keepdims=True)
    high = pre_grad.astype(jnp.bfloat16)
    low = (pre_grad - high.astype(jnp.float32)).astype(jnp.bfloat16)
    unit_grad = dot(high, in_ref[...], (1, 1)) + dot(low, in_ref[...], (1, 1))
    cube = inverse * inverse * inverse * jnp.mean(unit_grad * last, -1, keepdims=True)
    extra = inverse * unit_grad - last * cube
    for j in range(count):

        @pl.when(pick[0] == j)
        def _(j=j):
            place = placed(j, 0, tile)
            grads_ref[place, :] = (grads_ref[place, :].astype(jnp.float32) + extra).astype(jnp.bfloat16)

    @pl.when(pl.program_id(0) == pl.num_programs(0) - 1)
    def _():
        gain_grad_ref[...] = jnp.sum(gain_sum[...], 1)


def backward_streams(slots, start, half, mine, theirs, at, normed, mix, pre, stat, target, scale, pick, order, mixer_in, mixer_out, gain):
    count = len(slots)
    rows, width = half, slots[0].shape[1]
    tile = min(128, rows)
    steps = rows // tile
    whole = lambda shape: pl.BlockSpec(shape, lambda i: (0,) * len(shape))
    by_row = lambda cols: pl.BlockSpec((tile, cols), lambda i: (i, 0))
    shifted = lambda cols: pl.BlockSpec((tile, cols), lambda i: (at * steps + i, 0))
    within = pl.BlockSpec((tile, width), lambda i: (start // tile + i, 0))
    hidden = mixer_in.shape[1]
    return pl.pallas_call(
        lambda *refs: backward_kernel(count, half, *refs),
        grid=(steps,),
        in_specs=[pl.BlockSpec(memory_space=pltpu.SMEM)] * 2
        + [within] * count
        + [pl.BlockSpec((tile, width), lambda i, c=c: (at * steps + i, c)) for _, c in mine + theirs]
        + [shifted(width)] * STREAMS
        + [shifted(LANES)] * 3
        + [by_row(width), by_row(LANES)]
        + [whole(mixer_in.shape), whole(mixer_out.shape), whole(gain.shape), whole(gain.shape)],
        out_specs=[whole((count * half, width))]
        + [whole((STREAMS, width)), whole((width, hidden)), whole((hidden, LANES)), whole((1, LANES))],
        out_shape=[jax.ShapeDtypeStruct((count * half, width), jnp.bfloat16)]
        + [
            jax.ShapeDtypeStruct((STREAMS, width), jnp.float32),
            jax.ShapeDtypeStruct((width, hidden), jnp.float32),
            jax.ShapeDtypeStruct((hidden, LANES), jnp.float32),
            jax.ShapeDtypeStruct((1, LANES), jnp.float32),
        ],
        scratch_shapes=[
            pltpu.VMEM((tile, width), jnp.bfloat16),
            pltpu.VMEM((tile, LANES), jnp.float32),
            pltpu.VMEM((STREAMS, 8, width), jnp.float32),
        ],
        compiler_params=pltpu.CompilerParams(vmem_limit_bytes=VMEM),
        cost_estimate=pl.CostEstimate(
            flops=rows * width * 160,
            bytes_accessed=rows * width * 2 * (2 * count + 3 * STREAMS),
            transcendentals=0,
        ),
        name="backward_streams",
    )(pick, order, *slots, *(x for x, _ in mine + theirs), *normed, mix, pre, stat, target, scale, mixer_in, mixer_out, gain, 1.0 / gain)


def rope_tables(positions):
    side = ROT // 2
    freq = ROPE_BASE ** (-2.0 * jnp.arange(side, dtype=jnp.float32) / ROT)
    angle = positions.astype(jnp.float32)[:, None] * freq[None, :]
    cosine, sine = jnp.cos(angle), jnp.sin(angle)
    rest = HD - ROT
    return (
        jnp.pad(jnp.concatenate([cosine, cosine], 1), ((0, 0), (0, rest)), constant_values=1.0),
        jnp.pad(-sine, ((0, 0), (0, HD - side))),
        jnp.pad(sine, ((0, 0), (side, rest))),
    )


def turn(value, cosine, right, left, sign):
    side = ROT // 2
    moved = pltpu.roll(value, HD - side, 1) * right + pltpu.roll(value, side, 1) * left
    return value * cosine + moved * sign


def attention_kernel(count, half, heads, which, *refs):
    near, far, (cos_ref, right_ref, left_ref) = refs[:4], refs[4:8], refs[8:11]
    o_ref, dq_ref, dk_ref, dv_ref, all_ref = refs[11:16]
    q_s, k_s, v_s, g_s, k_t, v_t, g_t, dk_s, dv_s, p_s, o_s, dq_s = refs[16:]
    piece = heads * HD
    block = 2 * half
    scale = HD ** (-0.5)
    bf16, f32 = jnp.bfloat16, jnp.float32
    m = which[0]

    def cols(n):
        return slice(n * HD, (n + 1) * HD)

    def part(b):
        return pl.ds(pl.multiple_of(b * half, half), half)

    def span(j):
        return pl.ds(pl.multiple_of(j * block, block), block)

    def turned(value, here, sign):
        return turn(value, cos_ref[here, :], right_ref[here, :], left_ref[here, :], sign)

    for side, (q_ref, k_ref, v_ref, g_ref) in enumerate((near, far)):

        def prepare(a, carry, side=side, q_ref=q_ref, k_ref=k_ref, v_ref=v_ref, g_ref=g_ref):
            rows, here, there = part(a), part(side * count + a), part(2 * a + (side ^ m))
            for n in range(heads):
                q_s[there, cols(n)] = turned(q_ref[rows, cols(n)], here, 1.0).astype(bf16)
                keys = turned(k_ref[rows, cols(n)], here, 1.0)
                k_s[there, cols(n)] = keys.astype(bf16)
                k_t[cols(n), there] = keys.T.astype(bf16)
                v_t[cols(n), there] = v_ref[rows, cols(n)].astype(f32).T.astype(bf16)
                g_t[cols(n), there] = g_ref[rows, cols(n)].astype(f32).T.astype(bf16)
            v_s[there, :] = v_ref[rows, :]
            g_s[there, :] = g_ref[rows, :]
            dk_s[there, :] = jnp.zeros((half, piece), f32)
            dv_s[there, :] = jnp.zeros((half, piece), f32)
            return carry

        lax.fori_loop(0, count, prepare, 0)
    later = lax.broadcasted_iota(jnp.int32, (block, block), 0) > lax.broadcasted_iota(jnp.int32, (block, block), 1)

    def rows_of_eight(value, op):
        out = value[:8]
        for at in range(8, value.shape[0], 8):
            out = op(out, value[at : at + 8])
        return out

    def query_block(i, carry):
        here = span(i)
        queries = [q_s[here, cols(n)] for n in range(heads)]
        grads = [g_s[here, cols(n)] for n in range(heads)]

        def scores(j, tops, last=False):
            there = span(j)
            out = []
            for n in range(heads):
                s = dot(k_s[there, cols(n)], queries[n], (1, 1)) * (scale * 1.4426950408889634)
                if last:
                    s = jnp.where(later, -1e30, s)
                p_s[n, there, :] = s
                out.append(jnp.maximum(tops[n], rows_of_eight(s, jnp.maximum)))
            return tuple(out)

        tops = lax.fori_loop(0, i, scores, tuple(jnp.full((8, block), -1e30, f32) for _ in range(heads)))
        tops = [jnp.max(x, 0, keepdims=True) for x in scores(i, tops, True)]
        o_s[...] = jnp.zeros(o_s.shape, f32)
        dq_s[...] = jnp.zeros(dq_s.shape, f32)

        def mixing(j, sums):
            there = span(j)
            out = []
            for n in range(heads):
                p = jnp.exp2(p_s[n, there, :] - tops[n])
                p_s[n, there, :] = p
                out.append(sums[n] + rows_of_eight(p, jnp.add))
                o_s[n] += dot(v_t[cols(n), there], p.astype(bf16), (1, 0))
            return tuple(out)

        sums = lax.fori_loop(0, i + 1, mixing, tuple(jnp.zeros((8, block), f32) for _ in range(heads)))
        shares, deltas = [], []
        for n in range(heads):
            share = 1.0 / jnp.sum(sums[n], 0, keepdims=True)
            found = o_s[n] * share
            deltas.append(jnp.sum(found * g_t[cols(n), here].astype(f32), 0, keepdims=True))
            found = found.T.astype(bf16)
            for b in range(2):
                o_ref[part((b ^ m) * count + i), cols(n)] = found[b * half : (b + 1) * half]
            shares.append(share)

        def back(j, c):
            there = span(j)
            for n in range(heads):
                p = p_s[n, there, :] * shares[n]
                dp = dot(v_s[there, cols(n)], grads[n], (1, 1))
                ds = (p * (dp - deltas[n])).astype(bf16)
                dq_s[n] += dot(k_t[cols(n), there], ds, (1, 0))
                dk_s[there, cols(n)] += dot(ds, queries[n], (1, 0))
                dv_s[there, cols(n)] += dot(p.astype(bf16), grads[n], (1, 0))
            return c

        lax.fori_loop(0, i + 1, back, 0)
        for n in range(heads):
            found = dq_s[n].T * scale
            for b in range(2):
                rows = part((b ^ m) * count + i)
                value = turned(found[b * half : (b + 1) * half], rows, -1.0).astype(bf16)
                dq_ref[rows, cols(n)] = value
                all_ref[part(2 * i + (b ^ m)), cols(n)] = value
        return carry

    lax.fori_loop(0, count, query_block, 0)
    for side in range(2):

        def finish(a, carry, side=side):
            here, there, place = part(side * count + a), part(2 * a + (side ^ m)), part(2 * a + side)
            for n in range(heads):
                found = turned(dk_s[there, cols(n)] * scale, here, -1.0).astype(bf16)
                dk_ref[here, cols(n)] = found
                all_ref[place, cols(heads + n)] = found
            found = dv_s[there, :].astype(bf16)
            dv_ref[here, :] = found
            all_ref[place, 2 * piece : 3 * piece] = found
            return carry

        lax.fori_loop(0, count, finish, 0)


def attention(near, far, tables, which, count):
    rows, piece = 2 * near[0].shape[0], near[0].shape[1]
    heads, half = piece // HD, rows // (2 * count)
    vmem = pl.BlockSpec(memory_space=pltpu.VMEM)
    out = jax.ShapeDtypeStruct((rows, piece), jnp.bfloat16)
    wide = lambda *shape: pltpu.VMEM(shape, jnp.float32)
    return pl.pallas_call(
        lambda *refs: attention_kernel(count, half, heads, *refs),
        in_specs=[pl.BlockSpec(memory_space=pltpu.SMEM)] + [vmem] * 11,
        out_specs=[vmem] * 5,
        out_shape=[out] * 4 + [jax.ShapeDtypeStruct((rows, 3 * piece), jnp.bfloat16)],
        scratch_shapes=[pltpu.VMEM((rows, piece), jnp.bfloat16)] * 4
        + [pltpu.VMEM((piece, rows), jnp.bfloat16)] * 3
        + [
            wide(rows, piece),
            wide(rows, piece),
            wide(heads, rows, 2 * half),
            wide(heads, HD, 2 * half),
            wide(heads, HD, 2 * half),
        ],
        compiler_params=pltpu.CompilerParams(vmem_limit_bytes=VMEM),
        cost_estimate=pl.CostEstimate(
            flops=18 * rows * rows * piece, bytes_accessed=rows * piece * 20, transcendentals=rows * rows * heads // 2
        ),
        name="attention",
    )(which, *near, *far, *tables)


def project(streams, weights, types):
    rows, width = streams[0].shape
    count = len(streams)
    piece = weights.shape[1] // count
    tile = min(512, rows)

    def kernel(*refs):
        for c in range(count):
            found = dot(refs[c][...], refs[count][:, c * piece : (c + 1) * piece], (1, 0))
            refs[count + 1 + c][...] = found.astype(types[c])

    return pl.pallas_call(
        kernel,
        grid=(rows // tile,),
        in_specs=[pl.BlockSpec((tile, width), lambda i: (i, 0))] * count
        + [pl.BlockSpec(weights.shape, lambda i: (0, 0))],
        out_specs=[pl.BlockSpec((tile, piece), lambda i: (i, 0))] * count,
        out_shape=[jax.ShapeDtypeStruct((rows, piece), t) for t in types],
        compiler_params=pltpu.CompilerParams(vmem_limit_bytes=VMEM),
        cost_estimate=pl.CostEstimate(
            flops=2 * rows * width * piece * count, bytes_accessed=2 * rows * width * count, transcendentals=0
        ),
        name="project",
    )(*streams, weights)


def project_back(entries, weights):
    count = len(entries)
    rows, piece = entries[0].shape[0], entries[0].shape[1] // 3
    width = weights[0].shape[0]
    side = rows // 2

    def kernel(*refs):
        found = dot(refs[0][...], refs[count][...], (1, 1))
        for j in range(1, count):
            found = found + dot(refs[j][...], refs[count + j][...], (1, 1))
        refs[2 * count][...] = found[:side].astype(jnp.bfloat16)
        refs[2 * count + 1][...] = found[side:].astype(jnp.bfloat16)

    return pl.pallas_call(
        kernel,
        grid=(3, 2),
        in_specs=[pl.BlockSpec((rows, piece), lambda c, i: (0, c))] * count
        + [pl.BlockSpec((width // 2, piece), lambda c, i: (i, c))] * count,
        out_specs=[pl.BlockSpec((side, width // 2), lambda c, i: (0, 2 * c + i))] * 2,
        out_shape=[jax.ShapeDtypeStruct((side, 3 * width), jnp.bfloat16)] * 2,
        compiler_params=pltpu.CompilerParams(vmem_limit_bytes=VMEM),
        name="project_back",
    )(*entries, *weights)


def add_in_slots(near, far, order, count):
    rows, width = near.shape
    block = rows // count
    tile = min(256, block)
    steps = block // tile
    side = count // 2

    def kernel(order, a, b, c, d, low, high):
        low[...] = (a[...].astype(jnp.float32) + b[...].astype(jnp.float32)).astype(jnp.bfloat16)
        high[...] = (c[...].astype(jnp.float32) + d[...].astype(jnp.float32)).astype(jnp.bfloat16)

    def spec(shift):
        return pl.BlockSpec((tile, width), lambda j, i, order: (order[shift + j] * steps + i, 0))

    out = pl.BlockSpec((tile, width), lambda j, i, order: (j * steps + i, 0))
    return pl.pallas_call(
        kernel,
        grid_spec=pltpu.PrefetchScalarGridSpec(
            num_scalar_prefetch=1,
            grid=(side, steps),
            in_specs=[spec(0), spec(0), spec(side), spec(side)],
            out_specs=[out, out],
        ),
        out_shape=[jax.ShapeDtypeStruct((rows // 2, width), jnp.bfloat16)] * 2,
        compiler_params=pltpu.CompilerParams(vmem_limit_bytes=VMEM),
        name="add_in_slots",
    )(order, near, far, near, far)


def outer(groups):
    pieces = len(groups[0][0])
    rows = min(a.shape[0] for a, _ in groups[0][0])
    width = groups[0][0][0][0].shape[1]
    tile = min(512, width)
    sizes = [right[0][0].shape[1] for _, right in groups]
    specs, arrays = [], []
    for left, right in groups:
        for a, k in left:
            specs.append(pl.BlockSpec((rows, tile), lambda i, k=k: (k, i)))
            arrays.append(a)
        for b, k in right:
            specs.append(pl.BlockSpec((rows, b.shape[1]), lambda i, k=k: (k, 0)))
            arrays.append(b)

    def kernel(*refs):
        out, at = refs[-1], 0
        for g, size in enumerate(sizes):
            mine = refs[2 * pieces * g : 2 * pieces * (g + 1)]
            found = dot(mine[0][...], mine[pieces][...], (0, 0))
            for p in range(1, pieces):
                found = found + dot(mine[p][...], mine[pieces + p][...], (0, 0))
            out[:, at : at + size] = found.astype(jnp.bfloat16)
            at += size

    total_rows = rows * pieces
    return pl.pallas_call(
        kernel,
        grid=(width // tile,),
        in_specs=specs,
        out_specs=pl.BlockSpec((tile, sum(sizes)), lambda i: (i, 0)),
        out_shape=jax.ShapeDtypeStruct((width, sum(sizes)), jnp.bfloat16),
        compiler_params=pltpu.CompilerParams(vmem_limit_bytes=VMEM),
        cost_estimate=pl.CostEstimate(
            flops=2 * total_rows * width * sum(sizes),
            bytes_accessed=2 * total_rows * (width * len(groups) + sum(sizes)) + 2 * width * sum(sizes),
            transcendentals=0,
        ),
        name="outer",
    )(*arrays)


def total_over_dp(value, plane):
    z, zs = lax.axis_index("dp"), lax.axis_size("dp")
    rows = value.shape[0]
    side = rows // plane.cores
    cut = lambda x, at, size: lax.dynamic_slice_in_dim(x, at * size, size, 0)
    put = lambda out, x, at: lax.dynamic_update_slice_in_dim(out, x, at * x.shape[0], 0)
    value = cut(value, plane.m, side) + plane.swap(cut(value, 1 - plane.m, side))
    over_dp = lambda x, k: lax.ppermute(x, "dp", [(i, (i + k) % zs) for i in range(zs)])
    part = side // zs
    mine = cut(value, z, part)
    for k in range(1, zs):
        mine = mine + over_dp(cut(value, (z + k) % zs, part), k)
    out = put(jnp.zeros_like(value), mine, z)
    for k in range(1, zs):
        out = put(out, over_dp(mine, k), (z + zs - k) % zs)
    return out


def total_over_hist(out, plane):
    block = out.shape[0] // plane.size
    cut = lambda x, at: lax.dynamic_slice_in_dim(x, at * block, block, 0)
    mine = cut(out, plane.h)
    for j in range(1, plane.size):
        mine = mine + plane.direct(cut(out, plane.h ^ plane.place(j)), j)
    return mine


def over_plane(mine, plane):
    out = plane.ordered([mine] + [plane.direct(mine, j) for j in range(1, plane.size)])
    return plane.both(out, plane.swap(out), 0).reshape((2 * out.shape[0],) + out.shape[1:])


def interleave(own, sibling, m, half):
    rows, width = own.shape
    count = rows // half

    def kernel(which, own_ref, sibling_ref, out):
        at = lambda side: pl.ds(pl.multiple_of(side * half, half), half)
        out[at(which[0]), :] = own_ref[...]
        out[at(1 - which[0]), :] = sibling_ref[...]

    block = pl.BlockSpec((half, width), lambda a: (a, 0))
    return pl.pallas_call(
        kernel,
        grid=(count,),
        in_specs=[pl.BlockSpec(memory_space=pltpu.SMEM), block, block],
        out_specs=pl.BlockSpec((2 * half, width), lambda a: (a, 0)),
        out_shape=jax.ShapeDtypeStruct((2 * rows, width), own.dtype),
        compiler_params=pltpu.CompilerParams(vmem_limit_bytes=VMEM),
        name="interleave",
    )(m, own, sibling)


def place_wide(blocks, count, pieces, turned):
    depth, cols = blocks.shape[0] // count, blocks.shape[1]
    size = cols // pieces

    def kernel(*refs):
        for i in range(pieces):
            block = refs[0][:, i * size : (i + 1) * size].astype(jnp.float32)
            refs[1 + i][...] = block.T if turned[i] else block

    return pl.pallas_call(
        kernel,
        grid=(count,),
        in_specs=[pl.BlockSpec((depth, cols), lambda a: (a, 0))],
        out_specs=[
            pl.BlockSpec((size, depth), lambda a: (a, 0)) if t else pl.BlockSpec((depth, size), lambda a: (0, a))
            for t in turned
        ],
        out_shape=[
            jax.ShapeDtypeStruct((count * size, depth) if t else (depth, count * size), jnp.float32) for t in turned
        ],
        compiler_params=pltpu.CompilerParams(vmem_limit_bytes=VMEM),
        name="place_wide",
    )(blocks)


def after(value, *others):
    return lax.optimization_barrier((value,) + others)[0]


tie = lax.optimization_barrier


def shards(
    history,
    mixer_in,
    mixer_out,
    mixer_bias,
    norm_gain,
    query_weight,
    key_weight,
    value_weight,
    out_weight,
    up_weight,
    down_weight,
    target,
    loss_count,
    domain,
    domain_scale,
):
    plane = Plane()
    count, cores, h, m = plane.size, plane.cores, plane.h, plane.m
    layers, group_rows, width = history.shape
    rows = target.shape[0]
    half = rows // cores
    depth = query_weight.shape[0]
    assert layers == 1 and cores == 2 and domain.shape[0] == 1 and group_rows == count * rows
    hidden_units = mixer_in.shape[1]
    bf16, f32 = jnp.bfloat16, jnp.float32

    near = count * half
    which_m = m.astype(jnp.int32).reshape(1)
    which_h = h.astype(jnp.int32).reshape(1)

    z, zs = lax.axis_index("dp"), lax.axis_size("dp")
    part = plane.ordered([x[None] for x in plane.gather(norm_gain)])
    gain = lax.dynamic_update_slice_in_dim(jnp.zeros((zs,) + part.shape, bf16), part[None], z, 0)
    for k in range(1, zs):
        came = lax.ppermute(part, "dp", [(i, (i + k) % zs) for i in range(zs)])
        gain = lax.dynamic_update_slice_in_dim(gain, came[None], (z + zs - k) % zs, 0)
    gain = gain.reshape(zs * count, STREAMS, -1).transpose(1, 0, 2).reshape(STREAMS, width).astype(f32)

    parts = 2 if count % 2 == 0 else 1
    per = count // parts
    parted = history.reshape(parts, per, cores, half, width)
    own_rows = [
        lax.dynamic_index_in_dim(parted[g], m, 1, keepdims=False).reshape(per * half, width) for g in range(parts)
    ]
    swap_columns = lambda x: lax.all_to_all(x, "hist", 1, 0, tiled=True)
    slots = [plane.gather(after(own_rows[0], part))]
    up_mine = swap_columns(after(up_weight, part))
    up_full = lax.all_gather(up_mine, "dp", axis=0, tiled=True)
    for g in range(1, parts):
        slots.append(plane.gather(after(own_rows[g], slots[-1][1])))
    packed = jnp.stack([query_weight, key_weight, value_weight, out_weight.T], 0)
    packed = packed.reshape(4, depth, count, -1).transpose(1, 2, 0, 3).reshape(depth, -1)
    narrow_mine = swap_columns(after(packed, up_mine, gain, slots[-1][1]))
    narrow_full = lax.all_gather(narrow_mine, "dp", axis=0, tiled=True)
    piece = narrow_full.shape[1] // 4
    out_full = narrow_full[:, 3 * piece :]

    layer_of = [h ^ plane.place(j) for j in range(count)]
    order = jnp.stack(layer_of).astype(jnp.int32)
    pick = sum(jnp.where(layer_of[j] == count - 1, j, 0) for j in range(count)).astype(jnp.int32).reshape(1)

    def to_slots(values):
        return jnp.stack(
            [sum(jnp.where(layer_of[j] == l, values[..., l], 0) for l in range(count)) for j in range(count)], -1
        )

    def from_slots(values):
        return jnp.stack(
            [sum(jnp.where(layer_of[j] == l, values[..., j], 0) for j in range(count)) for l in range(count)], -1
        )

    pairs = STREAMS * count
    in_wide = jnp.pad(mixer_in, ((0, 0), (0, LANES - hidden_units)))
    out_wide = jnp.pad(
        to_slots(mixer_out).reshape(hidden_units, pairs), ((0, LANES - hidden_units), (0, LANES - pairs))
    )
    bias_wide = jnp.pad(to_slots(mixer_bias).reshape(1, pairs), ((0, 0), (0, LANES - pairs)))

    block = jnp.arange(count)[:, None] * rows + jnp.arange(half)[None, :]
    positions = jnp.concatenate([(block + m * half).reshape(-1), (block + (1 - m) * half).reshape(-1)])
    tables = rope_tables(positions)
    found = []
    for g in range(parts):
        found = forward_streams(slots[g], g, parts, found, pick, in_wide, out_wide, bias_wide, gain)
        if g == 0:
            tables, down_turned, *found = tie((tables, down_weight.T, *found))
    down_mine = swap_columns(down_turned)
    down_full = lax.all_gather(down_mine, "dp", axis=0, tiled=True)
    all_weights = plane.gather(narrow_full[:, : 3 * piece])
    near_streams, (mixes, pres, stats) = list(found[:STREAMS]), found[STREAMS:]
    far_streams = [None] * STREAMS
    for c in reversed(range(STREAMS)):
        far_streams[c] = plane.swap(near_streams[c])

    domain_one = jnp.sum(jnp.where(jnp.arange(domain_scale.shape[0]) == domain[0], domain_scale, 0.0))
    own_target = lax.dynamic_slice_in_dim(target, m * half, half, 0)
    own_scale = lax.dynamic_slice_in_dim(loss_count, m * half, half, 0).astype(f32) * domain_one
    branch_own = (own_target.astype(f32) * own_scale[:, None]).astype(bf16)
    near_grad = plane.ordered(plane.gather(after(branch_own, slots[-1][1])))
    far_grad = plane.swap(near_grad)

    def mlp(stream, grad):
        before = dot(stream, up_full, (1, 0))
        back = dot(grad, down_full, (1, 0)) * gelu_slope(before)
        return gelu_exact(before).astype(bf16), back.astype(bf16)

    near_hidden, near_back = mlp(near_streams[3], near_grad)
    far_hidden, far_back = mlp(far_streams[3], far_grad)
    both = lambda near_one, far_one: [(near_one, 0), (far_one, 0)]
    local = lambda one: [(one, 0), (one, 1)]
    grads = both(near_grad, far_grad)
    down_part = outer([(grads, both(near_hidden, far_hidden))])
    down_sum = lax.psum_scatter(down_part, "dp", scatter_dimension=0, tiled=True)
    near_back, far_back, all_weights[1], *far_streams = lax.optimization_barrier(
        (near_back, far_back, all_weights[1], *far_streams)
    )
    up_part = outer([(both(near_streams[3], far_streams[3]), both(near_back, far_back))])
    up_sum = lax.psum_scatter(up_part, "dp", scatter_dimension=0, tiled=True)

    own_mix = lax.dynamic_slice_in_dim(mixes, h * half, half, 0)[:, :pairs].reshape(half, STREAMS, count)

    def own_block(j):
        found = lax.dynamic_slice_in_dim(slots[0][j], h % per * half, half, 0)
        for g in range(1, parts):
            found = jnp.where(h // per == g, lax.dynamic_slice_in_dim(slots[g][j], h % per * half, half, 0), found)
        return found

    own_layers = [own_block(j) for j in range(count)]
    own_part = lambda x: lax.dynamic_slice_in_dim(x, h * half, half, 0)
    own_given = [own_part(x) for x in near_streams], own_part(mixes), own_part(pres), own_part(stats)
    near_given, far_given, _, _, own_given, own_layers, all_weights[2] = lax.optimization_barrier(
        (near_streams[:3] + [near_grad], far_streams[:3] + [far_grad], up_part, down_part, own_given, own_layers, all_weights[2])
    )

    types = (f32, f32, bf16, bf16)
    attended, query_back, key_back, value_back, backs = attention(
        project(near_given, narrow_full, types), project(far_given, narrow_full, types), tables, which_m, count
    )

    def owned(near_one, far_one):
        return plane.scatter_packed(*add_in_slots(near_one, plane.swap(far_one), order, count))

    near_back, far_back, up_part = lax.optimization_barrier((near_back, far_back, up_part))
    far_mlp = dot(far_back, up_full, (1, 1)).astype(bf16)
    near_mlp = dot(near_back, up_full, (1, 1)).astype(bf16)
    owned_mlp = owned(near_mlp, far_mlp)
    backs, attended, _, down_sum, all_weights = lax.optimization_barrier(
        (backs, attended, owned_mlp, down_sum, all_weights)
    )
    own_backs = [lax.dynamic_slice_in_dim(backs, layer_of[j] * rows, rows, 0) for j in range(count)]
    own_backs = own_backs[:1] + [plane.direct(own_backs[j], j) for j in range(1, count)]
    narrow_part = outer(
        [
            (both(near_streams[0], far_streams[0]), local(query_back)),
            (both(near_streams[1], far_streams[1]), local(key_back)),
            (both(near_streams[2], far_streams[2]), local(value_back)),
            (grads, local(attended)),
        ]
    )
    narrow_sum = lax.psum_scatter(narrow_part, "dp", scatter_dimension=0, tiled=True)
    own_backs, wide_sum, _ = lax.optimization_barrier((own_backs, jnp.concatenate([up_sum, down_sum], 1), narrow_part))
    near_backs, far_backs = project_back(own_backs, all_weights)
    far_backs = plane.swap(far_backs)

    attended = after(attended, near_backs)
    branch_far = (dot(attended[near:], out_full, (1, 1)) + dot(far_hidden, down_full, (1, 1))).astype(bf16)
    branch = (dot(attended[:near], out_full, (1, 1)) + dot(near_hidden, down_full, (1, 1))).astype(bf16)
    branch_slots = add_in_slots(branch, plane.swap(branch_far), order, count)
    branch_low, branch_high = plane.scatter_packed(*branch_slots)
    mix_own = from_slots(own_mix)
    mix_rows = plane.both(mix_own, plane.swap(mix_own), 0).reshape(rows, STREAMS, count)

    def spread(summed):
        return lax.all_to_all(summed, "hist", 0, 0, tiled=True)

    wide_sum = spread(wide_sum)

    scale_wide, _ = tie((jnp.broadcast_to(own_scale[:, None], (half, LANES)), branch_slots))
    found = backward_streams(
        own_layers,
        0,
        half,
        [(near_backs, 0), (near_backs, 1), (near_backs, 2), (owned_mlp[0], 0)],
        [(far_backs, 0), (far_backs, 1), (far_backs, 2), (owned_mlp[1], 0)],
        0,
        *own_given,
        own_target,
        scale_wide,
        pick,
        order,
        in_wide,
        out_wide,
        gain,
    )
    layer_grads, sums = found[0], found[1:]
    came = lax.all_to_all(layer_grads, "hist", 0, 0, tiled=True)
    gain_sum, in_sum, out_sum, bias_sum = sums
    out_sum = from_slots(out_sum[:, :pairs].reshape(LANES, STREAMS, count)).reshape(LANES, pairs)
    bias_sum = from_slots(bias_sum[:, :pairs].reshape(1, STREAMS, count)).reshape(1, pairs)
    spare = LANES - hidden_units - STREAMS
    spare -= spare % 8
    packed_sum = jnp.concatenate([out_sum, bias_sum], 0).reshape(-1)
    packed_sum = jnp.pad(packed_sum, (0, width * spare - packed_sum.shape[0])).reshape(width, spare)
    small = jnp.concatenate([in_sum[:, :hidden_units], gain_sum.T, packed_sum], 1)
    small = total_over_dp(jnp.pad(small, ((0, 0), (0, LANES - small.shape[1]))), plane)
    came, small, narrow_sum, wide_sum, branch_low = tie((came, small, narrow_sum, wide_sum, branch_low))
    swapped = plane.swap(came)
    narrow_sum = spread(narrow_sum)
    small = total_over_hist(small, plane)
    history_grad = interleave(came, swapped, which_m, half).reshape(history.shape)
    up_grad, down_grad = place_wide(wide_sum, count, 2, (False, True))
    history_grad, up_grad, down_grad, narrow_sum, small, branch_low, branch_high = tie(
        (history_grad, up_grad, down_grad, narrow_sum, small, branch_low, branch_high)
    )
    branch_rows = branch_low.astype(f32) + branch_high.astype(f32)
    residual = sum(own_mix[:, STREAMS - 1, j, None] * own_layers[j].astype(f32) for j in range(count))
    output_own = (residual + branch_rows).astype(bf16)
    output = plane.both(output_own, plane.swap(output_own), 0).reshape(rows, width)
    query_grad, key_grad, value_grad, out_grad = place_wide(narrow_sum, count, 4, (False, False, False, True))
    small = over_plane(small, plane)
    mixer_in_grad = small[:, :hidden_units]
    gain_all = small[:, hidden_units : hidden_units + STREAMS].T
    place = (z * count + h) * norm_gain.shape[1]
    norm_gain_grad = lax.dynamic_slice_in_dim(gain_all, place, norm_gain.shape[1], 1)
    tail = small[:, hidden_units + STREAMS : hidden_units + STREAMS + spare].reshape(-1)[: (LANES + 1) * pairs]
    tail = tail.reshape(LANES + 1, STREAMS, count)
    mixer_out_grad = tail[:hidden_units]
    mixer_bias_grad = tail[LANES]
    return (
        output,
        mix_rows,
        history_grad,
        mixer_in_grad,
        mixer_out_grad,
        mixer_bias_grad,
        norm_gain_grad,
        query_grad,
        key_grad,
        value_grad,
        out_grad,
        up_grad,
        down_grad,
    )


def solution(mesh):
    in_specs = (
        P("hist", "dp", None),
        P(),
        P(),
        P(),
        P(None, ("dp", "hist")),
        P(("dp", "hist"), "mp"),
        P(("dp", "hist"), "mp"),
        P(("dp", "hist"), "mp"),
        P("mp", ("dp", "hist")),
        P(("dp", "hist"), "mp"),
        P("mp", ("dp", "hist")),
        P(("dp", "hist"), None),
        P(("dp", "hist")),
        P("dp"),
        P(),
    )
    out_specs = (
        P(("dp", "hist"), None),
        P(("dp", "hist"), None, None),
        P("hist", "dp", None),
        P(),
        P(),
        P(),
        P(None, ("dp", "hist")),
        P(("dp", "hist"), "mp"),
        P(("dp", "hist"), "mp"),
        P(("dp", "hist"), "mp"),
        P("mp", ("dp", "hist")),
        P(("dp", "hist"), "mp"),
        P("mp", ("dp", "hist")),
    )
    return jax.shard_map(shards, mesh=mesh, in_specs=in_specs, out_specs=out_specs, check_vma=False)
```
